32 devices in a mesh: height: 2 (over core), plane: 16 (over z, y, x).
Axes of the slice: x: 2, y: 2, z: 4, core: 2. Of those that a mesh axis runs over, the one named last changes fastest.
Arguments:
- cotangent: float32 [32, 128, 128], P('height', 'plane'), may hold values from -36 to 36
- conductivity: float32 [4, 16, 16], P('height', 'plane'), may hold values from 0.2 to 5
- capacity: float32 [4, 16, 16], P('height', 'plane'), may hold values from 0.5 to 2
- sources: int32 [2, 128], replicated, may hold values from 0 to 1023
Outputs:
- adjoint_second: float32 [32, 128, 128], P('height', 'plane')
- adjoint_first: float32 [32, 128, 128], P('height', 'plane')
- source_grad: float32 [2, 128], replicated
The draws below stay inside these ranges and needn't reach their ends.
Inputs may be any that keep to these rules, and one draw needn't show every extreme that they name: `sources`: element numbers; element (ez, ex, ey) has number (ez * 16 + ex) * 16 + ey, and a number may repeat.
All inputs are finite; a program needn't handle non-finite values.
Results may differ from the reference program's by a relative error of at most 0.0001.
Values sent between devices are 32-bit elements; how exact they have to be, the bound alone decides.
No kernel may reach another device: no remote copies, remote signals or barrier semaphores. Data moves between devices by JAX's collectives and lax.ppermute only.
A program may use at most 64 MiB of HBM per device.

```python
import math
import jax
import jax.numpy as jnp
import numpy as np
from jax import lax

EY = 16
ITERS = 3
SRC = 128
EXG = 16
EZG = 4
NXN = 128
NYN = 128
NZN = 32
ELEMS = 1024


def draw_cotangent(key, part):
    sample_key = jax.random.fold_in(key, 11)
    sample = jnp.clip(jax.random.normal(sample_key, (NZN, NXN, NYN), jnp.float32), -4.0, 4.0)
    depth_ramp = 1.0 + 2.0 * jnp.arange(NZN, dtype=jnp.float32) / (NZN - 1)
    width_ramp = 1.0 + 2.0 * jnp.arange(NXN, dtype=jnp.float32) / (NXN - 1)
    return sample * depth_ramp[:, None, None] * width_ramp[None, :, None]


def place_ends(entries, own_key, least, high):
    index_at = [jax.random.randint(jax.random.fold_in(own_key, axis), (), 0, length) for axis, length in enumerate(entries.shape)]
    longest = entries.shape.index(max(entries.shape))
    neighbour = index_at[:longest] + [(index_at[longest] + 1) % entries.shape[longest]] + index_at[longest + 1:]
    return entries.at[tuple(index_at)].set(least).at[tuple(neighbour)].set(high)


def level_of(key, dims, cuts, least, largest):
    def one(dim, shards_of):
        steps = jax.random.uniform(jax.random.fold_in(jax.random.fold_in(key, 6), dim), (shards_of,), jnp.float32, least / len(cuts), largest / len(cuts))
        return jnp.repeat(jnp.exp(steps), dims[dim] // shards_of).reshape((-1,) + (1,) * (len(dims) - dim - 1))

    loudness = one(*cuts[0])
    for cut in cuts[1:]:
        loudness = loudness * one(*cut)
    return loudness


def setup_inputs(seed: int = 0) -> dict:
    streams_of = jax.random.split(jax.random.key(seed), 5)
    cotangent = draw_cotangent(jax.random.fold_in(streams_of[4], 71), 0)
    conductivity = jnp.clip(jnp.exp(math.log(5.0) - 3.218876 * jax.random.uniform(streams_of[1], (EZG, EXG, EY), jnp.float32) ** level_of(streams_of[1], (EZG, EXG, EY), ((0, 2), (1, 16)), -0.2, 0.2)), 0.2, 5.0)
    capacity = jnp.clip(jnp.exp(math.log(2.0) - 1.3862944 * jax.random.uniform(streams_of[2], (EZG, EXG, EY), jnp.float32) ** level_of(streams_of[2], (EZG, EXG, EY), ((0, 2), (1, 16)), -0.2, 0.2)), 0.5, 2.0)
    sources = place_ends(jax.random.randint(streams_of[3], (2, SRC), 0, ELEMS), jax.random.fold_in(streams_of[3], 1), 0, ELEMS - 1).astype(jnp.int32)
    return {"cotangent": cotangent, "conductivity": conductivity, "capacity": capacity, "sources": sources}


precise = lax.Precision.HIGHEST
INV_STEP = 20.0


def gll_tables():
    points = np.array([-1.0, -0.8717401485096066, -0.5917001814331423, -0.2092992179024789, 0.2092992179024789, 0.5917001814331423, 0.8717401485096066, 1.0])
    weights = np.array([1.0 / 28.0, 0.2107042271435061, 0.3411226924835044, 0.4124587946587038, 0.4124587946587038, 0.3411226924835044, 0.2107042271435061, 1.0 / 28.0])
    product = np.array([np.prod([points[column] - points[others] for others in range(8) if others != column]) for column in range(8)])
    derivative = np.zeros((8, 8))
    for row_idx in range(8):
        for col_idx in range(8):
            if row_idx != col_idx:
                derivative[row_idx, col_idx] = product[row_idx] / (product[col_idx] * (points[row_idx] - points[col_idx]))
        derivative[row_idx, row_idx] = -np.sum(derivative[row_idx])
    stiff_diag = np.sum(derivative ** 2 * weights[:, None], axis=0)
    return derivative, weights, stiff_diag


def multiplicity(extent):
    position = jnp.arange(extent, dtype=jnp.int32)
    ending = ((position % 8 == 7) & (position < extent - 1)).astype(jnp.float32)
    opening = ((position % 8 == 0) & (position > 0)).astype(jnp.float32)
    return 1.0 + ending + opening


def pair_sum(values, dim_index):
    ending = [slice(None)] * 3
    opening = [slice(None)] * 3
    ending[dim_index] = slice(7, -1, 8)
    opening[dim_index] = slice(8, None, 8)
    joined = values[tuple(ending)] + values[tuple(opening)]
    return values.at[tuple(ending)].set(joined).at[tuple(opening)].set(joined)


def assemble(values):
    return pair_sum(pair_sum(pair_sum(values, 1), 2), 0)


def reference(cotangent, conductivity, capacity, sources):
    derivative, weights, stiff_diag = gll_tables()
    depth_nodes, width_nodes, span_nodes = cotangent.shape
    diff = jnp.asarray(derivative, jnp.float32)
    weight_depth = jnp.asarray(np.tile(weights, depth_nodes // 8), jnp.float32)
    weight_width = jnp.asarray(np.tile(weights, width_nodes // 8), jnp.float32)
    weight_span = jnp.asarray(np.tile(weights, span_nodes // 8), jnp.float32)
    stiff_depth = jnp.asarray(np.tile(stiff_diag, depth_nodes // 8), jnp.float32)
    stiff_width = jnp.asarray(np.tile(stiff_diag, width_nodes // 8), jnp.float32)
    stiff_span = jnp.asarray(np.tile(stiff_diag, span_nodes // 8), jnp.float32)
    kappa_nodes = jnp.repeat(jnp.repeat(jnp.repeat(conductivity, 8, axis=0), 8, axis=1), 8, axis=2)
    cap_nodes = jnp.repeat(jnp.repeat(jnp.repeat(capacity, 8, axis=0), 8, axis=1), 8, axis=2)
    omega_nodes = weight_depth[:, None, None] * weight_width[None, :, None] * weight_span[None, None, :]
    mass_local = INV_STEP * cap_nodes * omega_nodes
    kappa_weight = kappa_nodes * omega_nodes
    diag_local = mass_local + kappa_nodes * (stiff_depth[:, None, None] * weight_width[None, :, None] * weight_span[None, None, :] + weight_depth[:, None, None] * stiff_width[None, :, None] * weight_span[None, None, :] + weight_depth[:, None, None] * weight_width[None, :, None] * stiff_span[None, None, :])
    diag_total = assemble(diag_local)
    share_weight = 1.0 / (multiplicity(depth_nodes)[:, None, None] * multiplicity(width_nodes)[None, :, None] * multiplicity(span_nodes)[None, None, :])
    shape_depth = (depth_nodes // 8, 8, width_nodes, span_nodes)
    shape_width = (depth_nodes, width_nodes // 8, 8, span_nodes)
    shape_span = (depth_nodes, width_nodes, span_nodes // 8, 8)
    full_shape = cotangent.shape

    def stiffness(values):
        grad_depth = jnp.einsum("ab,ebxy->eaxy", diff, values.reshape(shape_depth), precision=precise).reshape(full_shape)
        grad_width = jnp.einsum("ab,zeby->zeay", diff, values.reshape(shape_width), precision=precise).reshape(full_shape)
        grad_span = jnp.einsum("ab,zxeb->zxea", diff, values.reshape(shape_span), precision=precise).reshape(full_shape)
        back_depth = jnp.einsum("ab,eaxy->ebxy", diff, (kappa_weight * grad_depth).reshape(shape_depth), precision=precise).reshape(full_shape)
        back_width = jnp.einsum("ab,zeay->zeby", diff, (kappa_weight * grad_width).reshape(shape_width), precision=precise).reshape(full_shape)
        back_span = jnp.einsum("ab,zxea->zxeb", diff, (kappa_weight * grad_span).reshape(shape_span), precision=precise).reshape(full_shape)
        return mass_local * values + (back_depth + back_width + back_span)

    def inner_sum(left_values, right_values):
        return jnp.sum(left_values * right_values * share_weight)

    def adjoint_solve(source_term):
        iterate = jnp.zeros_like(source_term)
        residual = source_term
        precond = residual / diag_total
        direction = precond
        rho_now = inner_sum(residual, precond)
        for sweep_idx in range(ITERS):
            applied = assemble(stiffness(direction))
            step_len = rho_now / inner_sum(direction, applied)
            iterate = iterate + step_len * direction
            residual = residual - step_len * applied
            precond = residual / diag_total
            rho_next = inner_sum(residual, precond)
            direction = precond + (rho_next / rho_now) * direction
            rho_now = rho_next
        return iterate

    adjoint_second = adjoint_solve(assemble(mass_local * cotangent))
    adjoint_first = adjoint_solve(assemble(mass_local * adjoint_second))

    def element_sums(values):
        return (mass_local * values).reshape(depth_nodes // 8, 8, width_nodes // 8, 8, span_nodes // 8, 8).sum(axis=(1, 3, 5)).reshape(-1)

    grad_first = element_sums(adjoint_first)[sources[0]] / (8.0 * INV_STEP)
    grad_second = element_sums(adjoint_second)[sources[1]] / (8.0 * INV_STEP)
    return adjoint_second, adjoint_first, jnp.stack([grad_first, grad_second])
```

```python
import functools

import jax
import jax.numpy as jnp
import ml_dtypes
import numpy as np
from jax import lax
from jax.experimental import pallas as pl
from jax.experimental.pallas import tpu as pltpu
from jax.sharding import PartitionSpec as P

INV_STEP = 20.0
SHIFTS = (0.5, 1.5)
GROUP = 4
REACH = 4
TERMS = ((0, 0), (0, 1), (0, 2), (1, 0), (1, 1), (2, 0))
PAIRS = ((0, 0), (0, 1), (0, 2), (1, 1), (1, 2), (2, 2))
HIGHEST = lax.Precision.HIGHEST
F32 = jnp.float32


def gll_tables():
    points = np.array([-1.0, -0.8717401485096066, -0.5917001814331423, -0.2092992179024789, 0.2092992179024789, 0.5917001814331423, 0.8717401485096066, 1.0])
    weights = np.array([1.0 / 28.0, 0.2107042271435061, 0.3411226924835044, 0.4124587946587038, 0.4124587946587038, 0.3411226924835044, 0.2107042271435061, 1.0 / 28.0])
    product = np.array([np.prod([points[col] - points[others] for others in range(8) if others != col]) for col in range(8)])
    derivative = np.zeros((8, 8))
    for row in range(8):
        for col in range(8):
            if row != col:
                derivative[row, col] = product[row] / (product[col] * (points[row] - points[col]))
        derivative[row, row] = -np.sum(derivative[row])
    return derivative, weights, np.sum(derivative**2 * weights[:, None], axis=0)


def pieces(matrix):
    out, rest = [], matrix
    for _ in range(3):
        piece = rest.astype(ml_dtypes.bfloat16)
        out.append(piece)
        rest = rest - piece.astype(np.float64)
    return out


def tables(span):
    derivative, weights, stiff = gll_tables()
    line = (derivative.T * weights) @ derivative / weights[:, None]
    eye = np.eye(8)
    face = pieces(np.kron(line, eye) + np.kron(eye, line))
    face_mat = np.concatenate([face[m] for m, _ in TERMS], axis=1)
    row = pieces(np.kron(np.eye(span // 8), line.T))
    row_a = np.concatenate([np.concatenate([row[0], row[1]], 1)] * 2, axis=0)
    row_b = np.concatenate([row[2], row[0]], axis=0)
    tile = np.tile(weights, span // 8)
    ratio = stiff / weights
    omega = weights[:, None, None] * weights[None, :, None] * tile[None, None, :]
    quot = ratio[:, None, None] + ratio[None, :, None] + np.tile(ratio, span // 8)[None, None, :]
    return face_mat, row_a, row_b, omega.astype(np.float32), quot.astype(np.float32)


def swap(value, axis, pairs):
    if not pairs:
        return None
    return lax.ppermute(value, axis, [*pairs, *((b, a) for a, b in pairs)])


def pack_kernel(cot_ref, kap_ref, cap_ref, out_ref):
    depth, _, span = cot_ref.shape
    elems, _, parts = kap_ref.shape
    out_ref[: depth * 8, :] = cot_ref[...].reshape(depth * 8, span)
    spread = (lax.broadcasted_iota(jnp.int32, (parts, span), 1) // 8 == lax.broadcasted_iota(jnp.int32, (parts, span), 0)).astype(F32)
    coef = jnp.concatenate([kap_ref[...].reshape(elems, parts), cap_ref[...].reshape(elems, parts)], axis=0)
    rows = out_ref.shape[0] - depth * 8
    if rows > 2 * elems:
        coef = jnp.concatenate([coef, jnp.zeros((rows - 2 * elems, parts), F32)], axis=0)
    out_ref[depth * 8 :, :] = jnp.dot(coef, spread, precision=HIGHEST, preferred_element_type=F32)


class Layout:
    def __init__(self):
        wide = 2 * REACH + 1
        self.wide = wide
        self.cot = 0
        self.sums = self.cot + 3 * GROUP + 2
        self.minv = self.sums + wide + 2
        self.ratio = self.minv + wide
        self.basis = self.ratio + 5
        self.second = self.basis + 3 * wide
        self.total = self.second + wide


def basis_kernel(counts, sent, *refs):
    height, plane = counts
    lay = Layout()
    wide = lay.wide
    n_in = sum(1 for arr in sent if arr is not None) * height
    msgs = refs[:n_in]
    face_ref, row_a_ref, row_b_ref, omega_ref, quot_ref = refs[n_in : n_in + 5]
    fields_ref, info_ref = refs[n_in + 5 : n_in + 7]
    pool, coef, weigh = refs[n_in + 7 :]
    depth, _, span = pool.shape[1:]
    own_depth = depth // height
    elems = depth // 8
    own_elems = elems // height
    height_pos = lax.axis_index("height")
    plane_pos = lax.axis_index("plane")
    member = lax.rem(plane_pos, GROUP)
    group = plane_pos // GROUP
    even = lax.rem(group, 2) == 0
    early = lax.rem(group // 2, 2) == 0

    def stage(msg, piece, slot, block):
        rows = own_depth * 8 + (-(-(2 * own_elems) // 8)) * 8
        top = piece * rows
        pool[lay.cot + slot, pl.ds(block * own_depth, own_depth)] = msg[top : top + own_depth * 8, :].reshape(own_depth, 8, span)
        for kind in range(2):
            for elem in range(own_elems):
                at = top + own_depth * 8 + kind * own_elems + elem
                coef[slot, kind, block * own_elems + elem] = jnp.broadcast_to(msg[at : at + 1, :], (8, span))

    def blank(slot):
        pool[lay.cot + slot] = jnp.zeros((depth, 8, span), F32)
        coef[slot] = jnp.zeros(coef.shape[1:], F32)

    present = [name for name, arr in zip(("own", "pair", "cross", "far1", "far2"), sent) if arr is not None]
    for missing, slot in (("pair", None), ("cross", None)):
        if missing not in present:
            for piece in range(GROUP):
                base = jnp.where(even, 1 + 2 * GROUP, 1) if missing == "pair" else jnp.where(even, 1, 1 + 2 * GROUP)
                blank(base + piece)
    if "far1" not in present or "far2" not in present:
        if "far1" in present:
            blank(jnp.where(early, 0, 3 * GROUP + 1))
        else:
            blank(0)
            blank(3 * GROUP + 1)
    step = len(present)
    for turn in range(height):
        block = lax.rem(height_pos - turn + height, height)
        for pos, name in enumerate(present):
            msg = msgs[turn * step + pos]
            if name in ("own", "pair", "cross"):
                if name == "own":
                    base = 1 + GROUP
                elif name == "pair":
                    base = jnp.where(even, 1 + 2 * GROUP, 1)
                else:
                    base = jnp.where(even, 1, 1 + 2 * GROUP)
                for piece in range(GROUP):
                    stage(msg, piece, base + jnp.bitwise_xor(member, piece), block)
            else:
                first = early if name == "far1" else jnp.logical_not(early)
                stage(msg, 0, jnp.where(first, 3 * GROUP + 1, 0), block)

    lane = lax.broadcasted_iota(jnp.int32, (8, span), 1)
    sub = lax.broadcasted_iota(jnp.int32, (8, span), 0)
    opens = (lane % 8 == 0) & (lane > 0)
    closes = (lane % 8 == 7) & (lane < span - 1)

    def join_span(values):
        return values + jnp.where(opens, pltpu.roll(values, 1, 2), jnp.where(closes, pltpu.roll(values, span - 1, 2), 0.0))

    def join_depth(values):
        planes = []
        for elem in range(elems):
            first, last = values[elem * 8], values[elem * 8 + 7]
            if elem > 0:
                first = first + values[elem * 8 - 1]
            if elem < elems - 1:
                last = last + values[elem * 8 + 8]
            planes += [first[None], values[elem * 8 + 1 : elem * 8 + 7], last[None]]
        return jnp.concatenate(planes, axis=0)

    def join_width(base, at):
        low = pltpu.roll(pool[base + at - 1], 1, 1)
        high = pltpu.roll(pool[base + at + 1], 7, 1)
        return pool[base + at] + jnp.where(sub == 0, low, jnp.where(sub == 7, high, 0.0))

    def per_elem(slot, kind, count=elems, start=0):
        return jnp.concatenate([jnp.broadcast_to(coef[slot, kind, start + e][None], (8, 8, span)) for e in range(count)], axis=0)

    def omega(count=elems):
        return jnp.concatenate([omega_ref[...]] * count, axis=0)

    def operator(values, slot, start=0):
        count = values.shape[0] // 8
        flat = values.reshape(count * 64, span)
        one = flat.astype(jnp.bfloat16)
        rest = flat - one.astype(F32)
        two = rest.astype(jnp.bfloat16)
        three = (rest - two.astype(F32)).astype(jnp.bfloat16)
        split = (one, two, three)
        both = jnp.dot(jnp.concatenate([one, two], axis=1), row_a_ref[...], preferred_element_type=F32)
        lin = both[:, :span] + both[:, span:] + jnp.dot(jnp.concatenate([one, three], axis=1), row_b_ref[...], preferred_element_type=F32)
        blocks = []
        for e in range(count):
            stack = jnp.concatenate([split[f][e * 64 : e * 64 + 64] for _, f in TERMS], axis=0)
            blocks.append(jnp.dot(face_ref[...], stack, preferred_element_type=F32))
        lin = (lin + jnp.concatenate(blocks, axis=0)).reshape(values.shape)
        return omega(count) * ((INV_STEP * per_elem(slot, 1, count, start)) * values + per_elem(slot, 0, count, start) * lin)

    def loop(start, stop, body):
        lax.fori_loop(start, stop, lambda at, carry: (body(at), carry)[1], 0)

    diag_at, mass_at = lay.basis + wide, lay.second - 1

    def start_slab(at):
        slot = member + at
        heavy = omega() * (INV_STEP * per_elem(slot, 1))
        pool[lay.sums + at] = join_depth(join_span(heavy * pool[lay.cot + slot]))
        quot = jnp.concatenate([quot_ref[...]] * elems, axis=0)
        pool[diag_at + at] = join_depth(join_span(heavy + omega() * per_elem(slot, 0) * quot))

    def mass_slab(at):
        pool[mass_at + at - 1] = join_depth(join_span(omega() * (INV_STEP * per_elem(member + at, 1))))

    def first_slab(at):
        diag = join_width(diag_at, at)
        inverse = jnp.where(diag > 0.0, 1.0 / jnp.where(diag > 0.0, diag, 1.0), 0.0)
        pool[lay.minv + at - 1] = inverse
        pool[lay.basis + at - 1] = inverse * join_width(lay.sums, at)

    def ratio_slab(at):
        pool[lay.ratio + at - 3] = pool[lay.minv + at - 1] * join_width(mass_at - 1, at)

    loop(0, wide + 2, start_slab)
    loop(2, wide, mass_slab)
    loop(1, wide + 1, first_slab)
    loop(3, wide - 1, ratio_slab)

    mid = REACH + 1
    own = pl.ds(height_pos * own_depth, own_depth)
    zpos = lax.broadcasted_iota(jnp.int32, (own_depth, 8, span), 0) + height_pos * own_depth
    xpos = lax.broadcasted_iota(jnp.int32, (own_depth, 8, span), 1) + plane_pos * 8

    def copies(pos, extent):
        return jnp.where(((pos % 8 == 7) & (pos < extent - 1)) | ((pos % 8 == 0) & (pos > 0)), 0.5, 1.0)

    share = copies(zpos, depth) * copies(xpos, plane * 8) * jnp.where(opens | closes, 0.5, 1.0)
    weigh[...] = share / pool[lay.minv + REACH, own]

    for level in range(2):
        def apply(at, level=level):
            pool[lay.sums + at] = join_depth(join_span(operator(pool[lay.basis + level * wide + at - 1], member + at)))

        def advance(at, level=level):
            pool[lay.basis + (level + 1) * wide + at - 1] = (
                pool[lay.minv + at - 1] * join_width(lay.sums, at) - SHIFTS[level] * pool[lay.basis + level * wide + at - 1]
            )

        loop(1 + level, wide + 1 - level, apply)
        loop(2 + level, wide - level, advance)

    def second(vec):
        def begin(at):
            pool[lay.second + at - 3] = pool[lay.ratio + at - 3] * pool[lay.basis + vec * wide + at - 1]

        loop(3, 8, begin)
        for level in range(2):
            here = lay.second + (0, 5, 8)[level] - 3 - level
            after = lay.second + (0, 5, 8)[level + 1] - 4 - level

            def apply(at, here=here):
                pool[lay.sums + at] = join_depth(join_span(operator(pool[here + at], member + at)))

            def advance(at, here=here, after=after, level=level):
                pool[after + at] = pool[lay.minv + at - 1] * join_width(lay.sums, at) - SHIFTS[level] * pool[here + at]

            loop(3 + level, 8 - level, apply)
            loop(4 + level, 7 - level, advance)
        fields_ref[3 + vec] = pool[lay.second + 2, own]
        fields_ref[6 + vec] = pool[lay.second + 6, own]
        fields_ref[9 + vec] = pool[lay.second + 8, own]

    for vec in range(3):
        fields_ref[vec] = pool[lay.basis + vec * wide + REACH, own]
    loop(0, 3, second)

    slot = member + mid
    start = height_pos * own_elems

    def total(values):
        return jnp.sum(values, axis=0)

    def weighted(index):
        return weigh[...] * fields_ref[index]

    parts = []
    left = [weighted(i) for i in range(3)]
    parts += [total(left[i] * fields_ref[j]) for i, j in PAIRS]
    parts.append(total(fields_ref[2] * operator(fields_ref[2], slot, start)))
    for k, l in PAIRS:
        pairs = PAIRS if k == l else [(i, j) for i in range(3) for j in range(3)]
        left = [weighted(3 + 3 * k + i) for i in range(3)]
        parts += [total(left[i] * fields_ref[3 + 3 * l + j]) for i, j in pairs]
    energy = [operator(fields_ref[9 + j], slot, start) for j in range(3)]
    parts += [total(fields_ref[9 + i] * energy[j]) for i, j in PAIRS]
    lines = [jnp.sum(part, axis=0, keepdims=True) for part in parts]
    lines.append(jnp.zeros((span - len(lines), span), F32))
    sums = lax.dot_general(jnp.ones((8, span), F32), jnp.concatenate(lines, axis=0), (((1,), (1,)), ((), ())), precision=HIGHEST, preferred_element_type=F32)

    heavy = omega(own_elems) * (INV_STEP * per_elem(slot, 1, own_elems, start))
    rows = []
    for index in range(12):
        mass = heavy * fields_ref[index]
        for elem in range(own_elems):
            rows.append(jnp.sum(jnp.sum(mass[elem * 8 : elem * 8 + 8], axis=0), axis=0, keepdims=True))
    rows = jnp.concatenate(rows, axis=0)
    cells = span // 8
    per_row = span // cells
    spread = (lax.broadcasted_iota(jnp.int32, (span, span), 0) // 8 == lax.broadcasted_iota(jnp.int32, (span, span), 1) % cells).astype(F32)
    rows = jnp.dot(rows, spread, precision=HIGHEST, preferred_element_type=F32)
    place = lax.broadcasted_iota(jnp.int32, rows.shape, 0) % per_row == lax.broadcasted_iota(jnp.int32, rows.shape, 1) // cells
    rows = jnp.where(place, rows, 0.0).reshape(rows.shape[0] // per_row, per_row, span)
    packed = jnp.sum(rows, axis=1)
    info_ref[...] = jnp.concatenate([packed, sums[:1]], axis=0)


def galerkin(gram, energy):
    n00, n01, n02, n11, n12, n22 = gram
    h00, h01, h02 = n01 + SHIFTS[0] * n00, n11 + SHIFTS[0] * n01, n12 + SHIFTS[0] * n02
    h11, h12 = n12 + SHIFTS[1] * n11, n22 + SHIFTS[1] * n12
    low10, low20 = h01 / h00, h02 / h00
    piv1 = h11 - low10 * h01
    off12 = h12 - low10 * h02
    low21 = off12 / piv1
    piv2 = energy - low20 * h02 - low21 * off12
    y0 = n00
    y1 = n01 - low10 * y0
    y2 = n02 - low20 * y0 - low21 * y1
    c2 = y2 / piv2
    c1 = y1 / piv1 - low21 * c2
    c0 = y0 / h00 - low10 * c1 - low20 * c2
    return c0, c1, c2


def combine_kernel(info_ref, fields_ref, owner_ref, place_ref, second_ref, first_ref, grad_ref):
    devices, lines, span = info_ref.shape
    ones = jnp.ones((devices, span), F32)
    contract = (((0,), (0,)), ((), ()))
    wide = lax.dot_general(info_ref[:, lines - 1, :], ones, contract, precision=HIGHEST, preferred_element_type=F32)
    take = [wide[i : i + 1, :] for i in range(7 + 45 + 6)]
    coef = galerkin(take[:6], take[6])
    at = 7
    double = [(2.0 if i != j else 1.0) * coef[i] * coef[j] for i, j in PAIRS]
    every = [coef[i] * coef[j] for i in range(3) for j in range(3)]
    gram = []
    for k, l in PAIRS:
        factors = double if k == l else every
        gram.append(sum(f * t for f, t in zip(factors, take[at : at + len(factors)])))
        at += len(factors)
    energy = sum(f * t for f, t in zip(double, take[at : at + 6]))
    outer = galerkin(gram, energy)
    factors = list(coef) + [d * c for d in outer for c in coef]

    second_ref[...] = factors[0] * fields_ref[0] + factors[1] * fields_ref[1] + factors[2] * fields_ref[2]
    first = factors[3] * fields_ref[3]
    for i in range(4, 12):
        first = first + factors[i] * fields_ref[i]
    first_ref[...] = first

    per_line = 12 // (lines - 1)
    cells = span // per_line
    row = lax.broadcasted_iota(jnp.int32, (span, span), 0)
    for step in range(2):
        holder = (owner_ref[step : step + 1, :] == lax.broadcasted_iota(jnp.int32, (devices, span), 0)).astype(F32)
        here = place_ref[step : step + 1, :] == row % cells
        result = jnp.zeros((1, span), F32)
        for line in range(lines - 1):
            fields = [f for f in range(line * per_line, (line + 1) * per_line) if (f >= 3) == (step == 0)]
            if not fields:
                continue
            picked = lax.dot_general(info_ref[:, line, :], holder, contract, precision=HIGHEST, preferred_element_type=F32)
            picked = jnp.where(here, picked, 0.0)
            for f in fields:
                lo = (f - line * per_line) * cells
                result = result + factors[f] * jnp.sum(picked[lo : lo + cells], axis=0, keepdims=True)
        grad_ref[step : step + 1, :] = result * (1.0 / (8.0 * INV_STEP))


def per_device(counts, cotangent, conductivity, capacity, sources):
    height, plane = counts
    depth, _, span = cotangent.shape
    elems = depth // 8
    cells = span // 8
    vmem = pl.BlockSpec(memory_space=pltpu.VMEM)

    rows = depth * 8 + -(-(2 * elems) // 8) * 8
    message = pl.pallas_call(
        pack_kernel,
        out_shape=jax.ShapeDtypeStruct((rows, span), F32),
        in_specs=[vmem] * 3,
        out_specs=vmem,
    )(cotangent, conductivity, capacity)

    member = lax.axis_index("plane") % GROUP
    group = lax.axis_index("plane") // GROUP
    groups = plane // GROUP
    gathered = message
    width = 1
    while width < GROUP:
        other = swap(gathered, "plane", [(p, p ^ width) for p in range(plane) if p & width == 0])
        gathered = jnp.concatenate([gathered, other], axis=0)
        width *= 2

    def group_pairs(first, gap):
        return [(g * GROUP + m, (g + gap) * GROUP + m) for g in range(groups - gap) if first(g) for m in range(GROUP)]

    pair = swap(gathered, "plane", group_pairs(lambda g: g % 2 == 0, 1))
    cross = swap(gathered, "plane", group_pairs(lambda g: g % 2 == 1, 1))
    slabs = gathered.reshape(GROUP, rows, span)
    far = []
    for turn in range(2):
        pairs = group_pairs(lambda g, turn=turn: (g // 2) % 2 == turn, 2)
        if pairs:
            ends = jnp.where((group // 2) % 2 == turn, GROUP - 1, 0)
            edge = lax.dynamic_index_in_dim(slabs, jnp.bitwise_xor(member, ends), 0, keepdims=False)
            far.append(swap(edge, "plane", pairs))
        else:
            far.append(None)
    sent = (gathered, pair, cross, *far)
    blocks = [arr for arr in sent if arr is not None]
    operands = list(blocks)
    for turn in range(1, height):
        operands += [lax.ppermute(arr, "height", [(h, (h + turn) % height) for h in range(height)]) for arr in blocks]

    lay = Layout()
    consts = tables(span)
    slots = 3 * GROUP + 2
    fields, info = pl.pallas_call(
        functools.partial(basis_kernel, counts, tuple(None if arr is None else 0 for arr in sent)),
        out_shape=(jax.ShapeDtypeStruct((12, depth, 8, span), F32), jax.ShapeDtypeStruct((12 * elems * cells // span + 1, span), F32)),
        in_specs=[vmem] * (len(operands) + len(consts)),
        out_specs=(vmem, vmem),
        scratch_shapes=[
            pltpu.VMEM((lay.total, depth * height, 8, span), F32),
            pltpu.VMEM((slots, 2, elems * height, 8, span), F32),
            pltpu.VMEM((depth, 8, span), F32),
        ],
        compiler_params=pltpu.CompilerParams(vmem_limit_bytes=56 * 1024 * 1024),
    )(*operands, *[jnp.asarray(c) for c in consts])

    devices = height * plane
    shared = lax.all_to_all(jnp.broadcast_to(info[None], (devices, *info.shape)), ("height", "plane"), 0, 0, tiled=True)

    cell = sources % cells
    column = sources // cells
    wide_elem = column % plane
    deep_elem = column // plane
    owner = (deep_elem // elems) * plane + wide_elem
    place = (deep_elem % elems) * cells + cell
    return pl.pallas_call(
        combine_kernel,
        out_shape=(
            jax.ShapeDtypeStruct(cotangent.shape, F32),
            jax.ShapeDtypeStruct(cotangent.shape, F32),
            jax.ShapeDtypeStruct(sources.shape, F32),
        ),
        in_specs=[vmem] * 4,
        out_specs=(vmem, vmem, vmem),
        compiler_params=pltpu.CompilerParams(vmem_limit_bytes=32 * 1024 * 1024),
    )(shared, fields, owner, place)


def solution(mesh):
    counts = (mesh.shape["height"], mesh.shape["plane"])
    field = P("height", "plane", None)
    return jax.shard_map(
        functools.partial(per_device, counts),
        mesh=mesh,
        in_specs=(field, field, field, P()),
        out_specs=(field, field, P()),
        check_vma=False,
    )
```

```python
import functools

import jax
import jax.numpy as jnp
import ml_dtypes
import numpy as np
from jax import lax
from jax.experimental import pallas as pl
from jax.experimental.pallas import tpu as pltpu
from jax.sharding import PartitionSpec as P

INV_STEP = 20.0
SHIFTS = (0.5, 1.5)
GROUP = 4
REACH = 4
TERMS = ((0, 0), (0, 1), (0, 2), (1, 0), (1, 1), (2, 0))
PAIRS = ((0, 0), (0, 1), (0, 2), (1, 1), (1, 2), (2, 2))
HIGHEST = lax.Precision.HIGHEST
F32 = jnp.float32


def gll_tables():
    points = np.array([-1.0, -0.8717401485096066, -0.5917001814331423, -0.2092992179024789, 0.2092992179024789, 0.5917001814331423, 0.8717401485096066, 1.0])
    weights = np.array([1.0 / 28.0, 0.2107042271435061, 0.3411226924835044, 0.4124587946587038, 0.4124587946587038, 0.3411226924835044, 0.2107042271435061, 1.0 / 28.0])
    product = np.array([np.prod([points[col] - points[others] for others in range(8) if others != col]) for col in range(8)])
    derivative = np.zeros((8, 8))
    for row in range(8):
        for col in range(8):
            if row != col:
                derivative[row, col] = product[row] / (product[col] * (points[row] - points[col]))
        derivative[row, row] = -np.sum(derivative[row])
    return derivative, weights, np.sum(derivative**2 * weights[:, None], axis=0)


def pieces(matrix):
    out, rest = [], matrix
    for _ in range(3):
        piece = rest.astype(ml_dtypes.bfloat16)
        out.append(piece)
        rest = rest - piece.astype(np.float64)
    return out


def tables(span):
    derivative, weights, stiff = gll_tables()
    line = (derivative.T * weights) @ derivative / weights[:, None]
    eye = np.eye(8)
    face = pieces(np.kron(line, eye) + np.kron(eye, line))
    face_mat = np.concatenate([face[m] for m, _ in TERMS], axis=1)
    row = pieces(np.kron(np.eye(span // 8), line.T))
    row_a = np.concatenate([np.concatenate([row[0], row[1]], 1)] * 2, axis=0)
    row_b = np.concatenate([row[2], row[0]], axis=0)
    tile = np.tile(weights, span // 8)
    ratio = stiff / weights
    omega = weights[:, None, None] * weights[None, :, None] * tile[None, None, :]
    quot = ratio[:, None, None] + ratio[None, :, None] + np.tile(ratio, span // 8)[None, None, :]
    return face_mat, row_a, row_b, omega.astype(np.float32), quot.astype(np.float32)


def swap(value, axis, pairs):
    if not pairs:
        return None
    return lax.ppermute(value, axis, [*pairs, *((b, a) for a, b in pairs)])


def pack_kernel(cot_ref, kap_ref, cap_ref, out_ref):
    depth, _, span = cot_ref.shape
    elems, _, parts = kap_ref.shape
    out_ref[: depth * 8, :] = cot_ref[...].reshape(depth * 8, span)
    spread = (lax.broadcasted_iota(jnp.int32, (parts, span), 1) // 8 == lax.broadcasted_iota(jnp.int32, (parts, span), 0)).astype(F32)
    coef = jnp.concatenate([kap_ref[...].reshape(elems, parts), cap_ref[...].reshape(elems, parts)], axis=0)
    rows = out_ref.shape[0] - depth * 8
    if rows > 2 * elems:
        coef = jnp.concatenate([coef, jnp.zeros((rows - 2 * elems, parts), F32)], axis=0)
    out_ref[depth * 8 :, :] = jnp.dot(coef, spread, precision=HIGHEST, preferred_element_type=F32)


class Layout:
    def __init__(self):
        wide = 2 * REACH + 1
        self.wide = wide
        self.cot = 0
        self.sums = self.cot + 3 * GROUP + 2
        self.minv = self.sums + wide + 2
        self.ratio = self.minv + wide
        self.basis = self.ratio + 5
        self.second = self.basis + 3 * wide
        self.total = self.second + wide


def basis_kernel(counts, sent, *refs):
    height, plane = counts
    lay = Layout()
    wide = lay.wide
    n_in = sum(1 for arr in sent if arr is not None) * height
    msgs = refs[:n_in]
    face_ref, row_a_ref, row_b_ref, omega_ref, quot_ref = refs[n_in : n_in + 5]
    fields_ref, info_ref = refs[n_in + 5 : n_in + 7]
    pool, coef, weigh = refs[n_in + 7 :]
    depth, _, span = pool.shape[1:]
    own_depth = depth // height
    elems = depth // 8
    own_elems = elems // height
    height_pos = lax.axis_index("height")
    plane_pos = lax.axis_index("plane")
    member = lax.rem(plane_pos, GROUP)
    group = plane_pos // GROUP
    even = lax.rem(group, 2) == 0
    early = lax.rem(group // 2, 2) == 0

    def stage(msg, piece, slot, block):
        rows = own_depth * 8 + (-(-(2 * own_elems) // 8)) * 8
        top = piece * rows
        pool[lay.cot + slot, pl.ds(block * own_depth, own_depth)] = msg[top : top + own_depth * 8, :].reshape(own_depth, 8, span)
        for kind in range(2):
            for elem in range(own_elems):
                at = top + own_depth * 8 + kind * own_elems + elem
                coef[slot, kind, block * own_elems + elem] = jnp.broadcast_to(msg[at : at + 1, :], (8, span))

    def blank(slot):
        pool[lay.cot + slot] = jnp.zeros((depth, 8, span), F32)
        coef[slot] = jnp.zeros(coef.shape[1:], F32)

    present = [name for name, arr in zip(("own", "pair", "cross", "far1", "far2"), sent) if arr is not None]
    for missing, slot in (("pair", None), ("cross", None)):
        if missing not in present:
            for piece in range(GROUP):
                base = jnp.where(even, 1 + 2 * GROUP, 1) if missing == "pair" else jnp.where(even, 1, 1 + 2 * GROUP)
                blank(base + piece)
    if "far1" not in present or "far2" not in present:
        if "far1" in present:
            blank(jnp.where(early, 0, 3 * GROUP + 1))
        else:
            blank(0)
            blank(3 * GROUP + 1)
    step = len(present)
    for turn in range(height):
        block = lax.rem(height_pos - turn + height, height)
        for pos, name in enumerate(present):
            msg = msgs[turn * step + pos]
            if name in ("own", "pair", "cross"):
                if name == "own":
                    base = 1 + GROUP
                elif name == "pair":
                    base = jnp.where(even, 1 + 2 * GROUP, 1)
                else:
                    base = jnp.where(even, 1, 1 + 2 * GROUP)
                for piece in range(GROUP):
                    stage(msg, piece, base + jnp.bitwise_xor(member, piece), block)
            else:
                first = early if name == "far1" else jnp.logical_not(early)
                stage(msg, 0, jnp.where(first, 3 * GROUP + 1, 0), block)

    lane = lax.broadcasted_iota(jnp.int32, (8, span), 1)
    sub = lax.broadcasted_iota(jnp.int32, (8, span), 0)
    opens = (lane % 8 == 0) & (lane > 0)
    closes = (lane % 8 == 7) & (lane < span - 1)

    def join_span(values):
        return values + jnp.where(opens, pltpu.roll(values, 1, 2), jnp.where(closes, pltpu.roll(values, span - 1, 2), 0.0))

    def join_depth(values):
        planes = []
        for elem in range(elems):
            first, last = values[elem * 8], values[elem * 8 + 7]
            if elem > 0:
                first = first + values[elem * 8 - 1]
            if elem < elems - 1:
                last = last + values[elem * 8 + 8]
            planes += [first[None], values[elem * 8 + 1 : elem * 8 + 7], last[None]]
        return jnp.concatenate(planes, axis=0)

    def join_width(base, at):
        low = pltpu.roll(pool[base + at - 1], 1, 1)
        high = pltpu.roll(pool[base + at + 1], 7, 1)
        return pool[base + at] + jnp.where(sub == 0, low, jnp.where(sub == 7, high, 0.0))

    def per_elem(slot, kind, count=elems, start=0):
        return jnp.concatenate([jnp.broadcast_to(coef[slot, kind, start + e][None], (8, 8, span)) for e in range(count)], axis=0)

    def omega(count=elems):
        return jnp.concatenate([omega_ref[...]] * count, axis=0)

    def operator(values, slot, start=0):
        count = values.shape[0] // 8
        flat = values.reshape(count * 64, span)
        one = flat.astype(jnp.bfloat16)
        rest = flat - one.astype(F32)
        two = rest.astype(jnp.bfloat16)
        three = (rest - two.astype(F32)).astype(jnp.bfloat16)
        split = (one, two, three)
        both = jnp.dot(jnp.concatenate([one, two], axis=1), row_a_ref[...], preferred_element_type=F32)
        lin = both[:, :span] + both[:, span:] + jnp.dot(jnp.concatenate([one, three], axis=1), row_b_ref[...], preferred_element_type=F32)
        blocks = []
        for e in range(count):
            stack = jnp.concatenate([split[f][e * 64 : e * 64 + 64] for _, f in TERMS], axis=0)
            blocks.append(jnp.dot(face_ref[...], stack, preferred_element_type=F32))
        lin = (lin + jnp.concatenate(blocks, axis=0)).reshape(values.shape)
        return omega(count) * ((INV_STEP * per_elem(slot, 1, count, start)) * values + per_elem(slot, 0, count, start) * lin)

    def loop(start, stop, body):
        if elems > 4:
            lax.fori_loop(start, stop, lambda at, carry: (body(at), carry)[1], 0)
        else:
            for at in range(start, stop):
                body(at)

    diag_at, mass_at = lay.basis + wide, lay.second - 1

    def start_slab(at):
        slot = member + at
        heavy = omega() * (INV_STEP * per_elem(slot, 1))
        pool[lay.sums + at] = join_depth(join_span(heavy * pool[lay.cot + slot]))
        quot = jnp.concatenate([quot_ref[...]] * elems, axis=0)
        pool[diag_at + at] = join_depth(join_span(heavy + omega() * per_elem(slot, 0) * quot))

    def mass_slab(at):
        pool[mass_at + at - 1] = join_depth(join_span(omega() * (INV_STEP * per_elem(member + at, 1))))

    def first_slab(at):
        diag = join_width(diag_at, at)
        inverse = jnp.where(diag > 0.0, 1.0 / jnp.where(diag > 0.0, diag, 1.0), 0.0)
        pool[lay.minv + at - 1] = inverse
        pool[lay.basis + at - 1] = inverse * join_width(lay.sums, at)

    def ratio_slab(at):
        pool[lay.ratio + at - 3] = pool[lay.minv + at - 1] * join_width(mass_at - 1, at)

    loop(0, wide + 2, start_slab)
    loop(2, wide, mass_slab)
    loop(1, wide + 1, first_slab)
    loop(3, wide - 1, ratio_slab)

    mid = REACH + 1
    own = pl.ds(height_pos * own_depth, own_depth)
    zpos = lax.broadcasted_iota(jnp.int32, (own_depth, 8, span), 0) + height_pos * own_depth
    xpos = lax.broadcasted_iota(jnp.int32, (own_depth, 8, span), 1) + plane_pos * 8

    def copies(pos, extent):
        return jnp.where(((pos % 8 == 7) & (pos < extent - 1)) | ((pos % 8 == 0) & (pos > 0)), 0.5, 1.0)

    share = copies(zpos, depth) * copies(xpos, plane * 8) * jnp.where(opens | closes, 0.5, 1.0)
    weigh[...] = share / pool[lay.minv + REACH, own]

    for level in range(2):
        def apply(at, level=level):
            pool[lay.sums + at] = join_depth(join_span(operator(pool[lay.basis + level * wide + at - 1], member + at)))

        def advance(at, level=level):
            pool[lay.basis + (level + 1) * wide + at - 1] = (
                pool[lay.minv + at - 1] * join_width(lay.sums, at) - SHIFTS[level] * pool[lay.basis + level * wide + at - 1]
            )

        loop(1 + level, wide + 1 - level, apply)
        loop(2 + level, wide - level, advance)

    def second(vec):
        def begin(at):
            pool[lay.second + at - 3] = pool[lay.ratio + at - 3] * pool[lay.basis + vec * wide + at - 1]

        loop(3, 8, begin)
        for level in range(2):
            here = lay.second + (0, 5, 8)[level] - 3 - level
            after = lay.second + (0, 5, 8)[level + 1] - 4 - level

            def apply(at, here=here):
                pool[lay.sums + at] = join_depth(join_span(operator(pool[here + at], member + at)))

            def advance(at, here=here, after=after, level=level):
                pool[after + at] = pool[lay.minv + at - 1] * join_width(lay.sums, at) - SHIFTS[level] * pool[here + at]

            loop(3 + level, 8 - level, apply)
            loop(4 + level, 7 - level, advance)
        fields_ref[3 + vec] = pool[lay.second + 2, own]
        fields_ref[6 + vec] = pool[lay.second + 6, own]
        fields_ref[9 + vec] = pool[lay.second + 8, own]

    for vec in range(3):
        fields_ref[vec] = pool[lay.basis + vec * wide + REACH, own]
    loop(0, 3, second)

    slot = member + mid
    start = height_pos * own_elems

    def total(values):
        return jnp.sum(values, axis=0)

    def weighted(index):
        return weigh[...] * fields_ref[index]

    parts = []
    left = [weighted(i) for i in range(3)]
    parts += [total(left[i] * fields_ref[j]) for i, j in PAIRS]
    parts.append(total(fields_ref[2] * operator(fields_ref[2], slot, start)))
    for k, l in PAIRS:
        pairs = PAIRS if k == l else [(i, j) for i in range(3) for j in range(3)]
        left = [weighted(3 + 3 * k + i) for i in range(3)]
        parts += [total(left[i] * fields_ref[3 + 3 * l + j]) for i, j in pairs]
    energy = [operator(fields_ref[9 + j], slot, start) for j in range(3)]
    parts += [total(fields_ref[9 + i] * energy[j]) for i, j in PAIRS]
    lines = [jnp.sum(part, axis=0, keepdims=True) for part in parts]
    lines.append(jnp.zeros((span - len(lines), span), F32))
    sums = lax.dot_general(jnp.ones((8, span), F32), jnp.concatenate(lines, axis=0), (((1,), (1,)), ((), ())), precision=HIGHEST, preferred_element_type=F32)

    heavy = omega(own_elems) * (INV_STEP * per_elem(slot, 1, own_elems, start))
    rows = []
    for index in range(12):
        mass = heavy * fields_ref[index]
        for elem in range(own_elems):
            rows.append(jnp.sum(jnp.sum(mass[elem * 8 : elem * 8 + 8], axis=0), axis=0, keepdims=True))
    rows = jnp.concatenate(rows, axis=0)
    cells = span // 8
    per_row = span // cells
    spread = (lax.broadcasted_iota(jnp.int32, (span, span), 0) // 8 == lax.broadcasted_iota(jnp.int32, (span, span), 1) % cells).astype(F32)
    rows = jnp.dot(rows, spread, precision=HIGHEST, preferred_element_type=F32)
    place = lax.broadcasted_iota(jnp.int32, rows.shape, 0) % per_row == lax.broadcasted_iota(jnp.int32, rows.shape, 1) // cells
    rows = jnp.where(place, rows, 0.0).reshape(rows.shape[0] // per_row, per_row, span)
    packed = jnp.sum(rows, axis=1)
    info_ref[...] = jnp.concatenate([packed, sums[:1]], axis=0)


def galerkin(gram, energy):
    n00, n01, n02, n11, n12, n22 = gram
    h00, h01, h02 = n01 + SHIFTS[0] * n00, n11 + SHIFTS[0] * n01, n12 + SHIFTS[0] * n02
    h11, h12 = n12 + SHIFTS[1] * n11, n22 + SHIFTS[1] * n12
    low10, low20 = h01 / h00, h02 / h00
    piv1 = h11 - low10 * h01
    off12 = h12 - low10 * h02
    low21 = off12 / piv1
    piv2 = energy - low20 * h02 - low21 * off12
    y0 = n00
    y1 = n01 - low10 * y0
    y2 = n02 - low20 * y0 - low21 * y1
    c2 = y2 / piv2
    c1 = y1 / piv1 - low21 * c2
    c0 = y0 / h00 - low10 * c1 - low20 * c2
    return c0, c1, c2


def combine_kernel(info_ref, fields_ref, owner_ref, place_ref, second_ref, first_ref, grad_ref):
    devices, lines, span = info_ref.shape
    ones = jnp.ones((devices, span), F32)
    contract = (((0,), (0,)), ((), ()))
    wide = lax.dot_general(info_ref[:, lines - 1, :], ones, contract, precision=HIGHEST, preferred_element_type=F32)
    take = [wide[i : i + 1, :] for i in range(7 + 45 + 6)]
    coef = galerkin(take[:6], take[6])
    at = 7
    double = [(2.0 if i != j else 1.0) * coef[i] * coef[j] for i, j in PAIRS]
    every = [coef[i] * coef[j] for i in range(3) for j in range(3)]
    gram = []
    for k, l in PAIRS:
        factors = double if k == l else every
        gram.append(sum(f * t for f, t in zip(factors, take[at : at + len(factors)])))
        at += len(factors)
    energy = sum(f * t for f, t in zip(double, take[at : at + 6]))
    outer = galerkin(gram, energy)
    factors = list(coef) + [d * c for d in outer for c in coef]

    second_ref[...] = factors[0] * fields_ref[0] + factors[1] * fields_ref[1] + factors[2] * fields_ref[2]
    first = factors[3] * fields_ref[3]
    for i in range(4, 12):
        first = first + factors[i] * fields_ref[i]
    first_ref[...] = first

    per_line = 12 // (lines - 1)
    cells = span // per_line
    row = lax.broadcasted_iota(jnp.int32, (span, span), 0)
    for step in range(2):
        holder = (owner_ref[step : step + 1, :] == lax.broadcasted_iota(jnp.int32, (devices, span), 0)).astype(F32)
        here = place_ref[step : step + 1, :] == row % cells
        result = jnp.zeros((1, span), F32)
        for line in range(lines - 1):
            fields = [f for f in range(line * per_line, (line + 1) * per_line) if (f >= 3) == (step == 0)]
            if not fields:
                continue
            picked = lax.dot_general(info_ref[:, line, :], holder, contract, precision=HIGHEST, preferred_element_type=F32)
            picked = jnp.where(here, picked, 0.0)
            for f in fields:
                lo = (f - line * per_line) * cells
                result = result + factors[f] * jnp.sum(picked[lo : lo + cells], axis=0, keepdims=True)
        grad_ref[step : step + 1, :] = result * (1.0 / (8.0 * INV_STEP))


def per_device(counts, cotangent, conductivity, capacity, sources):
    height, plane = counts
    depth, _, span = cotangent.shape
    elems = depth // 8
    cells = span // 8
    vmem = pl.BlockSpec(memory_space=pltpu.VMEM)

    rows = depth * 8 + -(-(2 * elems) // 8) * 8
    message = pl.pallas_call(
        pack_kernel,
        out_shape=jax.ShapeDtypeStruct((rows, span), F32),
        in_specs=[vmem] * 3,
        out_specs=vmem,
    )(cotangent, conductivity, capacity)

    member = lax.axis_index("plane") % GROUP
    group = lax.axis_index("plane") // GROUP
    groups = plane // GROUP
    gathered = message
    width = 1
    while width < GROUP:
        other = swap(gathered, "plane", [(p, p ^ width) for p in range(plane) if p & width == 0])
        gathered = jnp.concatenate([gathered, other], axis=0)
        width *= 2

    def group_pairs(first, gap):
        return [(g * GROUP + m, (g + gap) * GROUP + m) for g in range(groups - gap) if first(g) for m in range(GROUP)]

    pair = swap(gathered, "plane", group_pairs(lambda g: g % 2 == 0, 1))
    cross = swap(gathered, "plane", group_pairs(lambda g: g % 2 == 1, 1))
    slabs = gathered.reshape(GROUP, rows, span)
    far = []
    for turn in range(2):
        pairs = group_pairs(lambda g, turn=turn: (g // 2) % 2 == turn, 2)
        if pairs:
            ends = jnp.where((group // 2) % 2 == turn, GROUP - 1, 0)
            edge = lax.dynamic_index_in_dim(slabs, jnp.bitwise_xor(member, ends), 0, keepdims=False)
            far.append(swap(edge, "plane", pairs))
        else:
            far.append(None)
    sent = (gathered, pair, cross, *far)
    blocks = [arr for arr in sent if arr is not None]
    operands = list(blocks)
    for turn in range(1, height):
        operands += [lax.ppermute(arr, "height", [(h, (h + turn) % height) for h in range(height)]) for arr in blocks]

    lay = Layout()
    consts = tables(span)
    slots = 3 * GROUP + 2
    fields, info = pl.pallas_call(
        functools.partial(basis_kernel, counts, tuple(None if arr is None else 0 for arr in sent)),
        out_shape=(jax.ShapeDtypeStruct((12, depth, 8, span), F32), jax.ShapeDtypeStruct((12 * elems * cells // span + 1, span), F32)),
        in_specs=[vmem] * (len(operands) + len(consts)),
        out_specs=(vmem, vmem),
        scratch_shapes=[
            pltpu.VMEM((lay.total, depth * height, 8, span), F32),
            pltpu.VMEM((slots, 2, elems * height, 8, span), F32),
            pltpu.VMEM((depth, 8, span), F32),
        ],
        compiler_params=pltpu.CompilerParams(vmem_limit_bytes=56 * 1024 * 1024),
    )(*operands, *[jnp.asarray(c) for c in consts])

    devices = height * plane
    shared = lax.all_to_all(jnp.broadcast_to(info[None], (devices, *info.shape)), ("height", "plane"), 0, 0, tiled=True)

    cell = sources % cells
    column = sources // cells
    wide_elem = column % plane
    deep_elem = column // plane
    owner = (deep_elem // elems) * plane + wide_elem
    place = (deep_elem % elems) * cells + cell
    return pl.pallas_call(
        combine_kernel,
        out_shape=(
            jax.ShapeDtypeStruct(cotangent.shape, F32),
            jax.ShapeDtypeStruct(cotangent.shape, F32),
            jax.ShapeDtypeStruct(sources.shape, F32),
        ),
        in_specs=[vmem] * 4,
        out_specs=(vmem, vmem, vmem),
        compiler_params=pltpu.CompilerParams(vmem_limit_bytes=32 * 1024 * 1024),
    )(shared, fields, owner, place)


def solution(mesh):
    counts = (mesh.shape["height"], mesh.shape["plane"])
    field = P("height", "plane", None)
    return jax.shard_map(
        functools.partial(per_device, counts),
        mesh=mesh,
        in_specs=(field, field, field, P()),
        out_specs=(field, field, P()),
        check_vma=False,
    )
```

```python
import functools

import jax
import jax.numpy as jnp
import ml_dtypes
import numpy as np
from jax import lax
from jax.experimental import pallas as pl
from jax.experimental.pallas import tpu as pltpu
from jax.sharding import PartitionSpec as P

INV_STEP = 20.0
SHIFTS = (0.5, 1.5)
GROUP = 4
REACH = 4
TERMS = ((0, 0), (0, 1), (1, 0), (1, 1), (2, 0))
PAIRS = ((0, 0), (0, 1), (0, 2), (1, 1), (1, 2), (2, 2))
TINY = 1e-30
HIGHEST = lax.Precision.HIGHEST
F32 = jnp.float32
BF16 = jnp.bfloat16


def gll_tables():
    points = np.array([-1.0, -0.8717401485096066, -0.5917001814331423, -0.2092992179024789, 0.2092992179024789, 0.5917001814331423, 0.8717401485096066, 1.0])
    weights = np.array([1.0 / 28.0, 0.2107042271435061, 0.3411226924835044, 0.4124587946587038, 0.4124587946587038, 0.3411226924835044, 0.2107042271435061, 1.0 / 28.0])
    product = np.array([np.prod([points[col] - points[others] for others in range(8) if others != col]) for col in range(8)])
    derivative = np.zeros((8, 8))
    for row in range(8):
        for col in range(8):
            if row != col:
                derivative[row, col] = product[row] / (product[col] * (points[row] - points[col]))
        derivative[row, row] = -np.sum(derivative[row])
    return derivative, weights, np.sum(derivative**2 * weights[:, None], axis=0)


def pieces(matrix):
    out, rest = [], matrix
    for _ in range(3):
        piece = rest.astype(ml_dtypes.bfloat16)
        out.append(piece)
        rest = rest - piece.astype(np.float64)
    return out


def tables(span):
    derivative, weights, stiff = gll_tables()
    line = (derivative.T * weights) @ derivative / weights[:, None]
    eye = np.eye(8)
    face = pieces(np.kron(line, eye) + np.kron(eye, line))
    face_mat = np.concatenate([face[m] for m, _ in TERMS], axis=1)
    ends_mat = np.concatenate([face_mat[0::8], face_mat[7::8]], axis=0)
    row = pieces(np.kron(np.eye(span // 8), line.T))
    row_a = np.concatenate([np.concatenate([row[0], row[1]], 1)] * 2, axis=0)
    none = np.zeros_like(row[2])
    row_b = np.concatenate([np.concatenate([row[2], none], 1), np.concatenate([none, row[2]], 1)], axis=0)
    tile = np.tile(weights, span // 8)
    ratio = stiff / weights
    omega = weights[:, None, None] * weights[None, :, None] * tile[None, None, :]
    quot = ratio[:, None, None] + ratio[None, :, None] + np.tile(ratio, span // 8)[None, None, :]
    return face_mat, ends_mat, row_a, row_b, omega.astype(np.float32), quot.astype(np.float32)


def swap(value, axis, pairs):
    if not pairs:
        return None
    return lax.ppermute(value, axis, [*pairs, *((b, a) for a, b in pairs)])


def coef_rows(elems):
    return -(-(2 * elems) // 8) * 8


def pack_kernel(cot_ref, kap_ref, cap_ref, out_ref, edge_ref):
    depth, _, span = cot_ref.shape
    elems, _, parts = kap_ref.shape
    out_ref[: depth * 8, :] = cot_ref[...].reshape(depth * 8, span)
    spread = (lax.broadcasted_iota(jnp.int32, (parts, span), 1) // 8 == lax.broadcasted_iota(jnp.int32, (parts, span), 0)).astype(F32)
    coef = jnp.concatenate([kap_ref[...].reshape(elems, parts) * (1.0 / INV_STEP), cap_ref[...].reshape(elems, parts)], axis=0)
    rows = coef_rows(elems)
    if rows > 2 * elems:
        coef = jnp.concatenate([coef, jnp.zeros((rows - 2 * elems, parts), F32)], axis=0)
    coef = jnp.dot(coef, spread, precision=HIGHEST, preferred_element_type=F32)
    out_ref[depth * 8 :, :] = coef
    last = lax.rem(lax.axis_index("plane"), GROUP) == GROUP - 1
    edge_ref[:depth, :] = jnp.where(last, cot_ref[:, 7, :], cot_ref[:, 0, :])
    edge_ref[depth:, :] = coef


class Layout:
    def __init__(self):
        wide = 2 * REACH + 1
        self.wide = wide
        self.cot = 0
        self.sums = self.cot + 3 * GROUP + 2
        self.minv = self.sums + wide + 2
        self.ratio = self.minv + wide
        self.basis = self.ratio + 5
        self.second = self.basis + 3 * wide
        self.total = self.second + wide


def basis_kernel(counts, present, *refs):
    height, plane = counts
    lay = Layout()
    wide = lay.wide
    n_in = len(present) * height
    msgs = refs[:n_in]
    face_ref, ends_ref, row_a_ref, row_b_ref, omega_ref, quot_ref = refs[n_in : n_in + 6]
    fields_ref, info_ref = refs[n_in + 6 : n_in + 8]
    pool, coef, weigh = refs[n_in + 8 :]
    rows, span = pool.shape[1:]
    depth = rows // 8
    own_depth = depth // height
    own_rows = own_depth * 8
    elems = depth // 8
    own_elems = elems // height
    height_pos = lax.axis_index("height")
    plane_pos = lax.axis_index("plane")
    member = lax.rem(plane_pos, GROUP)
    even = lax.rem(plane_pos // GROUP, 2) == 0
    slab_rows = own_rows + coef_rows(own_elems)
    whole = elems > 4

    def stage_coef(msg, top, slot, block):
        for kind in range(2):
            for elem in range(own_elems):
                at = top + kind * own_elems + elem
                coef[slot, kind, block * own_elems + elem] = jnp.broadcast_to(msg[at : at + 1, :], (8, span))

    def stage(msg, piece, slot, block):
        top = piece * slab_rows
        pool[lay.cot + slot, pl.ds(pl.multiple_of(block * own_rows, own_rows), own_rows)] = msg[top : top + own_rows, :]
        stage_coef(msg, top + own_rows, slot, block)

    def stage_face(msg, slot, block):
        top = GROUP * slab_rows
        face = msg[top : top + own_depth, :]
        spread = jnp.concatenate([jnp.broadcast_to(face[z : z + 1], (8, span)) for z in range(own_depth)], axis=0)
        pool[lay.cot + slot, pl.ds(pl.multiple_of(block * own_rows, own_rows), own_rows)] = spread
        stage_coef(msg, top + own_depth, slot, block)

    def sides(name):
        after = even if name == "pair" else jnp.logical_not(even)
        return jnp.where(after, 1 + 2 * GROUP, 1), jnp.where(after, 3 * GROUP + 1, 0)

    for name in ("pair", "cross"):
        if name not in present:
            base, beyond = sides(name)
            for slot in [base + piece for piece in range(GROUP)] + [beyond]:
                pool[lay.cot + slot] = jnp.zeros((rows, span), F32)
                coef[slot] = jnp.zeros(coef.shape[1:], F32)
    for turn in range(height):
        block = lax.rem(height_pos - turn + height, height)
        for pos, name in enumerate(present):
            msg = msgs[turn * len(present) + pos]
            if name == "own":
                base = 1 + GROUP
            else:
                base, beyond = sides(name)
                stage_face(msg, beyond, block)
            for piece in range(GROUP):
                stage(msg, piece, base + jnp.bitwise_xor(member, piece), block)

    lane = lax.broadcasted_iota(jnp.int32, (8, span), 1)
    sub = lax.broadcasted_iota(jnp.int32, (8, span), 0)
    opens = (lane % 8 == 0) & (lane > 0)
    closes = (lane % 8 == 7) & (lane < span - 1)

    def tall(mask, like):
        return jnp.concatenate([mask] * (like.shape[0] // 8), axis=0) if like.shape[0] > 8 else mask

    def join_span(values):
        up, down = pltpu.roll(values, 1, 1), pltpu.roll(values, span - 1, 1)
        return values + jnp.where(tall(opens, values), up, jnp.where(tall(closes, values), down, 0.0))

    def join_depth(values):
        planes = []
        for elem in range(elems):
            top = elem * 64
            first, last = values[top : top + 8], values[top + 56 : top + 64]
            if elem > 0:
                first = first + values[top - 8 : top]
            if elem < elems - 1:
                last = last + values[top + 64 : top + 72]
            planes += [first, values[top + 8 : top + 56], last]
        return jnp.concatenate(planes, axis=0)

    def face_at(at, width_node):
        return lay.sums + at, pl.ds(width_node, depth, stride=8)

    def join_width(at):
        low, high = face_at(at, 7), face_at(at + 1, 0)
        both = pool[low] + pool[high]
        pool[low] = both
        pool[high] = both

    def loop(start, stop, body, step=1):
        if whole:
            lax.fori_loop(start, stop, lambda at, carry: (body([at]), carry)[1], 0)
        else:
            for at in range(start, stop, step):
                body(list(range(at, min(at + step, stop))))

    def each(body):
        return lambda slabs: [body(at) for at in slabs]

    def split(values):
        one = values.astype(BF16)
        return one, (values - one.astype(F32)).astype(BF16)

    def along_span(halves):
        wides = [jnp.dot(jnp.concatenate(h, axis=1), row_a_ref[...], preferred_element_type=F32) for h in halves]
        if len(halves) == 2:
            extra = jnp.dot(jnp.concatenate([halves[0][0], halves[1][0]], axis=1), row_b_ref[...], preferred_element_type=F32)
            extras = [extra[:, :span], extra[:, span:]]
        else:
            extras = [jnp.dot(halves[0][0], row_b_ref[:span, :span], preferred_element_type=F32)]
        return [(w[:, :span] + w[:, span:]) + x for w, x in zip(wides, extras)]

    def along_face(matrix, halves, elem):
        top = elem * 64
        stacks = [jnp.concatenate([h[f][top : top + 64] for _, f in TERMS], axis=0) for h in halves]
        return jnp.dot(matrix, stacks[0] if len(stacks) == 1 else jnp.concatenate(stacks, axis=1), preferred_element_type=F32)

    def scaled(slot, kind, elem, scale):
        value = coef[slot, kind, elem]
        return value if scale == 1.0 else value * scale

    def operator(fields, slots, scale=1.0, start=0):
        halves = [split(v) for v in fields]
        lines = along_span(halves)
        out = [[] for _ in fields]
        for elem in range(fields[0].shape[0] // 64):
            top = elem * 64
            face = along_face(face_ref[...], halves, elem)
            for i, v in enumerate(fields):
                cap = tall(scaled(slots[i], 1, start + elem, scale), face)
                kap = tall(scaled(slots[i], 0, start + elem, scale), face)
                lin = lines[i][top : top + 64] + face[:, i * span : (i + 1) * span]
                out[i].append(cap * v[top : top + 64] + kap * lin)
        return [jnp.concatenate(o, axis=0) for o in out]

    def ends(sources, at, scale):
        halves = [split(pool[s]) for s in sources]
        edges = [pool[s, pl.ds(node, depth, stride=8)] for s, node in zip(sources, (7, 0))]
        lines = along_span([split(jnp.concatenate(edges, axis=0))])[0]
        both = [along_face(ends_ref[...], halves, elem) for elem in range(elems)]
        for i in range(2):
            joined = []
            for elem in range(elems):
                lin = lines[i * depth + elem * 8 : i * depth + elem * 8 + 8] + both[elem][8 * (1 - i) : 8 * (2 - i), i * span : (i + 1) * span]
                slot = member + at[i]
                joined.append(join_span(scaled(slot, 1, elem, scale) * edges[i][elem * 8 : elem * 8 + 8] + scaled(slot, 0, elem, scale) * lin))
            final = []
            for elem in range(elems):
                value = joined[elem]
                if elem > 0:
                    value = value + jnp.where(sub == 0, pltpu.roll(joined[elem - 1], 1, 0), 0.0)
                if elem < elems - 1:
                    value = value + jnp.where(sub == 7, pltpu.roll(joined[elem + 1], 7, 0), 0.0)
                final.append(value)
            pool[face_at(at[i], (7, 0)[i])] = jnp.concatenate(final, axis=0)

    def step(here, after, low, high, shift):
        def apply(slabs):
            made = operator([pool[here + at] for at in slabs], [member + at for at in slabs], 1.0 / shift)
            for at, value in zip(slabs, made):
                pool[lay.sums + at] = join_depth(join_span(value))

        def advance(at):
            pool[after + at] = pool[lay.minv + at - 1] * pool[lay.sums + at] - pool[here + at]

        ends((here + low, here + high), (low, high), 1.0 / shift)
        loop(low + 1, high, apply, 2)
        loop(low, high, each(join_width))
        loop(low + 1, high, each(advance))

    def constant(kind, at):
        layers = [[join_span(coef[member + at + side, kind, elem]) for elem in range(elems)] for side in (-1, 0, 1)]
        wide_sum = lambda low, mid, high: mid + jnp.where(sub == 0, low, jnp.where(sub == 7, high, 0.0))
        inside = [wide_sum(*(layers[side][elem] for side in range(3))) for elem in range(elems)]
        planes = []
        for elem in range(elems):
            first = inside[elem] if elem == 0 else inside[elem] + inside[elem - 1]
            last = inside[elem] if elem == elems - 1 else inside[elem] + inside[elem + 1]
            planes += [first] + [inside[elem]] * 6 + [last]
        return jnp.concatenate(planes, axis=0)

    def start_slab(at):
        cap = jnp.concatenate([tall(coef[member + at, 1, elem], face_ref) for elem in range(elems)], axis=0)
        pool[lay.sums + at] = join_depth(join_span(cap * pool[lay.cot + member + at]))

    def inverse_slab(at):
        quot = jnp.concatenate([quot_ref[...].reshape(64, span)] * elems, axis=0)
        mass = constant(1, at)
        inverse = 1.0 / jnp.maximum(mass + quot * constant(0, at), TINY)
        pool[lay.minv + at - 1] = inverse
        return inverse, mass

    def first_slab(at):
        inverse, _ = inverse_slab(at)
        pool[lay.basis + at - 1] = inverse * pool[lay.sums + at]

    def inner_slab(at):
        inverse, mass = inverse_slab(at)
        pool[lay.basis + at - 1] = inverse * pool[lay.sums + at]
        pool[lay.ratio + at - 3] = inverse * mass

    loop(0, wide + 2, each(start_slab))
    loop(0, wide + 1, each(join_width))
    loop(1, 3, each(first_slab))
    loop(3, wide - 1, each(inner_slab))
    loop(wide - 1, wide + 1, each(first_slab))

    mid = REACH + 1
    own = pl.ds(pl.multiple_of(height_pos * own_rows, own_rows), own_rows)
    shape = (own_depth, 8, span)
    zpos = lax.broadcasted_iota(jnp.int32, shape, 0) + height_pos * own_depth
    xpos = lax.broadcasted_iota(jnp.int32, shape, 1) + plane_pos * 8

    def copies(pos, extent):
        return jnp.where(((pos % 8 == 7) & (pos < extent - 1)) | ((pos % 8 == 0) & (pos > 0)), 0.5, 1.0)

    share = copies(zpos, depth) * copies(xpos, plane * 8) * jnp.where(opens | closes, 0.5, 1.0)
    omega = jnp.concatenate([omega_ref[...].reshape(64, span)] * own_elems, axis=0)
    weigh[...] = share.reshape(own_rows, span) * omega / pool[lay.minv + REACH, own]

    for level in range(2):
        step(lay.basis + level * wide - 1, lay.basis + (level + 1) * wide - 1, 1 + level, wide - level, SHIFTS[level])
    for vec in range(3):
        fields_ref[vec] = pool[lay.basis + vec * wide + REACH, own]

    def second(vec):
        def begin(at):
            pool[lay.second + at - 3] = pool[lay.ratio + at - 3] * pool[lay.basis + vec * wide + at - 1]

        loop(3, 8, each(begin))
        step(lay.second - 3, lay.second + 1, 3, 7, SHIFTS[0])
        step(lay.second + 1, lay.second + 3, 4, 6, SHIFTS[1])
        fields_ref[3 + vec] = pool[lay.second + 2, own]
        fields_ref[6 + vec] = pool[lay.second + 6, own]
        fields_ref[9 + vec] = pool[lay.second + 8, own]

    loop(0, 3, each(second))

    slot = member + mid
    start = height_pos * own_elems

    def total(values):
        return jnp.sum(values.reshape(shape), axis=0)

    parts = []
    left = [weigh[...] * fields_ref[i] for i in range(3)]
    parts += [total(left[i] * fields_ref[j]) for i, j in PAIRS]
    lasts = (2, 9, 10, 11)
    energy = []
    for k in (0, 2):
        energy += operator([fields_ref[i] for i in lasts[k : k + 2]], [slot] * 2, 1.0, start)
    energy = [omega * e for e in energy]
    parts.append(total(fields_ref[2] * energy[0]))
    for k, l in PAIRS:
        pairs = PAIRS if k == l else [(i, j) for i in range(3) for j in range(3)]
        left = [weigh[...] * fields_ref[3 + 3 * k + i] for i in range(3)]
        parts += [total(left[i] * fields_ref[3 + 3 * l + j]) for i, j in pairs]
    parts += [total(fields_ref[9 + i] * energy[1 + j]) for i, j in PAIRS]
    lines = [jnp.sum(part, axis=0, keepdims=True) for part in parts]
    lines.append(jnp.zeros((span - len(lines), span), F32))
    sums = lax.dot_general(jnp.ones((8, span), F32), jnp.concatenate(lines, axis=0), (((1,), (1,)), ((), ())), precision=HIGHEST, preferred_element_type=F32)

    heavy = jnp.concatenate([tall(coef[slot, 1, start + elem], face_ref) for elem in range(own_elems)], axis=0) * (omega * 0.125)
    rows_of = []
    for index in range(12):
        mass = heavy * fields_ref[index]
        for elem in range(own_elems):
            rows_of.append(jnp.sum(mass[elem * 64 : elem * 64 + 64], axis=0, keepdims=True))
    stack = jnp.concatenate(rows_of, axis=0)
    cells = span // 8
    per_row = span // cells
    spread = (lax.broadcasted_iota(jnp.int32, (span, span), 0) // 8 == lax.broadcasted_iota(jnp.int32, (span, span), 1) % cells).astype(F32)
    stack = jnp.dot(stack, spread, precision=HIGHEST, preferred_element_type=F32)
    place = lax.broadcasted_iota(jnp.int32, stack.shape, 0) % per_row == lax.broadcasted_iota(jnp.int32, stack.shape, 1) // cells
    stack = jnp.where(place, stack, 0.0).reshape(stack.shape[0] // per_row, per_row, span)
    info = jnp.concatenate([jnp.sum(stack, axis=1), sums[:1]], axis=0)
    info_ref[...] = jnp.broadcast_to(info[None], info_ref.shape)


def galerkin(gram, energy):
    n00, n01, n02, n11, n12, n22 = gram
    first, later = SHIFTS
    h00, h01, h02 = first * (n01 + n00), first * (n11 + n01), first * (n12 + n02)
    h11, h12 = later * (n12 + n11), later * (n22 + n12)
    low10, low20 = h01 / h00, h02 / h00
    piv1 = h11 - low10 * h01
    off12 = h12 - low10 * h02
    low21 = off12 / piv1
    piv2 = energy - low20 * h02 - low21 * off12
    y0 = n00
    y1 = n01 - low10 * y0
    y2 = n02 - low20 * y0 - low21 * y1
    c2 = y2 / piv2
    c1 = y1 / piv1 - low21 * c2
    c0 = y0 / h00 - low10 * c1 - low20 * c2
    return c0, c1, c2


def combine_kernel(info_ref, fields_ref, owner_ref, place_ref, second_ref, first_ref, grad_ref):
    devices, lines, span = info_ref.shape
    ones = jnp.ones((devices, span), F32)
    contract = (((0,), (0,)), ((), ()))
    wide = lax.dot_general(info_ref[:, lines - 1, :], ones, contract, precision=HIGHEST, preferred_element_type=F32)
    take = [wide[i : i + 1, :] for i in range(7 + 45 + 6)]
    coef = galerkin(take[:6], take[6])
    at = 7
    double = [(2.0 if i != j else 1.0) * coef[i] * coef[j] for i, j in PAIRS]
    every = [coef[i] * coef[j] for i in range(3) for j in range(3)]
    gram = []
    for k, l in PAIRS:
        factors = double if k == l else every
        gram.append(sum(f * t for f, t in zip(factors, take[at : at + len(factors)])))
        at += len(factors)
    energy = sum(f * t for f, t in zip(double, take[at : at + 6]))
    outer = galerkin(gram, energy)
    factors = list(coef) + [d * c for d in outer for c in coef]

    second = factors[0] * fields_ref[0] + factors[1] * fields_ref[1] + factors[2] * fields_ref[2]
    second_ref[...] = second.reshape(second_ref.shape)
    first = factors[3] * fields_ref[3]
    for i in range(4, 12):
        first = first + factors[i] * fields_ref[i]
    first_ref[...] = first.reshape(first_ref.shape)

    per_line = 12 // (lines - 1)
    cells = span // per_line
    row = lax.broadcasted_iota(jnp.int32, (span, span), 0)
    for step in range(2):
        holder = (owner_ref[step : step + 1, :] == lax.broadcasted_iota(jnp.int32, (devices, span), 0)).astype(F32)
        here = place_ref[step : step + 1, :] == row % cells
        result = jnp.zeros((1, span), F32)
        for line in range(lines - 1):
            fields = [f for f in range(line * per_line, (line + 1) * per_line) if (f >= 3) == (step == 0)]
            if not fields:
                continue
            picked = lax.dot_general(info_ref[:, line, :], holder, contract, precision=HIGHEST, preferred_element_type=F32)
            picked = jnp.where(here, picked, 0.0)
            for f in fields:
                lo = (f - line * per_line) * cells
                result = result + factors[f] * jnp.sum(picked[lo : lo + cells], axis=0, keepdims=True)
        grad_ref[step : step + 1, :] = result


def per_device(counts, cotangent, conductivity, capacity, sources):
    height, plane = counts
    depth, _, span = cotangent.shape
    elems = depth // 8
    cells = span // 8
    groups = plane // GROUP
    devices = height * plane
    vmem = pl.BlockSpec(memory_space=pltpu.VMEM)

    rows = depth * 8 + coef_rows(elems)
    message, edge = pl.pallas_call(
        pack_kernel,
        out_shape=(jax.ShapeDtypeStruct((rows, span), F32), jax.ShapeDtypeStruct((depth + coef_rows(elems), span), F32)),
        in_specs=[vmem] * 3,
        out_specs=(vmem, vmem),
    )(cotangent, conductivity, capacity)

    beyond = swap(edge, "plane", [(g * GROUP + GROUP - 1, (g + 1) * GROUP) for g in range(groups - 1)])
    gathered = message
    width = 1
    while width < GROUP:
        other = swap(gathered, "plane", [(p, p ^ width) for p in range(plane) if p & width == 0])
        gathered = jnp.concatenate([gathered, other], axis=0)
        width *= 2
    gathered = jnp.concatenate([gathered, edge if beyond is None else beyond], axis=0)

    def group_pairs(turn):
        return [(g * GROUP + m, (g + 1) * GROUP + m) for g in range(turn, groups - 1, 2) for m in range(GROUP)]

    sent = {"own": gathered, "pair": swap(gathered, "plane", group_pairs(0)), "cross": swap(gathered, "plane", group_pairs(1))}
    present = tuple(name for name, arr in sent.items() if arr is not None)
    operands = [sent[name] for name in present]
    for turn in range(1, height):
        operands += [lax.ppermute(sent[name], "height", [(h, (h + turn) % height) for h in range(height)]) for name in present]

    lay = Layout()
    consts = tables(span)
    slots = 3 * GROUP + 2
    fields, info = pl.pallas_call(
        functools.partial(basis_kernel, counts, present),
        out_shape=(jax.ShapeDtypeStruct((12, depth * 8, span), F32), jax.ShapeDtypeStruct((devices, 12 * elems * cells // span + 1, span), F32)),
        in_specs=[vmem] * (len(operands) + len(consts)),
        out_specs=(vmem, vmem),
        scratch_shapes=[
            pltpu.VMEM((lay.total, depth * 8 * height, span), F32),
            pltpu.VMEM((slots, 2, elems * height, 8, span), F32),
            pltpu.VMEM((depth * 8, span), F32),
        ],
        compiler_params=pltpu.CompilerParams(vmem_limit_bytes=56 * 1024 * 1024),
    )(*operands, *[jnp.asarray(c) for c in consts])

    shared = lax.all_to_all(info, ("height", "plane"), 0, 0, tiled=True)

    cell = sources % cells
    column = sources // cells
    wide_elem = column % plane
    deep_elem = column // plane
    owner = (deep_elem // elems) * plane + wide_elem
    place = (deep_elem % elems) * cells + cell
    return pl.pallas_call(
        combine_kernel,
        out_shape=(
            jax.ShapeDtypeStruct(cotangent.shape, F32),
            jax.ShapeDtypeStruct(cotangent.shape, F32),
            jax.ShapeDtypeStruct(sources.shape, F32),
        ),
        in_specs=[vmem] * 4,
        out_specs=(vmem, vmem, vmem),
        compiler_params=pltpu.CompilerParams(vmem_limit_bytes=32 * 1024 * 1024),
    )(shared, fields, owner, place)


def solution(mesh):
    counts = (mesh.shape["height"], mesh.shape["plane"])
    field = P("height", "plane", None)
    return jax.shard_map(
        functools.partial(per_device, counts),
        mesh=mesh,
        in_specs=(field, field, field, P()),
        out_specs=(field, field, P()),
        check_vma=False,
    )
```

```python
import functools

import jax
import jax.numpy as jnp
import ml_dtypes
import numpy as np
from jax import lax
from jax.experimental import pallas as pl
from jax.experimental.pallas import tpu as pltpu
from jax.sharding import PartitionSpec as P

INV_STEP = 20.0
SHIFTS = (0.5, 1.5)
GROUP = 4
REACH = 4
TERMS = ((0, 0), (0, 1), (1, 0), (1, 1), (2, 0))
PAIRS = ((0, 0), (0, 1), (0, 2), (1, 1), (1, 2), (2, 2))
TINY = 1e-30
HIGHEST = lax.Precision.HIGHEST
F32 = jnp.float32
BF16 = jnp.bfloat16


def gll_tables():
    points = np.array([-1.0, -0.8717401485096066, -0.5917001814331423, -0.2092992179024789, 0.2092992179024789, 0.5917001814331423, 0.8717401485096066, 1.0])
    weights = np.array([1.0 / 28.0, 0.2107042271435061, 0.3411226924835044, 0.4124587946587038, 0.4124587946587038, 0.3411226924835044, 0.2107042271435061, 1.0 / 28.0])
    product = np.array([np.prod([points[col] - points[others] for others in range(8) if others != col]) for col in range(8)])
    derivative = np.zeros((8, 8))
    for row in range(8):
        for col in range(8):
            if row != col:
                derivative[row, col] = product[row] / (product[col] * (points[row] - points[col]))
        derivative[row, row] = -np.sum(derivative[row])
    return derivative, weights, np.sum(derivative**2 * weights[:, None], axis=0)


def pieces(matrix):
    out, rest = [], matrix
    for _ in range(3):
        piece = rest.astype(ml_dtypes.bfloat16)
        out.append(piece)
        rest = rest - piece.astype(np.float64)
    return out


def tables(span):
    derivative, weights, stiff = gll_tables()
    line = (derivative.T * weights) @ derivative / weights[:, None]
    eye = np.eye(8)
    face = pieces(np.kron(line, eye) + np.kron(eye, line))
    face_mat = np.concatenate([face[m] for m, _ in TERMS], axis=1)
    ends_mat = np.concatenate([face_mat[0::8], face_mat[7::8]], axis=0)
    row = pieces(np.kron(np.eye(span // 8), line.T))
    row_a = np.concatenate([np.concatenate([row[0], row[1]], 1)] * 2, axis=0)
    none = np.zeros_like(row[2])
    row_b = np.concatenate([np.concatenate([row[2], none], 1), np.concatenate([none, row[2]], 1)], axis=0)
    tile = np.tile(weights, span // 8)
    ratio = stiff / weights
    omega = weights[:, None, None] * weights[None, :, None] * tile[None, None, :]
    quot = ratio[:, None, None] + ratio[None, :, None] + np.tile(ratio, span // 8)[None, None, :]
    return face_mat, ends_mat, row_a, row_b, omega.astype(np.float32), quot.astype(np.float32)


def swap(value, axis, pairs):
    if not pairs:
        return None
    return lax.ppermute(value, axis, [*pairs, *((b, a) for a, b in pairs)])


def coef_rows(elems):
    return -(-(2 * elems) // 8) * 8


def pack_kernel(cot_ref, kap_ref, cap_ref, out_ref, edge_ref):
    depth, _, span = cot_ref.shape
    elems, _, parts = kap_ref.shape
    out_ref[: depth * 8, :] = cot_ref[...].reshape(depth * 8, span)
    spread = (lax.broadcasted_iota(jnp.int32, (parts, span), 1) // 8 == lax.broadcasted_iota(jnp.int32, (parts, span), 0)).astype(F32)
    coef = jnp.concatenate([kap_ref[...].reshape(elems, parts) * (1.0 / INV_STEP), cap_ref[...].reshape(elems, parts)], axis=0)
    rows = coef_rows(elems)
    if rows > 2 * elems:
        coef = jnp.concatenate([coef, jnp.zeros((rows - 2 * elems, parts), F32)], axis=0)
    coef = jnp.dot(coef, spread, precision=HIGHEST, preferred_element_type=F32)
    out_ref[depth * 8 :, :] = coef
    last = lax.rem(lax.axis_index("plane"), GROUP) == GROUP - 1
    edge_ref[:depth, :] = jnp.where(last, cot_ref[:, 7, :], cot_ref[:, 0, :])
    edge_ref[depth:, :] = coef


class Layout:
    def __init__(self, tall):
        wide = 2 * REACH + 1
        self.wide = wide
        self.at_once = 1 if tall else 3
        self.sums = 0
        self.minv = max(wide, 5 * self.at_once)
        self.ratio = self.minv + wide
        self.basis = self.ratio + 5
        self.second = self.basis + 3 * wide
        self.total = self.second + wide * self.at_once


def basis_kernel(counts, present, *refs):
    height, plane = counts
    n_in = len(present) * height
    msgs = refs[:n_in]
    face_ref, ends_ref, row_a_ref, row_b_ref, omega_ref, quot_ref = refs[n_in : n_in + 6]
    fields_ref, info_ref = refs[n_in + 6 : n_in + 8]
    pool, raw, coef, weigh = refs[n_in + 8 :]
    rows, span = pool.shape[1:]
    depth = rows // 8
    own_depth = depth // height
    own_rows = own_depth * 8
    elems = depth // 8
    own_elems = elems // height
    height_pos = lax.axis_index("height")
    plane_pos = lax.axis_index("plane")
    member = lax.rem(plane_pos, GROUP)
    even = lax.rem(plane_pos // GROUP, 2) == 0
    slab_rows = own_rows + coef_rows(own_elems)
    whole = elems > 4
    lay = Layout(whole)
    wide = lay.wide

    lane = lax.broadcasted_iota(jnp.int32, (8, span), 1)
    sub = lax.broadcasted_iota(jnp.int32, (8, span), 0)
    opens = (lane % 8 == 0) & (lane > 0)
    closes = (lane % 8 == 7) & (lane < span - 1)

    def tall(mask, like):
        return jnp.concatenate([mask] * (like.shape[0] // 8), axis=0) if like.shape[0] > 8 else mask

    def join_span(values):
        up, down = pltpu.roll(values, 1, 1), pltpu.roll(values, span - 1, 1)
        return values + jnp.where(tall(opens, values), up, jnp.where(tall(closes, values), down, 0.0))

    def join_depth(values):
        planes = []
        layers = values.shape[0] // 64
        for elem in range(layers):
            top = elem * 64
            first, last = values[top : top + 8], values[top + 56 : top + 64]
            if elem > 0:
                first = first + values[top - 8 : top]
            if elem < layers - 1:
                last = last + values[top + 64 : top + 72]
            planes += [first, values[top + 8 : top + 56], last]
        return jnp.concatenate(planes, axis=0)

    def stage_coef(msg, top, slot, block):
        for kind in range(2):
            for elem in range(own_elems):
                at = top + kind * own_elems + elem
                coef[slot, kind, block * own_elems + elem] = jnp.broadcast_to(msg[at : at + 1, :], (8, span))

    def caps(msg, top):
        return [jnp.broadcast_to(msg[at : at + 1, :], (8, span)) for at in range(top + own_elems, top + 2 * own_elems)]

    def stage(msg, piece, slot, block):
        top = piece * slab_rows
        heavy = jnp.concatenate([c for c in caps(msg, top + own_rows) for _ in range(8)], axis=0)
        value = join_depth(join_span(heavy * msg[top : top + own_rows, :]))
        raw[slot, pl.ds(pl.multiple_of(block * own_rows, own_rows), own_rows)] = value
        stage_coef(msg, top + own_rows, slot, block)

    def stage_face(msg, slot, block):
        top = GROUP * slab_rows
        heavy = jnp.concatenate(caps(msg, top + own_depth), axis=0)
        face = join_span(heavy * msg[top : top + own_depth, :])
        value = join_depth(jnp.concatenate([jnp.broadcast_to(face[z : z + 1], (8, span)) for z in range(own_depth)], axis=0))
        raw[slot, pl.ds(pl.multiple_of(block * own_rows, own_rows), own_rows)] = value
        stage_coef(msg, top + own_depth, slot, block)

    def sides(name):
        after = even if name == "pair" else jnp.logical_not(even)
        return jnp.where(after, 1 + 2 * GROUP, 1), jnp.where(after, 3 * GROUP + 1, 0)

    for name in ("pair", "cross"):
        if name not in present:
            base, beyond = sides(name)
            for slot in [base + piece for piece in range(GROUP)] + [beyond]:
                raw[slot] = jnp.zeros((rows, span), F32)
                coef[slot] = jnp.zeros(coef.shape[1:], F32)
    for turn in range(height):
        block = lax.rem(height_pos - turn + height, height)
        for pos, name in enumerate(present):
            msg = msgs[turn * len(present) + pos]
            if name == "own":
                base = 1 + GROUP
            else:
                base, beyond = sides(name)
                stage_face(msg, beyond, block)
            for piece in range(GROUP):
                stage(msg, piece, base + jnp.bitwise_xor(member, piece), block)

    def face_at(slot, width_node):
        return slot, pl.ds(width_node, depth, stride=8)

    def join_width(store, slot):
        low, high = face_at(slot, 7), face_at(slot + 1, 0)
        both = store[low] + store[high]
        store[low] = both
        store[high] = both

    def loop(start, stop, body, step=1):
        if whole:
            lax.fori_loop(start, stop, lambda at, carry: (body([at]), carry)[1], 0)
        else:
            for at in range(start, stop, step):
                body(list(range(at, min(at + step, stop))))

    def each(body):
        return lambda slabs: [body(at) for at in slabs]

    def split(values):
        one = values.astype(BF16)
        return one, (values - one.astype(F32)).astype(BF16)

    def along_span(halves):
        wides = [jnp.dot(jnp.concatenate(h, axis=1), row_a_ref[...], preferred_element_type=F32) for h in halves]
        if len(halves) == 2:
            extra = jnp.dot(jnp.concatenate([halves[0][0], halves[1][0]], axis=1), row_b_ref[...], preferred_element_type=F32)
            extras = [extra[:, :span], extra[:, span:]]
        else:
            extras = [jnp.dot(halves[0][0], row_b_ref[:span, :span], preferred_element_type=F32)]
        return [(w[:, :span] + w[:, span:]) + x for w, x in zip(wides, extras)]

    def along_face(matrix, halves, elem):
        top = elem * 64
        stacks = [jnp.concatenate([h[f][top : top + 64] for _, f in TERMS], axis=0) for h in halves]
        return jnp.dot(matrix, stacks[0] if len(stacks) == 1 else jnp.concatenate(stacks, axis=1), preferred_element_type=F32)

    def scaled(slot, kind, elem, scale):
        value = coef[slot, kind, elem]
        return value if scale == 1.0 else value * scale

    def operator(fields, slots, scale=1.0, start=0):
        halves = [split(v) for v in fields]
        lines = along_span(halves)
        out = [[] for _ in fields]
        for elem in range(fields[0].shape[0] // 64):
            top = elem * 64
            face = along_face(face_ref[...], halves, elem)
            for i, v in enumerate(fields):
                cap = tall(scaled(slots[i], 1, start + elem, scale), face)
                kap = tall(scaled(slots[i], 0, start + elem, scale), face)
                lin = lines[i][top : top + 64] + face[:, i * span : (i + 1) * span]
                out[i].append(cap * v[top : top + 64] + kap * lin)
        return [jnp.concatenate(o, axis=0) for o in out]

    def ends(sources, targets, at, scale):
        halves = [split(pool[s]) for s in sources]
        edges = [pool[s, pl.ds(node, depth, stride=8)] for s, node in zip(sources, (7, 0))]
        lines = along_span([split(jnp.concatenate(edges, axis=0))])[0]
        both = [along_face(ends_ref[...], halves, elem) for elem in range(elems)]
        for i in range(2):
            joined = []
            for elem in range(elems):
                lin = lines[i * depth + elem * 8 : i * depth + elem * 8 + 8] + both[elem][8 * (1 - i) : 8 * (2 - i), i * span : (i + 1) * span]
                slot = member + at[i]
                joined.append(join_span(scaled(slot, 1, elem, scale) * edges[i][elem * 8 : elem * 8 + 8] + scaled(slot, 0, elem, scale) * lin))
            final = []
            for elem in range(elems):
                value = joined[elem]
                if elem > 0:
                    value = value + jnp.where(sub == 0, pltpu.roll(joined[elem - 1], 1, 0), 0.0)
                if elem < elems - 1:
                    value = value + jnp.where(sub == 7, pltpu.roll(joined[elem + 1], 7, 0), 0.0)
                final.append(value)
            pool[face_at(targets[i], (7, 0)[i])] = jnp.concatenate(final, axis=0)

    def step(chains, low, high, shift):
        def apply(work):
            made = operator([pool[here + at] for here, _, at in work], [member + at for _, _, at in work], 1.0 / shift)
            for (_, sums, at), value in zip(work, made):
                pool[sums + at] = join_depth(join_span(value))

        for here, sums, _ in chains:
            ends((here + low, here + high), (sums + low, sums + high), (low, high), 1.0 / shift)
        if whole:
            for here, sums, after in chains:
                loop(low + 1, high, each(lambda at: apply([(here, sums, at)])))
        else:
            work = [(here, sums, at) for here, sums, _ in chains for at in range(low + 1, high)]
            for first in range(0, len(work), 2):
                apply(work[first : first + 2])
        for here, sums, after in chains:
            loop(low, high, each(lambda at: join_width(pool, sums + at)))

            def advance(at):
                pool[after + at] = pool[lay.minv + at - 1] * pool[sums + at] - pool[here + at]

            loop(low + 1, high, each(advance))

    def constant(kind, at):
        layers = [[join_span(coef[member + at + side, kind, elem]) for elem in range(elems)] for side in (-1, 0, 1)]
        wide_sum = lambda low, mid, high: mid + jnp.where(sub == 0, low, jnp.where(sub == 7, high, 0.0))
        inside = [wide_sum(*(layers[side][elem] for side in range(3))) for elem in range(elems)]
        planes = []
        for elem in range(elems):
            first = inside[elem] if elem == 0 else inside[elem] + inside[elem - 1]
            last = inside[elem] if elem == elems - 1 else inside[elem] + inside[elem + 1]
            planes += [first] + [inside[elem]] * 6 + [last]
        return jnp.concatenate(planes, axis=0)

    def inverse_slab(at):
        quot = jnp.concatenate([quot_ref[...].reshape(64, span)] * elems, axis=0)
        mass = constant(1, at)
        inverse = 1.0 / jnp.maximum(mass + quot * constant(0, at), TINY)
        pool[lay.minv + at - 1] = inverse
        return inverse, mass

    def first_slab(at):
        inverse, _ = inverse_slab(at)
        pool[lay.basis + at - 1] = inverse * raw[member + at]

    def inner_slab(at):
        inverse, mass = inverse_slab(at)
        pool[lay.basis + at - 1] = inverse * raw[member + at]
        pool[lay.ratio + at - 3] = inverse * mass

    def join_blocks(slot):
        for block in range(1, height):
            low, high = pl.ds(block * own_rows - 8, 8), pl.ds(block * own_rows, 8)
            both = raw[slot, low] + raw[slot, high]
            raw[slot, low] = both
            raw[slot, high] = both

    loop(0, wide + 2, each(lambda at: join_blocks(member + at)))
    loop(0, wide + 1, each(lambda at: join_width(raw, member + at)))
    loop(1, 3, each(first_slab))
    loop(3, wide - 1, each(inner_slab))
    loop(wide - 1, wide + 1, each(first_slab))

    mid = REACH + 1

    def own(slot):
        value = pool[slot, :own_rows]
        for block in range(1, height):
            value = jnp.where(height_pos == block, pool[slot, block * own_rows : (block + 1) * own_rows], value)
        return value

    shape = (own_depth, 8, span)
    zpos = lax.broadcasted_iota(jnp.int32, shape, 0) + height_pos * own_depth
    xpos = lax.broadcasted_iota(jnp.int32, shape, 1) + plane_pos * 8

    def copies(pos, extent):
        return jnp.where(((pos % 8 == 7) & (pos < extent - 1)) | ((pos % 8 == 0) & (pos > 0)), 0.5, 1.0)

    share = copies(zpos, depth) * copies(xpos, plane * 8) * jnp.where(opens | closes, 0.5, 1.0)
    omega = jnp.concatenate([omega_ref[...].reshape(64, span)] * own_elems, axis=0)
    weigh[...] = share.reshape(own_rows, span) * omega / own(lay.minv + REACH)

    for level in range(2):
        step([(lay.basis + level * wide - 1, lay.sums - 1, lay.basis + (level + 1) * wide - 1)], 1 + level, wide - level, SHIFTS[level])
    for vec in range(3):
        fields_ref[vec] = own(lay.basis + vec * wide + REACH)

    def second(vecs):
        homes = [lay.second + wide * i for i in range(lay.at_once)]
        sums = [lay.sums + 5 * i - 3 for i in range(lay.at_once)]
        for vec, home in zip(vecs, homes):

            def begin(at):
                pool[home + at - 3] = pool[lay.ratio + at - 3] * pool[lay.basis + vec * wide + at - 1]

            loop(3, 8, each(begin))
        step([(h - 3, t, h + 1) for h, t in zip(homes, sums)], 3, 7, SHIFTS[0])
        step([(h + 1, t, h + 3) for h, t in zip(homes, sums)], 4, 6, SHIFTS[1])
        for vec, home in zip(vecs, homes):
            for level, slot in enumerate((2, 6, 8)):
                fields_ref[3 + 3 * level + vec] = own(home + slot)

    if lay.at_once == 3:
        second([0, 1, 2])
    else:
        loop(0, 3, each(lambda vec: second([vec])))

    slot = member + mid
    start = height_pos * own_elems

    def total(values):
        return jnp.sum(values.reshape(shape), axis=0)

    parts = []
    left = [weigh[...] * fields_ref[i] for i in range(3)]
    parts += [total(left[i] * fields_ref[j]) for i, j in PAIRS]
    lasts = (2, 9, 10, 11)
    energy = []
    for k in (0, 2):
        energy += operator([fields_ref[i] for i in lasts[k : k + 2]], [slot] * 2, 1.0, start)
    energy = [omega * e for e in energy]
    parts.append(total(fields_ref[2] * energy[0]))
    for k, l in PAIRS:
        pairs = PAIRS if k == l else [(i, j) for i in range(3) for j in range(3)]
        left = [weigh[...] * fields_ref[3 + 3 * k + i] for i in range(3)]
        parts += [total(left[i] * fields_ref[3 + 3 * l + j]) for i, j in pairs]
    parts += [total(fields_ref[9 + i] * energy[1 + j]) for i, j in PAIRS]
    lines = [jnp.sum(part, axis=0, keepdims=True) for part in parts]
    lines.append(jnp.zeros((span - len(lines), span), F32))
    sums = lax.dot_general(jnp.ones((8, span), F32), jnp.concatenate(lines, axis=0), (((1,), (1,)), ((), ())), precision=HIGHEST, preferred_element_type=F32)

    heavy = jnp.concatenate([tall(coef[slot, 1, start + elem], face_ref) for elem in range(own_elems)], axis=0) * (omega * 0.125)
    rows_of = []
    for index in range(12):
        mass = heavy * fields_ref[index]
        for elem in range(own_elems):
            rows_of.append(jnp.sum(mass[elem * 64 : elem * 64 + 64], axis=0, keepdims=True))
    stack = jnp.concatenate(rows_of, axis=0)
    cells = span // 8
    per_row = span // cells
    spread = (lax.broadcasted_iota(jnp.int32, (span, span), 0) // 8 == lax.broadcasted_iota(jnp.int32, (span, span), 1) % cells).astype(F32)
    stack = jnp.dot(stack, spread, precision=HIGHEST, preferred_element_type=F32)
    place = lax.broadcasted_iota(jnp.int32, stack.shape, 0) % per_row == lax.broadcasted_iota(jnp.int32, stack.shape, 1) // cells
    stack = jnp.where(place, stack, 0.0).reshape(stack.shape[0] // per_row, per_row, span)
    info = jnp.concatenate([jnp.sum(stack, axis=1), sums[:1]], axis=0)
    info_ref[...] = jnp.broadcast_to(info[None], info_ref.shape)


def galerkin(gram, energy):
    n00, n01, n02, n11, n12, n22 = gram
    first, later = SHIFTS
    h00, h01, h02 = first * (n01 + n00), first * (n11 + n01), first * (n12 + n02)
    h11, h12 = later * (n12 + n11), later * (n22 + n12)
    low10, low20 = h01 / h00, h02 / h00
    piv1 = h11 - low10 * h01
    off12 = h12 - low10 * h02
    low21 = off12 / piv1
    piv2 = energy - low20 * h02 - low21 * off12
    y0 = n00
    y1 = n01 - low10 * y0
    y2 = n02 - low20 * y0 - low21 * y1
    c2 = y2 / piv2
    c1 = y1 / piv1 - low21 * c2
    c0 = y0 / h00 - low10 * c1 - low20 * c2
    return c0, c1, c2


def combine_kernel(info_ref, fields_ref, owner_ref, place_ref, second_ref, first_ref, grad_ref):
    devices, lines, span = info_ref.shape
    ones = jnp.ones((devices, span), F32)
    contract = (((0,), (0,)), ((), ()))
    wide = lax.dot_general(info_ref[:, lines - 1, :], ones, contract, precision=HIGHEST, preferred_element_type=F32)
    take = [wide[i : i + 1, :] for i in range(7 + 45 + 6)]
    coef = galerkin(take[:6], take[6])
    at = 7
    double = [(2.0 if i != j else 1.0) * coef[i] * coef[j] for i, j in PAIRS]
    every = [coef[i] * coef[j] for i in range(3) for j in range(3)]
    gram = []
    for k, l in PAIRS:
        factors = double if k == l else every
        gram.append(sum(f * t for f, t in zip(factors, take[at : at + len(factors)])))
        at += len(factors)
    energy = sum(f * t for f, t in zip(double, take[at : at + 6]))
    outer = galerkin(gram, energy)
    factors = list(coef) + [d * c for d in outer for c in coef]

    second = factors[0] * fields_ref[0] + factors[1] * fields_ref[1] + factors[2] * fields_ref[2]
    second_ref[...] = second.reshape(second_ref.shape)
    first = factors[3] * fields_ref[3]
    for i in range(4, 12):
        first = first + factors[i] * fields_ref[i]
    first_ref[...] = first.reshape(first_ref.shape)

    per_line = 12 // (lines - 1)
    cells = span // per_line
    row = lax.broadcasted_iota(jnp.int32, (span, span), 0)
    for step in range(2):
        holder = (owner_ref[step : step + 1, :] == lax.broadcasted_iota(jnp.int32, (devices, span), 0)).astype(F32)
        here = place_ref[step : step + 1, :] == row % cells
        result = jnp.zeros((1, span), F32)
        for line in range(lines - 1):
            fields = [f for f in range(line * per_line, (line + 1) * per_line) if (f >= 3) == (step == 0)]
            if not fields:
                continue
            picked = lax.dot_general(info_ref[:, line, :], holder, contract, precision=HIGHEST, preferred_element_type=F32)
            picked = jnp.where(here, picked, 0.0)
            for f in fields:
                lo = (f - line * per_line) * cells
                result = result + factors[f] * jnp.sum(picked[lo : lo + cells], axis=0, keepdims=True)
        grad_ref[step : step + 1, :] = result


def per_device(counts, cotangent, conductivity, capacity, sources):
    height, plane = counts
    depth, _, span = cotangent.shape
    elems = depth // 8
    cells = span // 8
    groups = plane // GROUP
    devices = height * plane
    vmem = pl.BlockSpec(memory_space=pltpu.VMEM)

    rows = depth * 8 + coef_rows(elems)
    message, edge = pl.pallas_call(
        pack_kernel,
        out_shape=(jax.ShapeDtypeStruct((rows, span), F32), jax.ShapeDtypeStruct((depth + coef_rows(elems), span), F32)),
        in_specs=[vmem] * 3,
        out_specs=(vmem, vmem),
        compiler_params=pltpu.CompilerParams(vmem_limit_bytes=4 * 2**20),
    )(cotangent, conductivity, capacity)

    beyond = swap(edge, "plane", [(g * GROUP + GROUP - 1, (g + 1) * GROUP) for g in range(groups - 1)])
    gathered = message
    width = 1
    while width < GROUP:
        other = swap(gathered, "plane", [(p, p ^ width) for p in range(plane) if p & width == 0])
        gathered = jnp.concatenate([gathered, other], axis=0)
        width *= 2
    gathered = jnp.concatenate([gathered, edge if beyond is None else beyond], axis=0)

    def group_pairs(turn):
        return [(g * GROUP + m, (g + 1) * GROUP + m) for g in range(turn, groups - 1, 2) for m in range(GROUP)]

    sent = {"own": gathered, "pair": swap(gathered, "plane", group_pairs(0)), "cross": swap(gathered, "plane", group_pairs(1))}
    present = tuple(name for name, arr in sent.items() if arr is not None)
    operands = [sent[name] for name in present]
    for turn in range(1, height):
        operands += [lax.ppermute(sent[name], "height", [(h, (h + turn) % height) for h in range(height)]) for name in present]

    lay = Layout(elems * height > 4)
    consts = tables(span)
    slots = 3 * GROUP + 2
    slab_bytes = 4 * depth * 8 * height * span
    fields, info = pl.pallas_call(
        functools.partial(basis_kernel, counts, present),
        out_shape=(jax.ShapeDtypeStruct((12, depth * 8, span), F32), jax.ShapeDtypeStruct((devices, 12 * elems * cells // span + 1, span), F32)),
        in_specs=[vmem] * (len(operands) + len(consts)),
        out_specs=(vmem, vmem),
        scratch_shapes=[
            pltpu.VMEM((lay.total, depth * 8 * height, span), F32),
            pltpu.VMEM((slots, depth * 8 * height, span), F32),
            pltpu.VMEM((slots, 2, elems * height, 8, span), F32),
            pltpu.VMEM((depth * 8, span), F32),
        ],
        compiler_params=pltpu.CompilerParams(vmem_limit_bytes=(lay.total + 3 * slots + 14) * slab_bytes + 12 * 2**20),
    )(*operands, *[jnp.asarray(c) for c in consts])

    shared = lax.all_to_all(info, ("height", "plane"), 0, 0, tiled=True)

    cell = sources % cells
    column = sources // cells
    wide_elem = column % plane
    deep_elem = column // plane
    owner = (deep_elem // elems) * plane + wide_elem
    place = (deep_elem % elems) * cells + cell
    return pl.pallas_call(
        combine_kernel,
        out_shape=(
            jax.ShapeDtypeStruct(cotangent.shape, F32),
            jax.ShapeDtypeStruct(cotangent.shape, F32),
            jax.ShapeDtypeStruct(sources.shape, F32),
        ),
        in_specs=[vmem] * 4,
        out_specs=(vmem, vmem, vmem),
        compiler_params=pltpu.CompilerParams(vmem_limit_bytes=8 * 2**20),
    )(shared, fields, owner, place)


def solution(mesh):
    counts = (mesh.shape["height"], mesh.shape["plane"])
    field = P("height", "plane", None)
    return jax.shard_map(
        functools.partial(per_device, counts),
        mesh=mesh,
        in_specs=(field, field, field, P()),
        out_specs=(field, field, P()),
        check_vma=False,
    )
```

```python
import functools

import jax
import jax.numpy as jnp
import ml_dtypes
import numpy as np
from jax import lax
from jax.experimental import pallas as pl
from jax.experimental.pallas import tpu as pltpu
from jax.sharding import PartitionSpec as P

INV_STEP = 20.0
SHIFTS = (0.5, 1.5)
GROUP = 4
REACH = 4
PAIRS = ((0, 0), (0, 1), (0, 2), (1, 1), (1, 2), (2, 2))
TINY = 1e-30
HIGHEST = lax.Precision.HIGHEST
F32 = jnp.float32
BF16 = jnp.bfloat16


def gll_tables():
    points = np.array([-1.0, -0.8717401485096066, -0.5917001814331423, -0.2092992179024789, 0.2092992179024789, 0.5917001814331423, 0.8717401485096066, 1.0])
    weights = np.array([1.0 / 28.0, 0.2107042271435061, 0.3411226924835044, 0.4124587946587038, 0.4124587946587038, 0.3411226924835044, 0.2107042271435061, 1.0 / 28.0])
    product = np.array([np.prod([points[col] - points[others] for others in range(8) if others != col]) for col in range(8)])
    derivative = np.zeros((8, 8))
    for row in range(8):
        for col in range(8):
            if row != col:
                derivative[row, col] = product[row] / (product[col] * (points[row] - points[col]))
        derivative[row, row] = -np.sum(derivative[row])
    return derivative, weights, np.sum(derivative**2 * weights[:, None], axis=0)


def pieces(matrix):
    out, rest = [], matrix
    for _ in range(3):
        piece = rest.astype(ml_dtypes.bfloat16)
        out.append(piece)
        rest = rest - piece.astype(np.float64)
    return out


def tables(span):
    derivative, weights, stiff = gll_tables()
    line = (derivative.T * weights) @ derivative / weights[:, None]
    eye = np.eye(8)
    face = pieces(np.kron(line, eye) + np.kron(eye, line))
    face_mat = np.concatenate([np.concatenate([piece, piece], axis=1) for piece in face], axis=0)
    ends_mat = np.concatenate([np.concatenate([p[0::8], p[7::8]], axis=0) for p in np.split(face_mat, 3)], axis=0)
    row = pieces(np.kron(np.eye(span // 8), line.T))
    row_a = np.concatenate([np.concatenate([row[0], row[1]], 1)] * 2, axis=0)
    none = np.zeros_like(row[2])
    row_b = np.concatenate([np.concatenate([row[2], none], 1), np.concatenate([none, row[2]], 1)], axis=0)
    tile = np.tile(weights, span // 8)
    ratio = stiff / weights
    omega = weights[:, None, None] * weights[None, :, None] * tile[None, None, :]
    quot = ratio[:, None, None] + ratio[None, :, None] + np.tile(ratio, span // 8)[None, None, :]
    return face_mat, ends_mat, row_a, row_b, omega.astype(np.float32), quot.astype(np.float32)


def swap(value, axis, pairs):
    if not pairs:
        return None
    return lax.ppermute(value, axis, [*pairs, *((b, a) for a, b in pairs)])


def coef_rows(elems):
    return -(-(2 * elems) // 8) * 8


def seams(span):
    lane = lax.broadcasted_iota(jnp.int32, (8, span), 1)
    return (lane % 8 == 0) & (lane > 0), (lane % 8 == 7) & (lane < span - 1)


def tall(mask, like):
    return jnp.concatenate([mask] * (like.shape[0] // 8), axis=0) if like.shape[0] > 8 else mask


def join_span(values):
    span = values.shape[1]
    opens, closes = seams(span)
    up, down = pltpu.roll(values, 1, 1), pltpu.roll(values, span - 1, 1)
    return values + jnp.where(tall(opens, values), up, jnp.where(tall(closes, values), down, 0.0))


def join_depth(values):
    planes = []
    layers = values.shape[0] // 64
    for elem in range(layers):
        top = elem * 64
        first, last = values[top : top + 8], values[top + 56 : top + 64]
        if elem > 0:
            first = first + values[top - 8 : top]
        if elem < layers - 1:
            last = last + values[top + 64 : top + 72]
        planes += [first, values[top + 8 : top + 56], last]
    return jnp.concatenate(planes, axis=0)


def pack_kernel(cot_hbm, kap_hbm, cap_hbm, out_ref, edge_ref, cot_ref, kap_ref, cap_ref, sems):
    loads = [
        pltpu.make_async_copy(src, dst, sems.at[i])
        for i, (src, dst) in enumerate(((cot_hbm, cot_ref), (kap_hbm, kap_ref), (cap_hbm, cap_ref)))
    ]
    for load in loads:
        load.start()
    for load in loads:
        load.wait()
    depth, _, span = cot_ref.shape
    elems, _, parts = kap_ref.shape
    spread = (lax.broadcasted_iota(jnp.int32, (parts, span), 1) // 8 == lax.broadcasted_iota(jnp.int32, (parts, span), 0)).astype(F32)
    coef = jnp.concatenate([kap_ref[...].reshape(elems, parts) * (1.0 / INV_STEP), cap_ref[...].reshape(elems, parts)], axis=0)
    rows = coef_rows(elems)
    if rows > 2 * elems:
        coef = jnp.concatenate([coef, jnp.zeros((rows - 2 * elems, parts), F32)], axis=0)
    coef = jnp.dot(coef, spread, precision=HIGHEST, preferred_element_type=F32)
    heavy = jnp.concatenate([jnp.broadcast_to(coef[elems + e : elems + e + 1], (64, span)) for e in range(elems)], axis=0)
    value = join_depth(join_span(heavy * cot_ref[...].reshape(depth * 8, span)))
    out_ref[: depth * 8, :] = value
    out_ref[depth * 8 :, :] = coef
    last = lax.rem(lax.axis_index("plane"), GROUP) == GROUP - 1
    faces = [value.reshape(depth, 8, span)[:, node, :] for node in (0, 7)]
    edge_ref[:depth, :] = jnp.where(last, faces[1], faces[0])
    edge_ref[depth:, :] = coef


class Layout:
    def __init__(self, tall):
        wide = 2 * REACH + 1
        self.wide = wide
        self.at_once = 1 if tall else 3
        self.sums = 0
        self.minv = max(wide, 5 * self.at_once)
        self.ratio = self.minv + wide
        self.basis = self.ratio + 5
        self.second = self.basis + 3 * wide
        self.total = self.second + wide * self.at_once


def basis_kernel(counts, present, *refs):
    height, plane = counts
    n_in = len(present) * height
    msgs = refs[:n_in]
    face_ref, ends_ref, row_a_ref, row_b_ref, omega_ref, quot_ref = refs[n_in : n_in + 6]
    fields_ref, info_ref = refs[n_in + 6 : n_in + 8]
    pool, raw, coef, weigh = refs[n_in + 8 :]
    rows, span = pool.shape[1:]
    depth = rows // 8
    own_depth = depth // height
    own_rows = own_depth * 8
    elems = depth // 8
    own_elems = elems // height
    height_pos = lax.axis_index("height")
    plane_pos = lax.axis_index("plane")
    member = lax.rem(plane_pos, GROUP)
    even = lax.rem(plane_pos // GROUP, 2) == 0
    slab_rows = own_rows + coef_rows(own_elems)
    whole = elems > 4
    lay = Layout(whole)
    wide = lay.wide

    sub = lax.broadcasted_iota(jnp.int32, (8, span), 0)
    opens, closes = seams(span)

    def stage_coef(msg, top, slot, block):
        for kind in range(2):
            for elem in range(own_elems):
                at = top + kind * own_elems + elem
                coef[slot, kind, block * own_elems + elem] = jnp.broadcast_to(msg[at : at + 1, :], (8, span))

    def stage(msg, piece, slot, block):
        top = piece * slab_rows
        raw[slot, pl.ds(pl.multiple_of(block * own_rows, own_rows), own_rows)] = msg[top : top + own_rows, :]
        stage_coef(msg, top + own_rows, slot, block)

    def stage_face(msg, slot, block):
        top = GROUP * slab_rows
        face = msg[top : top + own_depth, :]
        spread = jnp.concatenate([jnp.broadcast_to(face[z : z + 1], (8, span)) for z in range(own_depth)], axis=0)
        raw[slot, pl.ds(pl.multiple_of(block * own_rows, own_rows), own_rows)] = spread
        stage_coef(msg, top + own_depth, slot, block)

    def sides(name):
        after = even if name == "pair" else jnp.logical_not(even)
        return jnp.where(after, 1 + 2 * GROUP, 1), jnp.where(after, 3 * GROUP + 1, 0)

    for name in ("pair", "cross"):
        if name not in present:
            base, beyond = sides(name)
            for slot in [base + piece for piece in range(GROUP)] + [beyond]:
                raw[slot] = jnp.zeros((rows, span), F32)
                coef[slot] = jnp.zeros(coef.shape[1:], F32)
    for turn in range(height):
        block = lax.rem(height_pos - turn + height, height)
        for pos, name in enumerate(present):
            msg = msgs[turn * len(present) + pos]
            if name == "own":
                base = 1 + GROUP
            else:
                base, beyond = sides(name)
                stage_face(msg, beyond, block)
            for piece in range(GROUP):
                stage(msg, piece, base + jnp.bitwise_xor(member, piece), block)

    def face_at(slot, width_node):
        return slot, pl.ds(width_node, depth, stride=8)

    def join_width(store, slot):
        low, high = face_at(slot, 7), face_at(slot + 1, 0)
        both = store[low] + store[high]
        store[low] = both
        store[high] = both

    def loop(start, stop, body, step=1):
        if whole:
            lax.fori_loop(start, stop, lambda at, carry: (body([at]), carry)[1], 0)
        else:
            for at in range(start, stop, step):
                body(list(range(at, min(at + step, stop))))

    def each(body):
        return lambda slabs: [body(at) for at in slabs]

    def split(values):
        one = values.astype(BF16)
        return one, (values - one.astype(F32)).astype(BF16)

    def along_span(halves):
        wides = [jnp.dot(jnp.concatenate(h, axis=1), row_a_ref[...], preferred_element_type=F32) for h in halves]
        if len(halves) == 2:
            extra = jnp.dot(jnp.concatenate([halves[0][0], halves[1][0]], axis=1), row_b_ref[...], preferred_element_type=F32)
            extras = [extra[:, :span], extra[:, span:]]
        else:
            extras = [jnp.dot(halves[0][0], row_b_ref[:span, :span], preferred_element_type=F32)]
        return [(w[:, :span] + w[:, span:]) + x for w, x in zip(wides, extras)]

    def along_face(matrix, halves, elem):
        top = elem * 64
        stacks = [jnp.concatenate([piece[top : top + 64] for piece in h], axis=0) for h in halves]
        made = jnp.dot(matrix, stacks[0] if len(stacks) == 1 else jnp.concatenate(stacks, axis=1), preferred_element_type=F32)
        count = made.shape[0] // 3
        return made[:count] + (made[count : 2 * count] + made[2 * count :])

    def scaled(slot, kind, elem, scale):
        value = coef[slot, kind, elem]
        return value if scale == 1.0 else value * scale

    def operator(fields, slots, scale=1.0, start=0):
        halves = [split(v) for v in fields]
        lines = along_span(halves)
        out = [[] for _ in fields]
        for elem in range(fields[0].shape[0] // 64):
            top = elem * 64
            face = along_face(face_ref[...], halves, elem)
            for i, v in enumerate(fields):
                cap = tall(scaled(slots[i], 1, start + elem, scale), face)
                kap = tall(scaled(slots[i], 0, start + elem, scale), face)
                lin = lines[i][top : top + 64] + face[:, i * span : (i + 1) * span]
                out[i].append(cap * v[top : top + 64] + kap * lin)
        return [jnp.concatenate(o, axis=0) for o in out]

    def ends(sources, targets, at, scale):
        halves = [split(pool[s]) for s in sources]
        edges = [pool[s, pl.ds(node, depth, stride=8)] for s, node in zip(sources, (7, 0))]
        lines = along_span([split(jnp.concatenate(edges, axis=0))])[0]
        both = [along_face(ends_ref[...], halves, elem) for elem in range(elems)]
        for i in range(2):
            joined = []
            for elem in range(elems):
                lin = lines[i * depth + elem * 8 : i * depth + elem * 8 + 8] + both[elem][8 * (1 - i) : 8 * (2 - i), i * span : (i + 1) * span]
                slot = member + at[i]
                joined.append(join_span(scaled(slot, 1, elem, scale) * edges[i][elem * 8 : elem * 8 + 8] + scaled(slot, 0, elem, scale) * lin))
            final = []
            for elem in range(elems):
                value = joined[elem]
                if elem > 0:
                    value = value + jnp.where(sub == 0, pltpu.roll(joined[elem - 1], 1, 0), 0.0)
                if elem < elems - 1:
                    value = value + jnp.where(sub == 7, pltpu.roll(joined[elem + 1], 7, 0), 0.0)
                final.append(value)
            pool[face_at(targets[i], (7, 0)[i])] = jnp.concatenate(final, axis=0)

    def step(chains, low, high, shift):
        def apply(work):
            made = operator([pool[here + at] for here, _, at in work], [member + at for _, _, at in work], 1.0 / shift)
            for (_, sums, at), value in zip(work, made):
                pool[sums + at] = join_depth(join_span(value))

        for here, sums, _ in chains:
            ends((here + low, here + high), (sums + low, sums + high), (low, high), 1.0 / shift)
        if whole:
            for here, sums, after in chains:
                loop(low + 1, high, each(lambda at: apply([(here, sums, at)])))
        else:
            work = [(here, sums, at) for here, sums, _ in chains for at in range(low + 1, high)]
            for first in range(0, len(work), 2):
                apply(work[first : first + 2])
        for here, sums, after in chains:
            loop(low, high, each(lambda at: join_width(pool, sums + at)))

            def advance(at):
                pool[after + at] = pool[lay.minv + at - 1] * pool[sums + at] - pool[here + at]

            loop(low + 1, high, each(advance))

    def constant(kind, at):
        layers = [[join_span(coef[member + at + side, kind, elem]) for elem in range(elems)] for side in (-1, 0, 1)]
        wide_sum = lambda low, mid, high: mid + jnp.where(sub == 0, low, jnp.where(sub == 7, high, 0.0))
        inside = [wide_sum(*(layers[side][elem] for side in range(3))) for elem in range(elems)]
        planes = []
        for elem in range(elems):
            first = inside[elem] if elem == 0 else inside[elem] + inside[elem - 1]
            last = inside[elem] if elem == elems - 1 else inside[elem] + inside[elem + 1]
            planes += [first] + [inside[elem]] * 6 + [last]
        return jnp.concatenate(planes, axis=0)

    def inverse_slab(at):
        quot = jnp.concatenate([quot_ref[...].reshape(64, span)] * elems, axis=0)
        mass = constant(1, at)
        inverse = 1.0 / jnp.maximum(mass + quot * constant(0, at), TINY)
        pool[lay.minv + at - 1] = inverse
        return inverse, mass

    def first_slab(at):
        inverse, _ = inverse_slab(at)
        pool[lay.basis + at - 1] = inverse * raw[member + at]

    def inner_slab(at):
        inverse, mass = inverse_slab(at)
        pool[lay.basis + at - 1] = inverse * raw[member + at]
        pool[lay.ratio + at - 3] = inverse * mass

    def join_blocks(slot):
        for block in range(1, height):
            low, high = pl.ds(block * own_rows - 8, 8), pl.ds(block * own_rows, 8)
            both = raw[slot, low] + raw[slot, high]
            raw[slot, low] = both
            raw[slot, high] = both

    loop(0, wide + 2, each(lambda at: join_blocks(member + at)))
    loop(0, wide + 1, each(lambda at: join_width(raw, member + at)))
    loop(1, 3, each(first_slab))
    loop(3, wide - 1, each(inner_slab))
    loop(wide - 1, wide + 1, each(first_slab))

    mid = REACH + 1

    def own(slot):
        value = pool[slot, :own_rows]
        for block in range(1, height):
            value = jnp.where(height_pos == block, pool[slot, block * own_rows : (block + 1) * own_rows], value)
        return value

    shape = (own_depth, 8, span)
    zpos = lax.broadcasted_iota(jnp.int32, shape, 0) + height_pos * own_depth
    xpos = lax.broadcasted_iota(jnp.int32, shape, 1) + plane_pos * 8

    def copies(pos, extent):
        return jnp.where(((pos % 8 == 7) & (pos < extent - 1)) | ((pos % 8 == 0) & (pos > 0)), 0.5, 1.0)

    share = copies(zpos, depth) * copies(xpos, plane * 8) * jnp.where(opens | closes, 0.5, 1.0)
    omega = jnp.concatenate([omega_ref[...].reshape(64, span)] * own_elems, axis=0)
    weigh[...] = share.reshape(own_rows, span) * omega / own(lay.minv + REACH)

    for level in range(2):
        step([(lay.basis + level * wide - 1, lay.sums - 1, lay.basis + (level + 1) * wide - 1)], 1 + level, wide - level, SHIFTS[level])
    for vec in range(3):
        fields_ref[vec] = own(lay.basis + vec * wide + REACH)

    def second(vecs):
        homes = [lay.second + wide * i for i in range(lay.at_once)]
        sums = [lay.sums + 5 * i - 3 for i in range(lay.at_once)]
        for vec, home in zip(vecs, homes):

            def begin(at):
                pool[home + at - 3] = pool[lay.ratio + at - 3] * pool[lay.basis + vec * wide + at - 1]

            loop(3, 8, each(begin))
        step([(h - 3, t, h + 1) for h, t in zip(homes, sums)], 3, 7, SHIFTS[0])
        step([(h + 1, t, h + 3) for h, t in zip(homes, sums)], 4, 6, SHIFTS[1])
        for vec, home in zip(vecs, homes):
            for level, slot in enumerate((2, 6, 8)):
                fields_ref[3 + 3 * level + vec] = own(home + slot)

    if lay.at_once == 3:
        second([0, 1, 2])
    else:
        loop(0, 3, each(lambda vec: second([vec])))

    slot = member + mid
    start = height_pos * own_elems

    def total(values):
        return jnp.sum(values.reshape(shape), axis=0)

    parts = []
    left = [weigh[...] * fields_ref[i] for i in range(3)]
    parts += [total(left[i] * fields_ref[j]) for i, j in PAIRS]
    lasts = (2, 9, 10, 11)
    energy = []
    for k in (0, 2):
        energy += operator([fields_ref[i] for i in lasts[k : k + 2]], [slot] * 2, 1.0, start)
    energy = [omega * e for e in energy]
    parts.append(total(fields_ref[2] * energy[0]))
    for k, l in PAIRS:
        pairs = PAIRS if k == l else [(i, j) for i in range(3) for j in range(3)]
        left = [weigh[...] * fields_ref[3 + 3 * k + i] for i in range(3)]
        parts += [total(left[i] * fields_ref[3 + 3 * l + j]) for i, j in pairs]
    parts += [total(fields_ref[9 + i] * energy[1 + j]) for i, j in PAIRS]
    lines = [jnp.sum(part, axis=0, keepdims=True) for part in parts]
    lines.append(jnp.zeros((span - len(lines), span), F32))
    sums = lax.dot_general(jnp.ones((8, span), F32), jnp.concatenate(lines, axis=0), (((1,), (1,)), ((), ())), precision=HIGHEST, preferred_element_type=F32)

    heavy = jnp.concatenate([jnp.concatenate([coef[slot, 1, start + elem]] * 8, axis=0) for elem in range(own_elems)], axis=0) * (omega * 0.125)
    rows_of = []
    for index in range(12):
        mass = heavy * fields_ref[index]
        for elem in range(own_elems):
            rows_of.append(jnp.sum(mass[elem * 64 : elem * 64 + 64], axis=0, keepdims=True))
    stack = jnp.concatenate(rows_of, axis=0)
    cells = span // 8
    per_row = span // cells
    spread = (lax.broadcasted_iota(jnp.int32, (span, span), 0) // 8 == lax.broadcasted_iota(jnp.int32, (span, span), 1) % cells).astype(F32)
    stack = jnp.dot(stack, spread, precision=HIGHEST, preferred_element_type=F32)
    place = lax.broadcasted_iota(jnp.int32, stack.shape, 0) % per_row == lax.broadcasted_iota(jnp.int32, stack.shape, 1) // cells
    stack = jnp.where(place, stack, 0.0).reshape(stack.shape[0] // per_row, per_row, span)
    info = jnp.concatenate([jnp.sum(stack, axis=1), sums[:1]], axis=0)
    info_ref[...] = jnp.broadcast_to(info[None], info_ref.shape)


def galerkin(gram, energy):
    n00, n01, n02, n11, n12, n22 = gram
    first, later = SHIFTS
    h00, h01, h02 = first * (n01 + n00), first * (n11 + n01), first * (n12 + n02)
    h11, h12 = later * (n12 + n11), later * (n22 + n12)
    low10, low20 = h01 / h00, h02 / h00
    piv1 = h11 - low10 * h01
    off12 = h12 - low10 * h02
    low21 = off12 / piv1
    piv2 = energy - low20 * h02 - low21 * off12
    y0 = n00
    y1 = n01 - low10 * y0
    y2 = n02 - low20 * y0 - low21 * y1
    c2 = y2 / piv2
    c1 = y1 / piv1 - low21 * c2
    c0 = y0 / h00 - low10 * c1 - low20 * c2
    return c0, c1, c2


def combine_kernel(info_ref, fields_ref, owner_ref, place_ref, second_ref, first_ref, grad_ref):
    devices, lines, span = info_ref.shape
    ones = jnp.ones((devices, span), F32)
    contract = (((0,), (0,)), ((), ()))
    wide = lax.dot_general(info_ref[:, lines - 1, :], ones, contract, precision=HIGHEST, preferred_element_type=F32)
    take = [wide[i : i + 1, :] for i in range(7 + 45 + 6)]
    coef = galerkin(take[:6], take[6])
    at = 7
    double = [(2.0 if i != j else 1.0) * coef[i] * coef[j] for i, j in PAIRS]
    every = [coef[i] * coef[j] for i in range(3) for j in range(3)]
    gram = []
    for k, l in PAIRS:
        factors = double if k == l else every
        gram.append(sum(f * t for f, t in zip(factors, take[at : at + len(factors)])))
        at += len(factors)
    energy = sum(f * t for f, t in zip(double, take[at : at + 6]))
    outer = galerkin(gram, energy)
    factors = list(coef) + [d * c for d in outer for c in coef]

    second = factors[0] * fields_ref[0] + factors[1] * fields_ref[1] + factors[2] * fields_ref[2]
    second_ref[...] = second.reshape(second_ref.shape)
    first = factors[3] * fields_ref[3]
    for i in range(4, 12):
        first = first + factors[i] * fields_ref[i]
    first_ref[...] = first.reshape(first_ref.shape)

    per_line = 12 // (lines - 1)
    cells = span // per_line
    row = lax.broadcasted_iota(jnp.int32, (span, span), 0)
    for step in range(2):
        holder = (owner_ref[step : step + 1, :] == lax.broadcasted_iota(jnp.int32, (devices, span), 0)).astype(F32)
        here = place_ref[step : step + 1, :] == row % cells
        result = jnp.zeros((1, span), F32)
        for line in range(lines - 1):
            fields = [f for f in range(line * per_line, (line + 1) * per_line) if (f >= 3) == (step == 0)]
            if not fields:
                continue
            picked = lax.dot_general(info_ref[:, line, :], holder, contract, precision=HIGHEST, preferred_element_type=F32)
            picked = jnp.where(here, picked, 0.0)
            for f in fields:
                lo = (f - line * per_line) * cells
                result = result + factors[f] * jnp.sum(picked[lo : lo + cells], axis=0, keepdims=True)
        grad_ref[step : step + 1, :] = result


def per_device(counts, cotangent, conductivity, capacity, sources):
    height, plane = counts
    depth, _, span = cotangent.shape
    elems = depth // 8
    cells = span // 8
    groups = plane // GROUP
    devices = height * plane
    vmem = pl.BlockSpec(memory_space=pltpu.VMEM)

    rows = depth * 8 + coef_rows(elems)
    message, edge = pl.pallas_call(
        pack_kernel,
        out_shape=(jax.ShapeDtypeStruct((rows, span), F32), jax.ShapeDtypeStruct((depth + coef_rows(elems), span), F32)),
        in_specs=[pl.BlockSpec(memory_space=pl.ANY)] * 3,
        out_specs=(vmem, vmem),
        scratch_shapes=[pltpu.VMEM(arr.shape, F32) for arr in (cotangent, conductivity, capacity)] + [pltpu.SemaphoreType.DMA((3,))],
        compiler_params=pltpu.CompilerParams(vmem_limit_bytes=4 * 2**20),
    )(cotangent, conductivity, capacity)

    beyond = swap(edge, "plane", [(g * GROUP + GROUP - 1, (g + 1) * GROUP) for g in range(groups - 1)])
    gathered = message
    width = 1
    while width < GROUP:
        other = swap(gathered, "plane", [(p, p ^ width) for p in range(plane) if p & width == 0])
        gathered = jnp.concatenate([gathered, other], axis=0)
        width *= 2
    gathered = jnp.concatenate([gathered, edge if beyond is None else beyond], axis=0)

    def group_pairs(turn):
        return [(g * GROUP + m, (g + 1) * GROUP + m) for g in range(turn, groups - 1, 2) for m in range(GROUP)]

    sent = {"own": gathered, "pair": swap(gathered, "plane", group_pairs(0)), "cross": swap(gathered, "plane", group_pairs(1))}
    present = tuple(name for name, arr in sent.items() if arr is not None)
    operands = [sent[name] for name in present]
    for turn in range(1, height):
        operands += [lax.ppermute(sent[name], "height", [(h, (h + turn) % height) for h in range(height)]) for name in present]

    lay = Layout(elems * height > 4)
    consts = tables(span)
    slots = 3 * GROUP + 2
    slab_bytes = 4 * depth * 8 * height * span
    fields, info = pl.pallas_call(
        functools.partial(basis_kernel, counts, present),
        out_shape=(jax.ShapeDtypeStruct((12, depth * 8, span), F32), jax.ShapeDtypeStruct((devices, 12 * elems * cells // span + 1, span), F32)),
        in_specs=[vmem] * (len(operands) + len(consts)),
        out_specs=(vmem, vmem),
        scratch_shapes=[
            pltpu.VMEM((lay.total, depth * 8 * height, span), F32),
            pltpu.VMEM((slots, depth * 8 * height, span), F32),
            pltpu.VMEM((slots, 2, elems * height, 8, span), F32),
            pltpu.VMEM((depth * 8, span), F32),
        ],
        compiler_params=pltpu.CompilerParams(vmem_limit_bytes=(lay.total + 3 * slots + 14) * slab_bytes + 12 * 2**20),
    )(*operands, *[jnp.asarray(c) for c in consts])

    shared = lax.all_to_all(info, ("height", "plane"), 0, 0, tiled=True)

    cell = sources % cells
    column = sources // cells
    wide_elem = column % plane
    deep_elem = column // plane
    owner = (deep_elem // elems) * plane + wide_elem
    place = (deep_elem % elems) * cells + cell
    return pl.pallas_call(
        combine_kernel,
        out_shape=(
            jax.ShapeDtypeStruct(cotangent.shape, F32),
            jax.ShapeDtypeStruct(cotangent.shape, F32),
            jax.ShapeDtypeStruct(sources.shape, F32),
        ),
        in_specs=[vmem] * 4,
        out_specs=(vmem, vmem, vmem),
        compiler_params=pltpu.CompilerParams(vmem_limit_bytes=8 * 2**20),
    )(shared, fields, owner, place)


def solution(mesh):
    counts = (mesh.shape["height"], mesh.shape["plane"])
    field = P("height", "plane", None)
    return jax.shard_map(
        functools.partial(per_device, counts),
        mesh=mesh,
        in_specs=(field, field, field, P()),
        out_specs=(field, field, P()),
        check_vma=False,
    )
```

```python
import functools

import jax
import jax.numpy as jnp
import ml_dtypes
import numpy as np
from jax import lax
from jax.experimental import pallas as pl
from jax.experimental.pallas import tpu as pltpu
from jax.sharding import PartitionSpec as P

INV_STEP = 20.0
SHIFTS = (0.5, 1.5)
GROUP = 4
REACH = 4
PAIRS = ((0, 0), (0, 1), (0, 2), (1, 1), (1, 2), (2, 2))
TINY = 1e-30
HIGHEST = lax.Precision.HIGHEST
F32 = jnp.float32
BF16 = jnp.bfloat16


def gll_tables():
    points = np.array([-1.0, -0.8717401485096066, -0.5917001814331423, -0.2092992179024789, 0.2092992179024789, 0.5917001814331423, 0.8717401485096066, 1.0])
    weights = np.array([1.0 / 28.0, 0.2107042271435061, 0.3411226924835044, 0.4124587946587038, 0.4124587946587038, 0.3411226924835044, 0.2107042271435061, 1.0 / 28.0])
    product = np.array([np.prod([points[col] - points[others] for others in range(8) if others != col]) for col in range(8)])
    derivative = np.zeros((8, 8))
    for row in range(8):
        for col in range(8):
            if row != col:
                derivative[row, col] = product[row] / (product[col] * (points[row] - points[col]))
        derivative[row, row] = -np.sum(derivative[row])
    return derivative, weights, np.sum(derivative**2 * weights[:, None], axis=0)


def pieces(matrix):
    out, rest = [], matrix
    for _ in range(3):
        piece = rest.astype(ml_dtypes.bfloat16)
        out.append(piece)
        rest = rest - piece.astype(np.float64)
    return out


def tables(span):
    derivative, weights, stiff = gll_tables()
    line = (derivative.T * weights) @ derivative / weights[:, None]
    eye = np.eye(8)
    face = pieces(np.kron(line, eye) + np.kron(eye, line))
    face_mat = np.concatenate([np.concatenate([piece, piece], axis=1) for piece in face], axis=0)
    ends_mat = np.concatenate([np.concatenate([p[0::8], p[7::8]], axis=0) for p in np.split(face_mat, 3)], axis=0)
    row = pieces(np.kron(np.eye(span // 8), line.T))
    row_a = np.concatenate([np.concatenate([row[0], row[1]], 1)] * 2, axis=0)
    none = np.zeros_like(row[2])
    row_b = np.concatenate([np.concatenate([row[2], none], 1), np.concatenate([none, row[2]], 1)], axis=0)
    tile = np.tile(weights, span // 8)
    ratio = stiff / weights
    omega = weights[:, None, None] * weights[None, :, None] * tile[None, None, :]
    quot = ratio[:, None, None] + ratio[None, :, None] + np.tile(ratio, span // 8)[None, None, :]
    return face_mat, ends_mat, row_a, row_b, omega.astype(np.float32), quot.astype(np.float32)


def coef_rows(elems):
    return -(-(2 * elems) // 8) * 8


def seams(span):
    lane = lax.broadcasted_iota(jnp.int32, (8, span), 1)
    return (lane % 8 == 0) & (lane > 0), (lane % 8 == 7) & (lane < span - 1)


def tall(mask, like):
    return jnp.concatenate([mask] * (like.shape[0] // 8), axis=0) if like.shape[0] > 8 else mask


def join_span(values):
    span = values.shape[1]
    opens, closes = seams(span)
    up, down = pltpu.roll(values, 1, 1), pltpu.roll(values, span - 1, 1)
    return values + jnp.where(tall(opens, values), up, jnp.where(tall(closes, values), down, 0.0))


def join_depth(values):
    planes = []
    layers = values.shape[0] // 64
    for elem in range(layers):
        top = elem * 64
        first, last = values[top : top + 8], values[top + 56 : top + 64]
        if elem > 0:
            first = first + values[top - 8 : top]
        if elem < layers - 1:
            last = last + values[top + 64 : top + 72]
        planes += [first, values[top + 8 : top + 56], last]
    return jnp.concatenate(planes, axis=0)


def pack_kernel(shape, raw_ref, out_ref):
    depth, elems, parts = shape
    span = raw_ref.shape[1]
    spread = (lax.broadcasted_iota(jnp.int32, (parts, span), 1) // 8 == lax.broadcasted_iota(jnp.int32, (parts, span), 0)).astype(F32)
    coef = raw_ref[depth * 8 :, :parts]
    coef = jnp.where(lax.broadcasted_iota(jnp.int32, coef.shape, 0) < elems, coef * (1.0 / INV_STEP), coef)
    coef = jnp.dot(coef, spread, precision=HIGHEST, preferred_element_type=F32)
    heavy = jnp.concatenate([jnp.broadcast_to(coef[elems + e : elems + e + 1], (64, span)) for e in range(elems)], axis=0)
    value = join_depth(join_span(heavy * raw_ref[: depth * 8, :]))
    out_ref[: depth * 8, :] = value
    out_ref[depth * 8 :, :] = coef


def edge_kernel(depth, msg_ref, out_ref):
    rows = msg_ref.shape[0] // 2
    low, high = (msg_ref[pl.ds(rows + node, depth, stride=8), :] for node in (0, 7))
    out_ref[:depth] = jnp.where(lax.rem(lax.axis_index("plane"), 2) == 0, high, low)
    out_ref[depth:] = msg_ref[rows + depth * 8 :, :]


def widen_kernel(depth, edge_ref, out_ref):
    span = edge_ref.shape[1]
    out_ref[: depth * 8] = jnp.concatenate([jnp.broadcast_to(edge_ref[z : z + 1, :], (8, span)) for z in range(depth)], axis=0)
    out_ref[depth * 8 :] = edge_ref[depth:, :]


class Layout:
    def __init__(self, tall):
        wide = 2 * REACH + 1
        self.wide = wide
        self.at_once = 1 if tall else 3
        self.sums = 0
        self.minv = max(wide, 5 * self.at_once)
        self.ratio = self.minv + wide
        self.basis = self.ratio + 5
        self.second = self.basis + 3 * wide
        self.total = self.second + wide * self.at_once


def basis_kernel(counts, *refs):
    height, plane = counts
    n_in = 6 * height
    msgs = refs[:n_in]
    face_ref, ends_ref, row_a_ref, row_b_ref, omega_ref, quot_ref = refs[n_in : n_in + 6]
    fields_ref, info_ref = refs[n_in + 6 : n_in + 8]
    pool, raw, coef, weigh = refs[n_in + 8 :]
    rows, span = pool.shape[1:]
    depth = rows // 8
    own_depth = depth // height
    own_rows = own_depth * 8
    elems = depth // 8
    own_elems = elems // height
    height_pos = lax.axis_index("height")
    plane_pos = lax.axis_index("plane")
    member = lax.rem(plane_pos, GROUP)
    even = lax.rem(plane_pos // GROUP, 2) == 0
    slab_rows = own_rows + coef_rows(own_elems)
    whole = elems > 4
    lay = Layout(whole)
    wide = lay.wide

    sub = lax.broadcasted_iota(jnp.int32, (8, span), 0)
    opens, closes = seams(span)

    def stage(msg, piece, slot, block):
        top = piece * slab_rows
        raw[slot, pl.ds(pl.multiple_of(block * own_rows, own_rows), own_rows)] = msg[top : top + own_rows, :]
        for kind in range(2):
            for elem in range(own_elems):
                at = top + own_rows + kind * own_elems + elem
                coef[slot, kind, block * own_elems + elem] = jnp.broadcast_to(msg[at : at + 1, :], (8, span))

    before, here, after = 1, 1 + GROUP, 1 + 2 * GROUP
    early = member < GROUP // 2
    lone = jnp.where(
        early,
        jnp.where(member == 0, 0, after + jnp.bitwise_xor(member, 3)),
        jnp.where(member == GROUP - 1, 3 * GROUP + 1, before + jnp.bitwise_xor(member, 3)),
    )
    roles = (
        (here, (0, 1)),
        (here, (2, 3)),
        (jnp.where(even, after, before), (0, 1)),
        (jnp.where(even, before, after), (0, 1)),
        (jnp.where(early, before, after), (2, 3)),
        (lone, (None,)),
    )
    for turn in range(height):
        block = lax.rem(height_pos - turn + height, height)
        for msg, (base, owners) in zip(msgs[turn * len(roles) :], roles):
            for piece, flip in enumerate(owners):
                stage(msg, piece, base if flip is None else base + jnp.bitwise_xor(member, flip), block)

    def face_at(slot, width_node):
        return slot, pl.ds(width_node, depth, stride=8)

    def join_width(store, slot):
        low, high = face_at(slot, 7), face_at(slot + 1, 0)
        both = store[low] + store[high]
        store[low] = both
        store[high] = both

    def loop(start, stop, body, step=1):
        if whole:
            lax.fori_loop(start, stop, lambda at, carry: (body([at]), carry)[1], 0)
        else:
            for at in range(start, stop, step):
                body(list(range(at, min(at + step, stop))))

    def each(body):
        return lambda slabs: [body(at) for at in slabs]

    def split(values):
        one = values.astype(BF16)
        return one, (values - one.astype(F32)).astype(BF16)

    def along_span(halves):
        wides = [jnp.dot(jnp.concatenate(h, axis=1), row_a_ref[...], preferred_element_type=F32) for h in halves]
        if len(halves) == 2:
            extra = jnp.dot(jnp.concatenate([halves[0][0], halves[1][0]], axis=1), row_b_ref[...], preferred_element_type=F32)
            extras = [extra[:, :span], extra[:, span:]]
        else:
            extras = [jnp.dot(halves[0][0], row_b_ref[:span, :span], preferred_element_type=F32)]
        return [(w[:, :span] + w[:, span:]) + x for w, x in zip(wides, extras)]

    def along_face(matrix, halves, elem):
        top = elem * 64
        stacks = [jnp.concatenate([piece[top : top + 64] for piece in h], axis=0) for h in halves]
        made = jnp.dot(matrix, stacks[0] if len(stacks) == 1 else jnp.concatenate(stacks, axis=1), preferred_element_type=F32)
        count = made.shape[0] // 3
        return made[:count] + (made[count : 2 * count] + made[2 * count :])

    def scaled(slot, kind, elem, scale):
        value = coef[slot, kind, elem]
        return value if scale == 1.0 else value * scale

    def operator(fields, slots, scale=1.0, start=0):
        halves = [split(v) for v in fields]
        lines = along_span(halves)
        out = [[] for _ in fields]
        for elem in range(fields[0].shape[0] // 64):
            top = elem * 64
            face = along_face(face_ref[...], halves, elem)
            for i, v in enumerate(fields):
                cap = tall(scaled(slots[i], 1, start + elem, scale), face)
                kap = tall(scaled(slots[i], 0, start + elem, scale), face)
                lin = lines[i][top : top + 64] + face[:, i * span : (i + 1) * span]
                out[i].append(cap * v[top : top + 64] + kap * lin)
        return [jnp.concatenate(o, axis=0) for o in out]

    def ends(sources, targets, at, scale):
        halves = [split(pool[s]) for s in sources]
        edges = [pool[s, pl.ds(node, depth, stride=8)] for s, node in zip(sources, (7, 0))]
        lines = along_span([split(jnp.concatenate(edges, axis=0))])[0]
        both = [along_face(ends_ref[...], halves, elem) for elem in range(elems)]
        for i in range(2):
            joined = []
            for elem in range(elems):
                lin = lines[i * depth + elem * 8 : i * depth + elem * 8 + 8] + both[elem][8 * (1 - i) : 8 * (2 - i), i * span : (i + 1) * span]
                slot = member + at[i]
                joined.append(join_span(scaled(slot, 1, elem, scale) * edges[i][elem * 8 : elem * 8 + 8] + scaled(slot, 0, elem, scale) * lin))
            final = []
            for elem in range(elems):
                value = joined[elem]
                if elem > 0:
                    value = value + jnp.where(sub == 0, pltpu.roll(joined[elem - 1], 1, 0), 0.0)
                if elem < elems - 1:
                    value = value + jnp.where(sub == 7, pltpu.roll(joined[elem + 1], 7, 0), 0.0)
                final.append(value)
            pool[face_at(targets[i], (7, 0)[i])] = jnp.concatenate(final, axis=0)

    def step(chains, low, high, shift):
        def apply(work):
            made = operator([pool[here + at] for here, _, at in work], [member + at for _, _, at in work], 1.0 / shift)
            for (_, sums, at), value in zip(work, made):
                pool[sums + at] = join_depth(join_span(value))

        for here, sums, _ in chains:
            ends((here + low, here + high), (sums + low, sums + high), (low, high), 1.0 / shift)
        if whole:
            for here, sums, after in chains:
                loop(low + 1, high, each(lambda at: apply([(here, sums, at)])))
        else:
            work = [(here, sums, at) for here, sums, _ in chains for at in range(low + 1, high)]
            for first in range(0, len(work), 2):
                apply(work[first : first + 2])
        for here, sums, after in chains:
            loop(low, high, each(lambda at: join_width(pool, sums + at)))

            def advance(at):
                pool[after + at] = pool[lay.minv + at - 1] * pool[sums + at] - pool[here + at]

            loop(low + 1, high, each(advance))

    def constant(kind, at):
        layers = [[join_span(coef[member + at + side, kind, elem]) for elem in range(elems)] for side in (-1, 0, 1)]
        wide_sum = lambda low, mid, high: mid + jnp.where(sub == 0, low, jnp.where(sub == 7, high, 0.0))
        inside = [wide_sum(*(layers[side][elem] for side in range(3))) for elem in range(elems)]
        planes = []
        for elem in range(elems):
            first = inside[elem] if elem == 0 else inside[elem] + inside[elem - 1]
            last = inside[elem] if elem == elems - 1 else inside[elem] + inside[elem + 1]
            planes += [first] + [inside[elem]] * 6 + [last]
        return jnp.concatenate(planes, axis=0)

    def inverse_slab(at):
        quot = jnp.concatenate([quot_ref[...].reshape(64, span)] * elems, axis=0)
        mass = constant(1, at)
        inverse = 1.0 / jnp.maximum(mass + quot * constant(0, at), TINY)
        pool[lay.minv + at - 1] = inverse
        return inverse, mass

    def first_slab(at):
        inverse, _ = inverse_slab(at)
        pool[lay.basis + at - 1] = inverse * raw[member + at]

    def inner_slab(at):
        inverse, mass = inverse_slab(at)
        pool[lay.basis + at - 1] = inverse * raw[member + at]
        pool[lay.ratio + at - 3] = inverse * mass

    def join_blocks(slot):
        for block in range(1, height):
            low, high = pl.ds(block * own_rows - 8, 8), pl.ds(block * own_rows, 8)
            both = raw[slot, low] + raw[slot, high]
            raw[slot, low] = both
            raw[slot, high] = both

    loop(0, wide + 2, each(lambda at: join_blocks(member + at)))
    loop(0, wide + 1, each(lambda at: join_width(raw, member + at)))
    loop(1, 3, each(first_slab))
    loop(3, wide - 1, each(inner_slab))
    loop(wide - 1, wide + 1, each(first_slab))

    mid = REACH + 1

    def own(slot):
        value = pool[slot, :own_rows]
        for block in range(1, height):
            value = jnp.where(height_pos == block, pool[slot, block * own_rows : (block + 1) * own_rows], value)
        return value

    shape = (own_depth, 8, span)
    zpos = lax.broadcasted_iota(jnp.int32, shape, 0) + height_pos * own_depth
    xpos = lax.broadcasted_iota(jnp.int32, shape, 1) + plane_pos * 8

    def copies(pos, extent):
        return jnp.where(((pos % 8 == 7) & (pos < extent - 1)) | ((pos % 8 == 0) & (pos > 0)), 0.5, 1.0)

    share = copies(zpos, depth) * copies(xpos, plane * 8) * jnp.where(opens | closes, 0.5, 1.0)
    omega = jnp.concatenate([omega_ref[...].reshape(64, span)] * own_elems, axis=0)
    weigh[...] = share.reshape(own_rows, span) * omega / own(lay.minv + REACH)

    for level in range(2):
        step([(lay.basis + level * wide - 1, lay.sums - 1, lay.basis + (level + 1) * wide - 1)], 1 + level, wide - level, SHIFTS[level])
    for vec in range(3):
        fields_ref[vec] = own(lay.basis + vec * wide + REACH)

    def second(vecs):
        homes = [lay.second + wide * i for i in range(lay.at_once)]
        sums = [lay.sums + 5 * i - 3 for i in range(lay.at_once)]
        for vec, home in zip(vecs, homes):

            def begin(at):
                pool[home + at - 3] = pool[lay.ratio + at - 3] * pool[lay.basis + vec * wide + at - 1]

            loop(3, 8, each(begin))
        step([(h - 3, t, h + 1) for h, t in zip(homes, sums)], 3, 7, SHIFTS[0])
        step([(h + 1, t, h + 3) for h, t in zip(homes, sums)], 4, 6, SHIFTS[1])
        for vec, home in zip(vecs, homes):
            for level, slot in enumerate((2, 6, 8)):
                fields_ref[3 + 3 * level + vec] = own(home + slot)

    if lay.at_once == 3:
        second([0, 1, 2])
    else:
        loop(0, 3, each(lambda vec: second([vec])))

    slot = member + mid
    start = height_pos * own_elems

    def total(values):
        return jnp.sum(values.reshape(shape), axis=0)

    parts = []
    left = [weigh[...] * fields_ref[i] for i in range(3)]
    parts += [total(left[i] * fields_ref[j]) for i, j in PAIRS]
    lasts = (2, 9, 10, 11)
    energy = []
    for k in (0, 2):
        energy += operator([fields_ref[i] for i in lasts[k : k + 2]], [slot] * 2, 1.0, start)
    energy = [omega * e for e in energy]
    parts.append(total(fields_ref[2] * energy[0]))
    for k, l in PAIRS:
        pairs = PAIRS if k == l else [(i, j) for i in range(3) for j in range(3)]
        left = [weigh[...] * fields_ref[3 + 3 * k + i] for i in range(3)]
        parts += [total(left[i] * fields_ref[3 + 3 * l + j]) for i, j in pairs]
    parts += [total(fields_ref[9 + i] * energy[1 + j]) for i, j in PAIRS]
    lines = [jnp.sum(part, axis=0, keepdims=True) for part in parts]
    lines.append(jnp.zeros((span - len(lines), span), F32))
    sums = lax.dot_general(jnp.ones((8, span), F32), jnp.concatenate(lines, axis=0), (((1,), (1,)), ((), ())), precision=HIGHEST, preferred_element_type=F32)

    heavy = jnp.concatenate([jnp.concatenate([coef[slot, 1, start + elem]] * 8, axis=0) for elem in range(own_elems)], axis=0) * (omega * 0.125)
    rows_of = []
    for index in range(12):
        mass = heavy * fields_ref[index]
        for elem in range(own_elems):
            rows_of.append(jnp.sum(mass[elem * 64 : elem * 64 + 64], axis=0, keepdims=True))
    stack = jnp.concatenate(rows_of, axis=0)
    cells = span // 8
    per_row = span // cells
    spread = (lax.broadcasted_iota(jnp.int32, (span, span), 0) // 8 == lax.broadcasted_iota(jnp.int32, (span, span), 1) % cells).astype(F32)
    stack = jnp.dot(stack, spread, precision=HIGHEST, preferred_element_type=F32)
    place = lax.broadcasted_iota(jnp.int32, stack.shape, 0) % per_row == lax.broadcasted_iota(jnp.int32, stack.shape, 1) // cells
    stack = jnp.where(place, stack, 0.0).reshape(stack.shape[0] // per_row, per_row, span)
    info = jnp.concatenate([jnp.sum(stack, axis=1), sums[:1]], axis=0)
    info_ref[...] = jnp.broadcast_to(info[None], info_ref.shape)


def galerkin(gram, energy):
    n00, n01, n02, n11, n12, n22 = gram
    first, later = SHIFTS
    h00, h01, h02 = first * (n01 + n00), first * (n11 + n01), first * (n12 + n02)
    h11, h12 = later * (n12 + n11), later * (n22 + n12)
    low10, low20 = h01 / h00, h02 / h00
    piv1 = h11 - low10 * h01
    off12 = h12 - low10 * h02
    low21 = off12 / piv1
    piv2 = energy - low20 * h02 - low21 * off12
    y0 = n00
    y1 = n01 - low10 * y0
    y2 = n02 - low20 * y0 - low21 * y1
    c2 = y2 / piv2
    c1 = y1 / piv1 - low21 * c2
    c0 = y0 / h00 - low10 * c1 - low20 * c2
    return c0, c1, c2


def combine_kernel(info_ref, fields_ref, owner_ref, place_ref, second_ref, first_ref, grad_ref):
    devices, lines, span = info_ref.shape
    ones = jnp.ones((devices, span), F32)
    contract = (((0,), (0,)), ((), ()))
    wide = lax.dot_general(info_ref[:, lines - 1, :], ones, contract, precision=HIGHEST, preferred_element_type=F32)
    take = [wide[i : i + 1, :] for i in range(7 + 45 + 6)]
    coef = galerkin(take[:6], take[6])
    at = 7
    double = [(2.0 if i != j else 1.0) * coef[i] * coef[j] for i, j in PAIRS]
    every = [coef[i] * coef[j] for i in range(3) for j in range(3)]
    gram = []
    for k, l in PAIRS:
        factors = double if k == l else every
        gram.append(sum(f * t for f, t in zip(factors, take[at : at + len(factors)])))
        at += len(factors)
    energy = sum(f * t for f, t in zip(double, take[at : at + 6]))
    outer = galerkin(gram, energy)
    factors = list(coef) + [d * c for d in outer for c in coef]

    second = factors[0] * fields_ref[0] + factors[1] * fields_ref[1] + factors[2] * fields_ref[2]
    second_ref[...] = second.reshape(second_ref.shape)
    first = factors[3] * fields_ref[3]
    for i in range(4, 12):
        first = first + factors[i] * fields_ref[i]
    first_ref[...] = first.reshape(first_ref.shape)

    per_line = 12 // (lines - 1)
    cells = span // per_line
    row = lax.broadcasted_iota(jnp.int32, (span, span), 0)
    for step in range(2):
        holder = (owner_ref[step : step + 1, :] == lax.broadcasted_iota(jnp.int32, (devices, span), 0)).astype(F32)
        here = place_ref[step : step + 1, :] == row % cells
        result = jnp.zeros((1, span), F32)
        for line in range(lines - 1):
            fields = [f for f in range(line * per_line, (line + 1) * per_line) if (f >= 3) == (step == 0)]
            if not fields:
                continue
            picked = lax.dot_general(info_ref[:, line, :], holder, contract, precision=HIGHEST, preferred_element_type=F32)
            picked = jnp.where(here, picked, 0.0)
            for f in fields:
                lo = (f - line * per_line) * cells
                result = result + factors[f] * jnp.sum(picked[lo : lo + cells], axis=0, keepdims=True)
        grad_ref[step : step + 1, :] = result


def per_device(counts, cotangent, conductivity, capacity, sources):
    height, plane = counts
    depth, _, span = cotangent.shape
    elems = depth // 8
    cells = span // 8
    groups = plane // GROUP
    devices = height * plane
    vmem = pl.BlockSpec(memory_space=pltpu.VMEM)

    rows = depth * 8 + coef_rows(elems)
    lines = [conductivity.reshape(elems, cells), capacity.reshape(elems, cells)]
    lines = [jnp.pad(line, ((0, 0), (0, span - cells))) for line in lines]
    filler = jnp.zeros((rows - depth * 8 - 2 * elems, span), F32)
    raw = jnp.concatenate([cotangent.reshape(depth * 8, span), *lines, filler], axis=0)
    message = pl.pallas_call(
        functools.partial(pack_kernel, (depth, elems, cells)),
        out_shape=jax.ShapeDtypeStruct((rows, span), F32),
        in_specs=[vmem],
        out_specs=vmem,
        compiler_params=pltpu.CompilerParams(vmem_limit_bytes=4 * 2**20),
    )(raw)

    def move(value, pairs):
        return lax.ppermute(value, "plane", pairs) if pairs else jnp.zeros_like(value)

    def both_ways(pairs):
        return [*pairs, *((b, a) for a, b in pairs)]

    def shift(gap, moving):
        return [(g * GROUP + m, (g + gap) * GROUP + m) for g in range(groups) for m in moving if 0 <= g + gap < groups]

    half = jnp.concatenate([message, move(message, [(p, p ^ 1) for p in range(plane)])], axis=0)
    every = range(GROUP)
    pair = move(half, both_ways([(a, b) for a, b in shift(1, every) if (a // GROUP) % 2 == 0]))
    cross = move(half, both_ways([(a, b) for a, b in shift(1, every) if (a // GROUP) % 2 == 1]))
    other = move(half, [(p, p ^ 2) for p in range(plane)])
    side = move(other, shift(1, (0, 1)) + shift(-1, (2, 3)))
    edge = pl.pallas_call(
        functools.partial(edge_kernel, depth),
        out_shape=jax.ShapeDtypeStruct((rows - depth * 7, span), F32),
        in_specs=[vmem],
        out_specs=vmem,
        compiler_params=pltpu.CompilerParams(vmem_limit_bytes=4 * 2**20),
    )(other)
    edge = move(edge, shift(2, (0,)) + shift(-1, (1,)) + shift(1, (2,)) + shift(-2, (3,)))
    lone = pl.pallas_call(
        functools.partial(widen_kernel, depth),
        out_shape=jax.ShapeDtypeStruct((rows, span), F32),
        in_specs=[vmem],
        out_specs=vmem,
        cost_estimate=pl.CostEstimate(flops=1000000, bytes_accessed=1000000, transcendentals=0),
        compiler_params=pltpu.CompilerParams(vmem_limit_bytes=4 * 2**20),
    )(edge)
    sent = (half, other, pair, cross, side, lone)
    operands = list(sent)
    for turn in range(1, height):
        operands += [lax.ppermute(arr, "height", [(h, (h + turn) % height) for h in range(height)]) for arr in sent]

    lay = Layout(elems * height > 4)
    consts = tables(span)
    slots = 3 * GROUP + 2
    slab_bytes = 4 * depth * 8 * height * span
    fields, info = pl.pallas_call(
        functools.partial(basis_kernel, counts),
        out_shape=(jax.ShapeDtypeStruct((12, depth * 8, span), F32), jax.ShapeDtypeStruct((devices, 12 * elems * cells // span + 1, span), F32)),
        in_specs=[vmem] * (len(operands) + len(consts)),
        out_specs=(vmem, vmem),
        scratch_shapes=[
            pltpu.VMEM((lay.total, depth * 8 * height, span), F32),
            pltpu.VMEM((slots, depth * 8 * height, span), F32),
            pltpu.VMEM((slots, 2, elems * height, 8, span), F32),
            pltpu.VMEM((depth * 8, span), F32),
        ],
        compiler_params=pltpu.CompilerParams(vmem_limit_bytes=(lay.total + 3 * slots + 14) * slab_bytes + 12 * 2**20),
    )(*operands, *[jnp.asarray(c) for c in consts])

    shared = lax.all_to_all(info, ("height", "plane"), 0, 0, tiled=True)

    cell = sources % cells
    column = sources // cells
    wide_elem = column % plane
    deep_elem = column // plane
    owner = (deep_elem // elems) * plane + wide_elem
    place = (deep_elem % elems) * cells + cell
    return pl.pallas_call(
        combine_kernel,
        out_shape=(
            jax.ShapeDtypeStruct(cotangent.shape, F32),
            jax.ShapeDtypeStruct(cotangent.shape, F32),
            jax.ShapeDtypeStruct(sources.shape, F32),
        ),
        in_specs=[vmem] * 4,
        out_specs=(vmem, vmem, vmem),
        compiler_params=pltpu.CompilerParams(vmem_limit_bytes=8 * 2**20),
    )(shared, fields, owner, place)


def solution(mesh):
    counts = (mesh.shape["height"], mesh.shape["plane"])
    field = P("height", "plane", None)
    return jax.shard_map(
        functools.partial(per_device, counts),
        mesh=mesh,
        in_specs=(field, field, field, P()),
        out_specs=(field, field, P()),
        check_vma=False,
    )
```

```python
import functools

import jax
import jax.numpy as jnp
import ml_dtypes
import numpy as np
from jax import lax
from jax.experimental import pallas as pl
from jax.experimental.pallas import tpu as pltpu
from jax.sharding import PartitionSpec as P

INV_STEP = 20.0
SHIFTS = (0.5, 1.5)
GROUP = 4
REACH = 4
PAIRS = ((0, 0), (0, 1), (0, 2), (1, 1), (1, 2), (2, 2))
BANDS = ((0, 0), (0, 1), (1, 1), (1, 2), (2, 2))
TINY = 1e-30
HIGHEST = lax.Precision.HIGHEST
F32 = jnp.float32
BF16 = jnp.bfloat16


def gll_tables():
    points = np.array([-1.0, -0.8717401485096066, -0.5917001814331423, -0.2092992179024789, 0.2092992179024789, 0.5917001814331423, 0.8717401485096066, 1.0])
    weights = np.array([1.0 / 28.0, 0.2107042271435061, 0.3411226924835044, 0.4124587946587038, 0.4124587946587038, 0.3411226924835044, 0.2107042271435061, 1.0 / 28.0])
    product = np.array([np.prod([points[col] - points[others] for others in range(8) if others != col]) for col in range(8)])
    derivative = np.zeros((8, 8))
    for row in range(8):
        for col in range(8):
            if row != col:
                derivative[row, col] = product[row] / (product[col] * (points[row] - points[col]))
        derivative[row, row] = -np.sum(derivative[row])
    return derivative, weights, np.sum(derivative**2 * weights[:, None], axis=0)


def pieces(matrix):
    out, rest = [], matrix
    for _ in range(3):
        piece = rest.astype(ml_dtypes.bfloat16)
        out.append(piece)
        rest = rest - piece.astype(np.float64)
    return out


def tables(span):
    derivative, weights, stiff = gll_tables()
    line = (derivative.T * weights) @ derivative / weights[:, None]
    eye = np.eye(8)
    face = pieces(np.kron(line, eye) + np.kron(eye, line))
    face_mat = np.concatenate([np.concatenate([piece, piece], axis=1) for piece in face], axis=0)
    ends_mat = np.concatenate([np.concatenate([p[0::8], p[7::8]], axis=0) for p in np.split(face_mat, 3)], axis=0)
    row = pieces(np.kron(np.eye(span // 8), line.T))
    row_a = np.concatenate([np.concatenate([row[0], row[1]], 1)] * 2, axis=0)
    none = np.zeros_like(row[2])
    row_b = np.concatenate([np.concatenate([row[2], none], 1), np.concatenate([none, row[2]], 1)], axis=0)
    tile = np.tile(weights, span // 8)
    ratio = stiff / weights
    omega = weights[:, None, None] * weights[None, :, None] * tile[None, None, :]
    quot = ratio[:, None, None] + ratio[None, :, None] + np.tile(ratio, span // 8)[None, None, :]
    return face_mat, ends_mat, row_a, row_b, omega.astype(np.float32), quot.astype(np.float32)


def coef_rows(elems):
    return -(-(2 * elems) // 8) * 8


def seams(span):
    lane = lax.broadcasted_iota(jnp.int32, (8, span), 1)
    return (lane % 8 == 0) & (lane > 0), (lane % 8 == 7) & (lane < span - 1)


def tall(mask, like):
    return jnp.concatenate([mask] * (like.shape[0] // 8), axis=0) if like.shape[0] > 8 else mask


def join_span(values):
    span = values.shape[1]
    opens, closes = seams(span)
    up, down = pltpu.roll(values, 1, 1), pltpu.roll(values, span - 1, 1)
    return values + jnp.where(tall(opens, values), up, jnp.where(tall(closes, values), down, 0.0))


def join_depth(values):
    planes = []
    layers = values.shape[0] // 64
    for elem in range(layers):
        top = elem * 64
        first, last = values[top : top + 8], values[top + 56 : top + 64]
        if elem > 0:
            first = first + values[top - 8 : top]
        if elem < layers - 1:
            last = last + values[top + 64 : top + 72]
        planes += [first, values[top + 8 : top + 56], last]
    return jnp.concatenate(planes, axis=0)


def pack_kernel(shape, raw_ref, out_ref):
    depth, elems, parts = shape
    span = raw_ref.shape[1]
    spread = (lax.broadcasted_iota(jnp.int32, (parts, span), 1) // 8 == lax.broadcasted_iota(jnp.int32, (parts, span), 0)).astype(F32)
    coef = raw_ref[depth * 8 :, :parts]
    pair = [coef[2 * e : 2 * e + 1] * (1.0 / INV_STEP) for e in range(elems)] + [coef[2 * e + 1 : 2 * e + 2] for e in range(elems)]
    coef = jnp.concatenate([*pair, coef[2 * elems :]], axis=0)
    coef = jnp.dot(coef, spread, precision=HIGHEST, preferred_element_type=F32)
    heavy = jnp.concatenate([jnp.broadcast_to(coef[elems + e : elems + e + 1], (64, span)) for e in range(elems)], axis=0)
    value = join_depth(join_span(heavy * raw_ref[: depth * 8, :]))
    out_ref[: depth * 8, :] = value
    out_ref[depth * 8 :, :] = coef


def edge_kernel(depth, msg_ref, out_ref):
    rows = msg_ref.shape[0] // 2
    low, high = (msg_ref[pl.ds(rows + node, depth, stride=8), :] for node in (0, 7))
    out_ref[:depth] = jnp.where(lax.rem(lax.axis_index("plane"), 2) == 0, high, low)
    out_ref[depth:] = msg_ref[rows + depth * 8 :, :]


def widen_kernel(depth, edge_ref, out_ref):
    span = edge_ref.shape[1]
    out_ref[: depth * 8] = jnp.concatenate([jnp.broadcast_to(edge_ref[z : z + 1, :], (8, span)) for z in range(depth)], axis=0)
    out_ref[depth * 8 :] = edge_ref[depth:, :]


class Layout:
    def __init__(self, tall):
        wide = 2 * REACH + 1
        self.wide = wide
        self.at_once = 1 if tall else 3
        self.sums = 0
        self.minv = max(wide, 5 * self.at_once)
        self.ratio = self.minv + wide
        self.basis = self.ratio + 5
        self.second = self.basis + 3 * wide
        self.total = self.second + wide * self.at_once


def basis_kernel(counts, *refs):
    height, plane = counts
    n_in = 6 * height
    msgs = refs[:n_in]
    face_ref, ends_ref, row_a_ref, row_b_ref, omega_ref, quot_ref = refs[n_in : n_in + 6]
    fields_ref, info_ref = refs[n_in + 6 : n_in + 8]
    pool, raw, coef, weigh = refs[n_in + 8 :]
    rows, span = pool.shape[1:]
    depth = rows // 8
    own_depth = depth // height
    own_rows = own_depth * 8
    elems = depth // 8
    own_elems = elems // height
    height_pos = lax.axis_index("height")
    plane_pos = lax.axis_index("plane")
    member = lax.rem(plane_pos, GROUP)
    even = lax.rem(plane_pos // GROUP, 2) == 0
    slab_rows = own_rows + coef_rows(own_elems)
    whole = elems > 4
    lay = Layout(whole)
    wide = lay.wide

    sub = lax.broadcasted_iota(jnp.int32, (8, span), 0)
    opens, closes = seams(span)

    def stage(msg, piece, slot, block):
        top = piece * slab_rows
        raw[slot, pl.ds(pl.multiple_of(block * own_rows, own_rows), own_rows)] = msg[top : top + own_rows, :]
        for kind in range(2):
            for elem in range(own_elems):
                at = top + own_rows + kind * own_elems + elem
                coef[slot, kind, block * own_elems + elem] = jnp.broadcast_to(msg[at : at + 1, :], (8, span))

    before, here, after = 1, 1 + GROUP, 1 + 2 * GROUP
    early = member < GROUP // 2
    lone = jnp.where(
        early,
        jnp.where(member == 0, 0, after + jnp.bitwise_xor(member, 3)),
        jnp.where(member == GROUP - 1, 3 * GROUP + 1, before + jnp.bitwise_xor(member, 3)),
    )
    roles = (
        (here, (0, 1)),
        (here, (2, 3)),
        (jnp.where(even, after, before), (0, 1)),
        (jnp.where(even, before, after), (0, 1)),
        (jnp.where(early, before, after), (2, 3)),
        (lone, (None,)),
    )
    for turn in range(height):
        block = lax.rem(height_pos - turn + height, height)
        for msg, (base, owners) in zip(msgs[turn * len(roles) :], roles):
            for piece, flip in enumerate(owners):
                stage(msg, piece, base if flip is None else base + jnp.bitwise_xor(member, flip), block)

    def face_at(slot, width_node):
        return slot, pl.ds(width_node, depth, stride=8)

    def join_width(store, slot):
        low, high = face_at(slot, 7), face_at(slot + 1, 0)
        both = store[low] + store[high]
        store[low] = both
        store[high] = both

    def loop(start, stop, body, step=1):
        if whole:
            lax.fori_loop(start, stop, lambda at, carry: (body([at]), carry)[1], 0)
        else:
            for at in range(start, stop, step):
                body(list(range(at, min(at + step, stop))))

    def each(body):
        return lambda slabs: [body(at) for at in slabs]

    def split(values):
        one = values.astype(BF16)
        return one, (values - one.astype(F32)).astype(BF16)

    def along_span(halves):
        wides = [jnp.dot(jnp.concatenate(h, axis=1), row_a_ref[...], preferred_element_type=F32) for h in halves]
        if len(halves) == 2:
            extra = jnp.dot(jnp.concatenate([halves[0][0], halves[1][0]], axis=1), row_b_ref[...], preferred_element_type=F32)
            extras = [extra[:, :span], extra[:, span:]]
        else:
            extras = [jnp.dot(halves[0][0], row_b_ref[:span, :span], preferred_element_type=F32)]
        return [(w[:, :span] + w[:, span:]) + x for w, x in zip(wides, extras)]

    def along_face(matrix, halves, elem):
        top = elem * 64
        stacks = [jnp.concatenate([piece[top : top + 64] for piece in h], axis=0) for h in halves]
        made = jnp.dot(matrix, stacks[0] if len(stacks) == 1 else jnp.concatenate(stacks, axis=1), preferred_element_type=F32)
        count = made.shape[0] // 3
        return made[:count] + (made[count : 2 * count] + made[2 * count :])

    def scaled(slot, kind, elem, scale):
        value = coef[slot, kind, elem]
        return value if scale == 1.0 else value * scale

    def operator(fields, slots, scale=1.0, start=0):
        halves = [split(v) for v in fields]
        lines = along_span(halves)
        out = [[] for _ in fields]
        for elem in range(fields[0].shape[0] // 64):
            top = elem * 64
            face = along_face(face_ref[...], halves, elem)
            for i, v in enumerate(fields):
                cap = tall(scaled(slots[i], 1, start + elem, scale), face)
                kap = tall(scaled(slots[i], 0, start + elem, scale), face)
                lin = lines[i][top : top + 64] + face[:, i * span : (i + 1) * span]
                out[i].append(cap * v[top : top + 64] + kap * lin)
        return [jnp.concatenate(o, axis=0) for o in out]

    def ends(sources, targets, at, scale):
        halves = [split(pool[s]) for s in sources]
        edges = [pool[s, pl.ds(node, depth, stride=8)] for s, node in zip(sources, (7, 0))]
        lines = along_span([split(jnp.concatenate(edges, axis=0))])[0]
        both = [along_face(ends_ref[...], halves, elem) for elem in range(elems)]
        for i in range(2):
            joined = []
            for elem in range(elems):
                lin = lines[i * depth + elem * 8 : i * depth + elem * 8 + 8] + both[elem][8 * (1 - i) : 8 * (2 - i), i * span : (i + 1) * span]
                slot = member + at[i]
                joined.append(join_span(scaled(slot, 1, elem, scale) * edges[i][elem * 8 : elem * 8 + 8] + scaled(slot, 0, elem, scale) * lin))
            final = []
            for elem in range(elems):
                value = joined[elem]
                if elem > 0:
                    value = value + jnp.where(sub == 0, pltpu.roll(joined[elem - 1], 1, 0), 0.0)
                if elem < elems - 1:
                    value = value + jnp.where(sub == 7, pltpu.roll(joined[elem + 1], 7, 0), 0.0)
                final.append(value)
            pool[face_at(targets[i], (7, 0)[i])] = jnp.concatenate(final, axis=0)

    def step(chains, low, high, shift):
        def apply(work):
            made = operator([pool[here + at] for here, _, at in work], [member + at for _, _, at in work], 1.0 / shift)
            for (_, sums, at), value in zip(work, made):
                pool[sums + at] = join_depth(join_span(value))

        if whole:
            for here, sums, after in chains:
                loop(low + 1, high, each(lambda at: apply([(here, sums, at)])))
        else:
            work = [(here, sums, at) for here, sums, _ in chains for at in range(low + 1, high)]
            for first in range(0, len(work), 2):
                apply(work[first : first + 2])
        for here, sums, _ in chains:
            ends((here + low, here + high), (sums + low, sums + high), (low, high), 1.0 / shift)
        for here, sums, after in chains:
            loop(low, high, each(lambda at: join_width(pool, sums + at)))

            def advance(at):
                pool[after + at] = pool[lay.minv + at - 1] * pool[sums + at] - pool[here + at]

            loop(low + 1, high, each(advance))

    def constant(kind, at):
        layers = [[join_span(coef[member + at + side, kind, elem]) for elem in range(elems)] for side in (-1, 0, 1)]
        wide_sum = lambda low, mid, high: mid + jnp.where(sub == 0, low, jnp.where(sub == 7, high, 0.0))
        inside = [wide_sum(*(layers[side][elem] for side in range(3))) for elem in range(elems)]
        planes = []
        for elem in range(elems):
            first = inside[elem] if elem == 0 else inside[elem] + inside[elem - 1]
            last = inside[elem] if elem == elems - 1 else inside[elem] + inside[elem + 1]
            planes += [first] + [inside[elem]] * 6 + [last]
        return jnp.concatenate(planes, axis=0)

    def inverse_slab(at):
        quot = jnp.concatenate([quot_ref[...].reshape(64, span)] * elems, axis=0)
        mass = constant(1, at)
        inverse = 1.0 / jnp.maximum(mass + quot * constant(0, at), TINY)
        pool[lay.minv + at - 1] = inverse
        return inverse, mass

    def first_slab(at):
        inverse, _ = inverse_slab(at)
        pool[lay.basis + at - 1] = inverse * raw[member + at]

    def inner_slab(at):
        inverse, mass = inverse_slab(at)
        pool[lay.basis + at - 1] = inverse * raw[member + at]
        pool[lay.ratio + at - 3] = inverse * mass

    def join_blocks(slot):
        for block in range(1, height):
            low, high = pl.ds(block * own_rows - 8, 8), pl.ds(block * own_rows, 8)
            both = raw[slot, low] + raw[slot, high]
            raw[slot, low] = both
            raw[slot, high] = both

    loop(0, wide + 2, each(lambda at: join_blocks(member + at)))
    loop(0, wide + 1, each(lambda at: join_width(raw, member + at)))
    loop(1, 3, each(first_slab))
    loop(3, wide - 1, each(inner_slab))
    loop(wide - 1, wide + 1, each(first_slab))

    mid = REACH + 1

    def own(slot):
        value = pool[slot, :own_rows]
        for block in range(1, height):
            value = jnp.where(height_pos == block, pool[slot, block * own_rows : (block + 1) * own_rows], value)
        return value

    shape = (own_depth, 8, span)
    zpos = lax.broadcasted_iota(jnp.int32, shape, 0) + height_pos * own_depth
    xpos = lax.broadcasted_iota(jnp.int32, shape, 1) + plane_pos * 8

    def copies(pos, extent):
        return jnp.where(((pos % 8 == 7) & (pos < extent - 1)) | ((pos % 8 == 0) & (pos > 0)), 0.5, 1.0)

    share = copies(zpos, depth) * copies(xpos, plane * 8) * jnp.where(opens | closes, 0.5, 1.0)
    omega = jnp.concatenate([omega_ref[...].reshape(64, span)] * own_elems, axis=0)
    weigh[...] = share.reshape(own_rows, span) * omega / own(lay.minv + REACH)

    for level in range(2):
        step([(lay.basis + level * wide - 1, lay.sums - 1, lay.basis + (level + 1) * wide - 1)], 1 + level, wide - level, SHIFTS[level])
    for vec in range(3):
        fields_ref[vec] = own(lay.basis + vec * wide + REACH)

    def second(vecs):
        homes = [lay.second + wide * i for i in range(lay.at_once)]
        sums = [lay.sums + 5 * i - 3 for i in range(lay.at_once)]
        for vec, home in zip(vecs, homes):

            def begin(at):
                pool[home + at - 3] = pool[lay.ratio + at - 3] * pool[lay.basis + vec * wide + at - 1]

            loop(3, 8, each(begin))
        step([(h - 3, t, h + 1) for h, t in zip(homes, sums)], 3, 7, SHIFTS[0])
        step([(h + 1, t, h + 3) for h, t in zip(homes, sums)], 4, 6, SHIFTS[1])
        for vec, home in zip(vecs, homes):
            for level, slot in enumerate((2, 6, 8)):
                fields_ref[3 + 3 * level + vec] = own(home + slot)

    if lay.at_once == 3:
        second([0, 1, 2])
    else:
        loop(0, 3, each(lambda vec: second([vec])))

    slot = member + mid
    start = height_pos * own_elems

    def total(values):
        return jnp.sum(values.reshape(shape), axis=0)

    parts = []
    left = [weigh[...] * fields_ref[i] for i in range(3)]
    parts += [total(left[i] * fields_ref[j]) for i, j in BANDS]
    lasts = (2, 9, 10, 11)
    energy = []
    for k in (0, 2):
        energy += operator([fields_ref[i] for i in lasts[k : k + 2]], [slot] * 2, 1.0, start)
    energy = [omega * e for e in energy]
    parts.append(total(fields_ref[2] * energy[0]))
    for k, l in BANDS:
        left = [weigh[...] * fields_ref[3 + 3 * k + i] for i in range(3)]
        parts += [total(left[i] * fields_ref[3 + 3 * l + j]) for i, j in PAIRS]
    parts += [total(fields_ref[9 + i] * energy[1 + j]) for i, j in PAIRS]
    lines = [jnp.sum(part, axis=0, keepdims=True) for part in parts]
    lines.append(jnp.zeros((span - len(lines), span), F32))
    sums = lax.dot_general(jnp.ones((8, span), F32), jnp.concatenate(lines, axis=0), (((1,), (1,)), ((), ())), precision=HIGHEST, preferred_element_type=F32)

    heavy = jnp.concatenate([jnp.concatenate([coef[slot, 1, start + elem]] * 8, axis=0) for elem in range(own_elems)], axis=0) * (omega * 0.125)
    rows_of = []
    for index in range(12):
        mass = heavy * fields_ref[index]
        for elem in range(own_elems):
            rows_of.append(jnp.sum(mass[elem * 64 : elem * 64 + 64], axis=0, keepdims=True))
    stack = jnp.concatenate(rows_of, axis=0)
    cells = span // 8
    per_row = span // cells
    spread = (lax.broadcasted_iota(jnp.int32, (span, span), 0) // 8 == lax.broadcasted_iota(jnp.int32, (span, span), 1) % cells).astype(F32)
    stack = jnp.dot(stack, spread, precision=HIGHEST, preferred_element_type=F32)
    place = lax.broadcasted_iota(jnp.int32, stack.shape, 0) % per_row == lax.broadcasted_iota(jnp.int32, stack.shape, 1) // cells
    stack = jnp.where(place, stack, 0.0).reshape(stack.shape[0] // per_row, per_row, span)
    info = jnp.concatenate([jnp.sum(stack, axis=1), sums[:1]], axis=0)
    info_ref[...] = jnp.broadcast_to(info[None], info_ref.shape)


def galerkin(gram, energy):
    n00, n01, n11, n12, n22 = gram
    first, later = SHIFTS
    n02 = (first / later) * (n11 + n01) - n01
    h00, h01, h02 = first * (n01 + n00), first * (n11 + n01), first * (n12 + n02)
    h11, h12 = later * (n12 + n11), later * (n22 + n12)
    low10, low20 = h01 / h00, h02 / h00
    piv1 = h11 - low10 * h01
    off12 = h12 - low10 * h02
    low21 = off12 / piv1
    piv2 = energy - low20 * h02 - low21 * off12
    y0 = n00
    y1 = n01 - low10 * y0
    y2 = n02 - low20 * y0 - low21 * y1
    c2 = y2 / piv2
    c1 = y1 / piv1 - low21 * c2
    c0 = y0 / h00 - low10 * c1 - low20 * c2
    return c0, c1, c2


def combine_kernel(info_ref, fields_ref, owner_ref, place_ref, second_ref, first_ref, grad_ref):
    devices, lines, span = info_ref.shape
    ones = jnp.ones((devices, span), F32)
    contract = (((0,), (0,)), ((), ()))
    wide = lax.dot_general(info_ref[:, lines - 1, :], ones, contract, precision=HIGHEST, preferred_element_type=F32)
    take = [wide[i : i + 1, :] for i in range(6 + 30 + 6)]
    coef = galerkin(take[:5], take[5])
    double = [(2.0 if i != j else 1.0) * coef[i] * coef[j] for i, j in PAIRS]
    gram = [sum(f * t for f, t in zip(double, take[at : at + 6])) for at in range(6, 36, 6)]
    at = 36
    energy = sum(f * t for f, t in zip(double, take[at : at + 6]))
    outer = galerkin(gram, energy)
    factors = list(coef) + [d * c for d in outer for c in coef]

    second = factors[0] * fields_ref[0] + factors[1] * fields_ref[1] + factors[2] * fields_ref[2]
    second_ref[...] = second.reshape(second_ref.shape)
    first = factors[3] * fields_ref[3]
    for i in range(4, 12):
        first = first + factors[i] * fields_ref[i]
    first_ref[...] = first.reshape(first_ref.shape)

    per_line = 12 // (lines - 1)
    cells = span // per_line
    row = lax.broadcasted_iota(jnp.int32, (span, span), 0)
    for step in range(2):
        holder = (owner_ref[step : step + 1, :] == lax.broadcasted_iota(jnp.int32, (devices, span), 0)).astype(F32)
        here = place_ref[step : step + 1, :] == row % cells
        result = jnp.zeros((1, span), F32)
        for line in range(lines - 1):
            fields = [f for f in range(line * per_line, (line + 1) * per_line) if (f >= 3) == (step == 0)]
            if not fields:
                continue
            picked = lax.dot_general(info_ref[:, line, :], holder, contract, precision=HIGHEST, preferred_element_type=F32)
            picked = jnp.where(here, picked, 0.0)
            for f in fields:
                lo = (f - line * per_line) * cells
                result = result + factors[f] * jnp.sum(picked[lo : lo + cells], axis=0, keepdims=True)
        grad_ref[step : step + 1, :] = result


def per_device(counts, cotangent, conductivity, capacity, sources):
    height, plane = counts
    depth, _, span = cotangent.shape
    elems = depth // 8
    cells = span // 8
    groups = plane // GROUP
    devices = height * plane
    vmem = pl.BlockSpec(memory_space=pltpu.VMEM)

    rows = depth * 8 + coef_rows(elems)
    lines = jnp.concatenate([conductivity, capacity], axis=1).reshape(elems * 2, cells)
    lines = jnp.pad(lines, ((0, rows - depth * 8 - 2 * elems), (0, span - cells)))
    raw = jnp.concatenate([cotangent.reshape(depth * 8, span), lines], axis=0)
    message = pl.pallas_call(
        functools.partial(pack_kernel, (depth, elems, cells)),
        out_shape=jax.ShapeDtypeStruct((rows, span), F32),
        in_specs=[vmem],
        out_specs=vmem,
        compiler_params=pltpu.CompilerParams(vmem_limit_bytes=4 * 2**20),
    )(raw)

    def move(value, pairs):
        return lax.ppermute(value, "plane", pairs) if pairs else jnp.zeros_like(value)

    def both_ways(pairs):
        return [*pairs, *((b, a) for a, b in pairs)]

    def shift(gap, moving):
        return [(g * GROUP + m, (g + gap) * GROUP + m) for g in range(groups) for m in moving if 0 <= g + gap < groups]

    half = jnp.concatenate([message, move(message, [(p, p ^ 1) for p in range(plane)])], axis=0)
    every = range(GROUP)
    pair = move(half, both_ways([(a, b) for a, b in shift(1, every) if (a // GROUP) % 2 == 0]))
    cross = move(half, both_ways([(a, b) for a, b in shift(1, every) if (a // GROUP) % 2 == 1]))
    other = move(half, [(p, p ^ 2) for p in range(plane)])
    side = move(other, shift(1, (0, 1)) + shift(-1, (2, 3)))
    edge = pl.pallas_call(
        functools.partial(edge_kernel, depth),
        out_shape=jax.ShapeDtypeStruct((rows - depth * 7, span), F32),
        in_specs=[vmem],
        out_specs=vmem,
        compiler_params=pltpu.CompilerParams(vmem_limit_bytes=4 * 2**20),
    )(other)
    edge = move(edge, shift(2, (0,)) + shift(-1, (1,)) + shift(1, (2,)) + shift(-2, (3,)))
    lone = pl.pallas_call(
        functools.partial(widen_kernel, depth),
        out_shape=jax.ShapeDtypeStruct((rows, span), F32),
        in_specs=[vmem],
        out_specs=vmem,
        cost_estimate=pl.CostEstimate(flops=1000000, bytes_accessed=1000000, transcendentals=0),
        compiler_params=pltpu.CompilerParams(vmem_limit_bytes=4 * 2**20),
    )(edge)
    sent = (half, other, pair, cross, side, lone)
    operands = list(sent)
    for turn in range(1, height):
        operands += [lax.ppermute(arr, "height", [(h, (h + turn) % height) for h in range(height)]) for arr in sent]

    lay = Layout(elems * height > 4)
    consts = tables(span)
    slots = 3 * GROUP + 2
    slab_bytes = 4 * depth * 8 * height * span
    fields, info = pl.pallas_call(
        functools.partial(basis_kernel, counts),
        out_shape=(jax.ShapeDtypeStruct((12, depth * 8, span), F32), jax.ShapeDtypeStruct((devices, 12 * elems * cells // span + 1, span), F32)),
        in_specs=[vmem] * (len(operands) + len(consts)),
        out_specs=(vmem, vmem),
        scratch_shapes=[
            pltpu.VMEM((lay.total, depth * 8 * height, span), F32),
            pltpu.VMEM((slots, depth * 8 * height, span), F32),
            pltpu.VMEM((slots, 2, elems * height, 8, span), F32),
            pltpu.VMEM((depth * 8, span), F32),
        ],
        compiler_params=pltpu.CompilerParams(vmem_limit_bytes=(lay.total + 3 * slots + 14) * slab_bytes + 12 * 2**20),
    )(*operands, *[jnp.asarray(c) for c in consts])

    shared = lax.all_to_all(info, ("height", "plane"), 0, 0, tiled=True)

    cell = sources % cells
    column = sources // cells
    wide_elem = column % plane
    deep_elem = column // plane
    owner = (deep_elem // elems) * plane + wide_elem
    place = (deep_elem % elems) * cells + cell
    return pl.pallas_call(
        combine_kernel,
        out_shape=(
            jax.ShapeDtypeStruct(cotangent.shape, F32),
            jax.ShapeDtypeStruct(cotangent.shape, F32),
            jax.ShapeDtypeStruct(sources.shape, F32),
        ),
        in_specs=[vmem] * 4,
        out_specs=(vmem, vmem, vmem),
        compiler_params=pltpu.CompilerParams(vmem_limit_bytes=8 * 2**20),
    )(shared, fields, owner, place)


def solution(mesh):
    counts = (mesh.shape["height"], mesh.shape["plane"])
    field = P("height", "plane", None)
    return jax.shard_map(
        functools.partial(per_device, counts),
        mesh=mesh,
        in_specs=(field, field, field, P()),
        out_specs=(field, field, P()),
        check_vma=False,
    )
```

```python
import functools

import jax
import jax.numpy as jnp
import ml_dtypes
import numpy as np
from jax import lax
from jax.experimental import pallas as pl
from jax.experimental.pallas import tpu as pltpu
from jax.sharding import PartitionSpec as P

INV_STEP = 20.0
SHIFTS = (0.5, 1.5)
GROUP = 4
REACH = 4
PAIRS = ((0, 0), (0, 1), (0, 2), (1, 1), (1, 2), (2, 2))
BANDS = ((0, 0), (0, 1), (1, 1), (1, 2), (2, 2))
TINY = 1e-30
HIGHEST = lax.Precision.HIGHEST
F32 = jnp.float32
BF16 = jnp.bfloat16


def gll_tables():
    points = np.array([-1.0, -0.8717401485096066, -0.5917001814331423, -0.2092992179024789, 0.2092992179024789, 0.5917001814331423, 0.8717401485096066, 1.0])
    weights = np.array([1.0 / 28.0, 0.2107042271435061, 0.3411226924835044, 0.4124587946587038, 0.4124587946587038, 0.3411226924835044, 0.2107042271435061, 1.0 / 28.0])
    product = np.array([np.prod([points[col] - points[others] for others in range(8) if others != col]) for col in range(8)])
    derivative = np.zeros((8, 8))
    for row in range(8):
        for col in range(8):
            if row != col:
                derivative[row, col] = product[row] / (product[col] * (points[row] - points[col]))
        derivative[row, row] = -np.sum(derivative[row])
    return derivative, weights, np.sum(derivative**2 * weights[:, None], axis=0)


def pieces(matrix):
    out, rest = [], matrix
    for _ in range(3):
        piece = rest.astype(ml_dtypes.bfloat16)
        out.append(piece)
        rest = rest - piece.astype(np.float64)
    return out


def tables(span):
    derivative, weights, stiff = gll_tables()
    line = (derivative.T * weights) @ derivative / weights[:, None]
    eye = np.eye(8)
    face = pieces(np.kron(line, eye) + np.kron(eye, line))
    face_mat = np.concatenate([np.concatenate([piece, piece], axis=1) for piece in face], axis=0)
    ends_mat = np.concatenate([np.concatenate([p[0::8], p[7::8]], axis=0) for p in np.split(face_mat, 3)], axis=0)
    row = pieces(np.kron(np.eye(span // 8), line.T))
    row_a = np.concatenate([np.concatenate([row[0], row[1]], 1)] * 2, axis=0)
    none = np.zeros_like(row[2])
    row_b = np.concatenate([np.concatenate([row[2], none], 1), np.concatenate([none, row[2]], 1)], axis=0)
    tile = np.tile(weights, span // 8)
    ratio = stiff / weights
    omega = weights[:, None, None] * weights[None, :, None] * tile[None, None, :]
    quot = ratio[:, None, None] + ratio[None, :, None] + np.tile(ratio, span // 8)[None, None, :]
    return face_mat, ends_mat, row_a, row_b, omega.astype(np.float32), quot.astype(np.float32)


def coef_rows(elems):
    return -(-(2 * elems) // 8) * 8


def seams(span):
    lane = lax.broadcasted_iota(jnp.int32, (8, span), 1)
    return (lane % 8 == 0) & (lane > 0), (lane % 8 == 7) & (lane < span - 1)


def tall(mask, like):
    return jnp.concatenate([mask] * (like.shape[0] // 8), axis=0) if like.shape[0] > 8 else mask


def join_span(values):
    span = values.shape[1]
    opens, closes = seams(span)
    up, down = pltpu.roll(values, 1, 1), pltpu.roll(values, span - 1, 1)
    return values + jnp.where(tall(opens, values), up, jnp.where(tall(closes, values), down, 0.0))


def join_depth(values):
    planes = []
    layers = values.shape[0] // 64
    for elem in range(layers):
        top = elem * 64
        first, last = values[top : top + 8], values[top + 56 : top + 64]
        if elem > 0:
            first = first + values[top - 8 : top]
        if elem < layers - 1:
            last = last + values[top + 64 : top + 72]
        planes += [first, values[top + 8 : top + 56], last]
    return jnp.concatenate(planes, axis=0)


def pack_kernel(shape, raw_ref, out_ref):
    depth, elems, parts = shape
    span = raw_ref.shape[1]
    spread = (lax.broadcasted_iota(jnp.int32, (parts, span), 1) // 8 == lax.broadcasted_iota(jnp.int32, (parts, span), 0)).astype(F32)
    coef = raw_ref[depth * 8 :, :parts]
    pair = [coef[2 * e : 2 * e + 1] * (1.0 / INV_STEP) for e in range(elems)] + [coef[2 * e + 1 : 2 * e + 2] for e in range(elems)]
    coef = jnp.concatenate([*pair, coef[2 * elems :]], axis=0)
    coef = jnp.dot(coef, spread, precision=HIGHEST, preferred_element_type=F32)
    heavy = jnp.concatenate([jnp.broadcast_to(coef[elems + e : elems + e + 1], (64, span)) for e in range(elems)], axis=0)
    value = join_depth(join_span(heavy * raw_ref[: depth * 8, :]))
    out_ref[: depth * 8, :] = value
    out_ref[depth * 8 :, :] = coef


def edge_kernel(depth, msg_ref, out_ref):
    rows = msg_ref.shape[0] // 2
    low, high = (msg_ref[pl.ds(rows + node, depth, stride=8), :] for node in (0, 7))
    out_ref[:depth] = jnp.where(lax.rem(lax.axis_index("plane"), 2) == 0, high, low)
    out_ref[depth:] = msg_ref[rows + depth * 8 :, :]


def widen_kernel(depth, edge_ref, out_ref):
    span = edge_ref.shape[1]
    out_ref[: depth * 8] = jnp.concatenate([jnp.broadcast_to(edge_ref[z : z + 1, :], (8, span)) for z in range(depth)], axis=0)
    out_ref[depth * 8 :] = edge_ref[depth:, :]


class Layout:
    def __init__(self, tall):
        wide = 2 * REACH + 1
        self.wide = wide
        self.at_once = 1 if tall else 3
        self.sums = 0
        self.minv = max(wide, 5 * self.at_once)
        self.ratio = self.minv + wide
        self.basis = self.ratio + 5
        self.second = self.basis + 3 * wide
        self.total = self.second + wide * self.at_once


def basis_kernel(counts, *refs):
    height, plane = counts
    n_in = 5 * height
    msgs = refs[:n_in]
    face_ref, ends_ref, row_a_ref, row_b_ref, omega_ref, quot_ref = refs[n_in : n_in + 6]
    fields_ref, info_ref = refs[n_in + 6 : n_in + 8]
    pool, raw, coef, weigh = refs[n_in + 8 :]
    rows, span = pool.shape[1:]
    depth = rows // 8
    own_depth = depth // height
    own_rows = own_depth * 8
    elems = depth // 8
    own_elems = elems // height
    height_pos = lax.axis_index("height")
    plane_pos = lax.axis_index("plane")
    member = lax.rem(plane_pos, GROUP)
    even = lax.rem(plane_pos // GROUP, 2) == 0
    slab_rows = own_rows + coef_rows(own_elems)
    whole = elems > 4
    lay = Layout(whole)
    wide = lay.wide

    sub = lax.broadcasted_iota(jnp.int32, (8, span), 0)
    opens, closes = seams(span)

    def stage(msg, piece, slot, block):
        top = piece * slab_rows
        raw[slot, pl.ds(pl.multiple_of(block * own_rows, own_rows), own_rows)] = msg[top : top + own_rows, :]
        for kind in range(2):
            for elem in range(own_elems):
                at = top + own_rows + kind * own_elems + elem
                coef[slot, kind, block * own_elems + elem] = jnp.broadcast_to(msg[at : at + 1, :], (8, span))

    before, here, after = 1, 1 + GROUP, 1 + 2 * GROUP
    early = member < GROUP // 2
    lone = jnp.where(
        early,
        jnp.where(member == 0, 0, after + jnp.bitwise_xor(member, 3)),
        jnp.where(member == GROUP - 1, 3 * GROUP + 1, before + jnp.bitwise_xor(member, 3)),
    )
    def slots(base, flips):
        return [base + jnp.bitwise_xor(member, flip) for flip in flips]

    roles = (
        slots(here, (0, 1)),
        slots(here, (2, 3)),
        slots(jnp.where(even, after, before), (0, 1)),
        slots(jnp.where(even, before, after), (0, 1)),
        [*slots(jnp.where(early, before, after), (2, 3)), lone],
    )
    for turn in range(height):
        block = lax.rem(height_pos - turn + height, height)
        for msg, places in zip(msgs[turn * len(roles) :], roles):
            for piece, slot in enumerate(places):
                stage(msg, piece, slot, block)

    def face_at(slot, width_node):
        return slot, pl.ds(width_node, depth, stride=8)

    def join_width(store, slot):
        low, high = face_at(slot, 7), face_at(slot + 1, 0)
        both = store[low] + store[high]
        store[low] = both
        store[high] = both

    def loop(start, stop, body, step=1):
        if whole:
            lax.fori_loop(start, stop, lambda at, carry: (body([at]), carry)[1], 0)
        else:
            for at in range(start, stop, step):
                body(list(range(at, min(at + step, stop))))

    def each(body):
        return lambda slabs: [body(at) for at in slabs]

    def split(values):
        one = values.astype(BF16)
        return one, (values - one.astype(F32)).astype(BF16)

    def along_span(halves):
        wides = [jnp.dot(jnp.concatenate(h, axis=1), row_a_ref[...], preferred_element_type=F32) for h in halves]
        if len(halves) == 2:
            extra = jnp.dot(jnp.concatenate([halves[0][0], halves[1][0]], axis=1), row_b_ref[...], preferred_element_type=F32)
            extras = [extra[:, :span], extra[:, span:]]
        else:
            extras = [jnp.dot(halves[0][0], row_b_ref[:span, :span], preferred_element_type=F32)]
        return [(w[:, :span] + w[:, span:]) + x for w, x in zip(wides, extras)]

    def along_face(matrix, halves, elem):
        top = elem * 64
        stacks = [jnp.concatenate([piece[top : top + 64] for piece in h], axis=0) for h in halves]
        made = jnp.dot(matrix, stacks[0] if len(stacks) == 1 else jnp.concatenate(stacks, axis=1), preferred_element_type=F32)
        count = made.shape[0] // 3
        return made[:count] + (made[count : 2 * count] + made[2 * count :])

    def scaled(slot, kind, elem, scale):
        value = coef[slot, kind, elem]
        return value if scale == 1.0 else value * scale

    def operator(fields, slots, scale=1.0, start=0):
        halves = [split(v) for v in fields]
        lines = along_span(halves)
        out = [[] for _ in fields]
        for elem in range(fields[0].shape[0] // 64):
            top = elem * 64
            face = along_face(face_ref[...], halves, elem)
            for i, v in enumerate(fields):
                cap = tall(scaled(slots[i], 1, start + elem, scale), face)
                kap = tall(scaled(slots[i], 0, start + elem, scale), face)
                lin = lines[i][top : top + 64] + face[:, i * span : (i + 1) * span]
                out[i].append(cap * v[top : top + 64] + kap * lin)
        return [jnp.concatenate(o, axis=0) for o in out]

    def ends(sources, targets, at, scale):
        halves = [split(pool[s]) for s in sources]
        edges = [pool[s, pl.ds(node, depth, stride=8)] for s, node in zip(sources, (7, 0))]
        lines = along_span([split(jnp.concatenate(edges, axis=0))])[0]
        both = [along_face(ends_ref[...], halves, elem) for elem in range(elems)]
        for i in range(2):
            joined = []
            for elem in range(elems):
                lin = lines[i * depth + elem * 8 : i * depth + elem * 8 + 8] + both[elem][8 * (1 - i) : 8 * (2 - i), i * span : (i + 1) * span]
                slot = member + at[i]
                joined.append(join_span(scaled(slot, 1, elem, scale) * edges[i][elem * 8 : elem * 8 + 8] + scaled(slot, 0, elem, scale) * lin))
            final = []
            for elem in range(elems):
                value = joined[elem]
                if elem > 0:
                    value = value + jnp.where(sub == 0, pltpu.roll(joined[elem - 1], 1, 0), 0.0)
                if elem < elems - 1:
                    value = value + jnp.where(sub == 7, pltpu.roll(joined[elem + 1], 7, 0), 0.0)
                final.append(value)
            pool[face_at(targets[i], (7, 0)[i])] = jnp.concatenate(final, axis=0)

    def step(chains, low, high, shift):
        def apply(work):
            made = operator([pool[here + at] for here, _, at in work], [member + at for _, _, at in work], 1.0 / shift)
            for (_, sums, at), value in zip(work, made):
                pool[sums + at] = join_depth(join_span(value))

        if whole:
            for here, sums, after in chains:
                loop(low + 1, high, each(lambda at: apply([(here, sums, at)])))
        else:
            work = [(here, sums, at) for here, sums, _ in chains for at in range(low + 1, high)]
            for first in range(0, len(work), 2):
                apply(work[first : first + 2])
        for here, sums, _ in chains:
            ends((here + low, here + high), (sums + low, sums + high), (low, high), 1.0 / shift)
        for here, sums, after in chains:
            loop(low, high, each(lambda at: join_width(pool, sums + at)))

            def advance(at):
                pool[after + at] = pool[lay.minv + at - 1] * pool[sums + at] - pool[here + at]

            loop(low + 1, high, each(advance))

    def constant(kind, at):
        layers = [[join_span(coef[member + at + side, kind, elem]) for elem in range(elems)] for side in (-1, 0, 1)]
        wide_sum = lambda low, mid, high: mid + jnp.where(sub == 0, low, jnp.where(sub == 7, high, 0.0))
        inside = [wide_sum(*(layers[side][elem] for side in range(3))) for elem in range(elems)]
        planes = []
        for elem in range(elems):
            first = inside[elem] if elem == 0 else inside[elem] + inside[elem - 1]
            last = inside[elem] if elem == elems - 1 else inside[elem] + inside[elem + 1]
            planes += [first] + [inside[elem]] * 6 + [last]
        return jnp.concatenate(planes, axis=0)

    def inverse_slab(at):
        quot = jnp.concatenate([quot_ref[...].reshape(64, span)] * elems, axis=0)
        mass = constant(1, at)
        inverse = 1.0 / jnp.maximum(mass + quot * constant(0, at), TINY)
        pool[lay.minv + at - 1] = inverse
        return inverse, mass

    def first_slab(at):
        inverse, _ = inverse_slab(at)
        pool[lay.basis + at - 1] = inverse * raw[member + at]

    def inner_slab(at):
        inverse, mass = inverse_slab(at)
        pool[lay.basis + at - 1] = inverse * raw[member + at]
        pool[lay.ratio + at - 3] = inverse * mass

    def join_blocks(slot):
        for block in range(1, height):
            low, high = pl.ds(block * own_rows - 8, 8), pl.ds(block * own_rows, 8)
            both = raw[slot, low] + raw[slot, high]
            raw[slot, low] = both
            raw[slot, high] = both

    loop(0, wide + 2, each(lambda at: join_blocks(member + at)))
    loop(0, wide + 1, each(lambda at: join_width(raw, member + at)))
    loop(1, 3, each(first_slab))
    loop(3, wide - 1, each(inner_slab))
    loop(wide - 1, wide + 1, each(first_slab))

    mid = REACH + 1

    def own(slot):
        value = pool[slot, :own_rows]
        for block in range(1, height):
            value = jnp.where(height_pos == block, pool[slot, block * own_rows : (block + 1) * own_rows], value)
        return value

    shape = (own_depth, 8, span)
    zpos = lax.broadcasted_iota(jnp.int32, shape, 0) + height_pos * own_depth
    xpos = lax.broadcasted_iota(jnp.int32, shape, 1) + plane_pos * 8

    def copies(pos, extent):
        return jnp.where(((pos % 8 == 7) & (pos < extent - 1)) | ((pos % 8 == 0) & (pos > 0)), 0.5, 1.0)

    share = copies(zpos, depth) * copies(xpos, plane * 8) * jnp.where(opens | closes, 0.5, 1.0)
    omega = jnp.concatenate([omega_ref[...].reshape(64, span)] * own_elems, axis=0)
    weigh[...] = share.reshape(own_rows, span) * omega / own(lay.minv + REACH)

    for level in range(2):
        step([(lay.basis + level * wide - 1, lay.sums - 1, lay.basis + (level + 1) * wide - 1)], 1 + level, wide - level, SHIFTS[level])
    for vec in range(3):
        fields_ref[vec] = own(lay.basis + vec * wide + REACH)

    def second(vecs):
        homes = [lay.second + wide * i for i in range(lay.at_once)]
        sums = [lay.sums + 5 * i - 3 for i in range(lay.at_once)]
        for vec, home in zip(vecs, homes):

            def begin(at):
                pool[home + at - 3] = pool[lay.ratio + at - 3] * pool[lay.basis + vec * wide + at - 1]

            loop(3, 8, each(begin))
        step([(h - 3, t, h + 1) for h, t in zip(homes, sums)], 3, 7, SHIFTS[0])
        step([(h + 1, t, h + 3) for h, t in zip(homes, sums)], 4, 6, SHIFTS[1])
        for vec, home in zip(vecs, homes):
            for level, slot in enumerate((2, 6, 8)):
                fields_ref[3 + 3 * level + vec] = own(home + slot)

    if lay.at_once == 3:
        second([0, 1, 2])
    else:
        loop(0, 3, each(lambda vec: second([vec])))

    slot = member + mid
    start = height_pos * own_elems

    def total(values):
        return jnp.sum(values.reshape(shape), axis=0)

    parts = []
    left = [weigh[...] * fields_ref[i] for i in range(3)]
    parts += [total(left[i] * fields_ref[j]) for i, j in BANDS]
    lasts = (2, 9, 10, 11)
    energy = []
    for k in (0, 2):
        energy += operator([fields_ref[i] for i in lasts[k : k + 2]], [slot] * 2, 1.0, start)
    energy = [omega * e for e in energy]
    parts.append(total(fields_ref[2] * energy[0]))
    for k, l in BANDS:
        left = [weigh[...] * fields_ref[3 + 3 * k + i] for i in range(3)]
        parts += [total(left[i] * fields_ref[3 + 3 * l + j]) for i, j in PAIRS]
    parts += [total(fields_ref[9 + i] * energy[1 + j]) for i, j in PAIRS]
    lines = [jnp.sum(part, axis=0, keepdims=True) for part in parts]
    lines.append(jnp.zeros((span - len(lines), span), F32))
    sums = lax.dot_general(jnp.ones((8, span), F32), jnp.concatenate(lines, axis=0), (((1,), (1,)), ((), ())), precision=HIGHEST, preferred_element_type=F32)

    heavy = jnp.concatenate([jnp.concatenate([coef[slot, 1, start + elem]] * 8, axis=0) for elem in range(own_elems)], axis=0) * (omega * 0.125)
    rows_of = []
    for index in range(12):
        mass = heavy * fields_ref[index]
        for elem in range(own_elems):
            rows_of.append(jnp.sum(mass[elem * 64 : elem * 64 + 64], axis=0, keepdims=True))
    stack = jnp.concatenate(rows_of, axis=0)
    cells = span // 8
    per_row = span // cells
    spread = (lax.broadcasted_iota(jnp.int32, (span, span), 0) // 8 == lax.broadcasted_iota(jnp.int32, (span, span), 1) % cells).astype(F32)
    stack = jnp.dot(stack, spread, precision=HIGHEST, preferred_element_type=F32)
    place = lax.broadcasted_iota(jnp.int32, stack.shape, 0) % per_row == lax.broadcasted_iota(jnp.int32, stack.shape, 1) // cells
    stack = jnp.where(place, stack, 0.0).reshape(stack.shape[0] // per_row, per_row, span)
    info = jnp.concatenate([jnp.sum(stack, axis=1), sums[:1]], axis=0)
    info_ref[...] = jnp.broadcast_to(info[None], info_ref.shape)


def galerkin(gram, energy):
    n00, n01, n11, n12, n22 = gram
    first, later = SHIFTS
    n02 = (first / later) * (n11 + n01) - n01
    h00, h01, h02 = first * (n01 + n00), first * (n11 + n01), first * (n12 + n02)
    h11, h12 = later * (n12 + n11), later * (n22 + n12)
    low10, low20 = h01 / h00, h02 / h00
    piv1 = h11 - low10 * h01
    off12 = h12 - low10 * h02
    low21 = off12 / piv1
    piv2 = energy - low20 * h02 - low21 * off12
    y0 = n00
    y1 = n01 - low10 * y0
    y2 = n02 - low20 * y0 - low21 * y1
    c2 = y2 / piv2
    c1 = y1 / piv1 - low21 * c2
    c0 = y0 / h00 - low10 * c1 - low20 * c2
    return c0, c1, c2


def combine_kernel(info_ref, fields_ref, owner_ref, place_ref, second_ref, first_ref, grad_ref):
    devices, lines, span = info_ref.shape
    ones = jnp.ones((devices, span), F32)
    contract = (((0,), (0,)), ((), ()))
    wide = lax.dot_general(info_ref[:, lines - 1, :], ones, contract, precision=HIGHEST, preferred_element_type=F32)
    take = [wide[i : i + 1, :] for i in range(6 + 30 + 6)]
    coef = galerkin(take[:5], take[5])
    double = [(2.0 if i != j else 1.0) * coef[i] * coef[j] for i, j in PAIRS]
    gram = [sum(f * t for f, t in zip(double, take[at : at + 6])) for at in range(6, 36, 6)]
    at = 36
    energy = sum(f * t for f, t in zip(double, take[at : at + 6]))
    outer = galerkin(gram, energy)
    factors = list(coef) + [d * c for d in outer for c in coef]

    second = factors[0] * fields_ref[0] + factors[1] * fields_ref[1] + factors[2] * fields_ref[2]
    second_ref[...] = second.reshape(second_ref.shape)
    first = factors[3] * fields_ref[3]
    for i in range(4, 12):
        first = first + factors[i] * fields_ref[i]
    first_ref[...] = first.reshape(first_ref.shape)

    per_line = 12 // (lines - 1)
    cells = span // per_line
    row = lax.broadcasted_iota(jnp.int32, (span, span), 0)
    for step in range(2):
        holder = (owner_ref[step : step + 1, :] == lax.broadcasted_iota(jnp.int32, (devices, span), 0)).astype(F32)
        here = place_ref[step : step + 1, :] == row % cells
        result = jnp.zeros((1, span), F32)
        for line in range(lines - 1):
            fields = [f for f in range(line * per_line, (line + 1) * per_line) if (f >= 3) == (step == 0)]
            if not fields:
                continue
            picked = lax.dot_general(info_ref[:, line, :], holder, contract, precision=HIGHEST, preferred_element_type=F32)
            picked = jnp.where(here, picked, 0.0)
            for f in fields:
                lo = (f - line * per_line) * cells
                result = result + factors[f] * jnp.sum(picked[lo : lo + cells], axis=0, keepdims=True)
        grad_ref[step : step + 1, :] = result


def per_device(counts, cotangent, conductivity, capacity, sources):
    height, plane = counts
    depth, _, span = cotangent.shape
    elems = depth // 8
    cells = span // 8
    groups = plane // GROUP
    devices = height * plane
    vmem = pl.BlockSpec(memory_space=pltpu.VMEM)

    rows = depth * 8 + coef_rows(elems)
    lines = jnp.concatenate([conductivity, capacity], axis=1).reshape(elems * 2, cells)
    lines = jnp.pad(lines, ((0, rows - depth * 8 - 2 * elems), (0, span - cells)))
    raw = jnp.concatenate([cotangent.reshape(depth * 8, span), lines], axis=0)
    message = pl.pallas_call(
        functools.partial(pack_kernel, (depth, elems, cells)),
        out_shape=jax.ShapeDtypeStruct((rows, span), F32),
        in_specs=[vmem],
        out_specs=vmem,
        compiler_params=pltpu.CompilerParams(vmem_limit_bytes=4 * 2**20),
    )(raw)

    def move(value, pairs):
        return lax.ppermute(value, "plane", pairs) if pairs else jnp.zeros_like(value)

    def both_ways(pairs):
        return [*pairs, *((b, a) for a, b in pairs)]

    def shift(gap, moving):
        return [(g * GROUP + m, (g + gap) * GROUP + m) for g in range(groups) for m in moving if 0 <= g + gap < groups]

    half = jnp.concatenate([message, move(message, [(p, p ^ 1) for p in range(plane)])], axis=0)
    every = range(GROUP)
    pair = move(half, both_ways([(a, b) for a, b in shift(1, every) if (a // GROUP) % 2 == 0]))
    cross = move(half, both_ways([(a, b) for a, b in shift(1, every) if (a // GROUP) % 2 == 1]))
    other = move(half, [(p, p ^ 2) for p in range(plane)])
    side = move(other, shift(1, (0, 1)) + shift(-1, (2, 3)))
    edge = pl.pallas_call(
        functools.partial(edge_kernel, depth),
        out_shape=jax.ShapeDtypeStruct((rows - depth * 7, span), F32),
        in_specs=[vmem],
        out_specs=vmem,
        compiler_params=pltpu.CompilerParams(vmem_limit_bytes=4 * 2**20),
    )(other)
    edge = move(edge, shift(2, (0,)) + shift(-1, (1,)) + shift(1, (2,)) + shift(-2, (3,)))
    lone = pl.pallas_call(
        functools.partial(widen_kernel, depth),
        out_shape=jax.ShapeDtypeStruct((rows, span), F32),
        in_specs=[vmem],
        out_specs=vmem,
        cost_estimate=pl.CostEstimate(flops=100000000, bytes_accessed=3000000, transcendentals=0),
        compiler_params=pltpu.CompilerParams(vmem_limit_bytes=4 * 2**20),
    )(edge)
    sent = (half, other, pair, cross, jnp.concatenate([side, lone], axis=0))
    operands = list(sent)
    for turn in range(1, height):
        operands += [lax.ppermute(arr, "height", [(h, (h + turn) % height) for h in range(height)]) for arr in sent]

    lay = Layout(elems * height > 4)
    consts = tables(span)
    slots = 3 * GROUP + 2
    slab_bytes = 4 * depth * 8 * height * span
    fields, info = pl.pallas_call(
        functools.partial(basis_kernel, counts),
        out_shape=(jax.ShapeDtypeStruct((12, depth * 8, span), F32), jax.ShapeDtypeStruct((devices, 12 * elems * cells // span + 1, span), F32)),
        in_specs=[vmem] * (len(operands) + len(consts)),
        out_specs=(vmem, vmem),
        scratch_shapes=[
            pltpu.VMEM((lay.total, depth * 8 * height, span), F32),
            pltpu.VMEM((slots, depth * 8 * height, span), F32),
            pltpu.VMEM((slots, 2, elems * height, 8, span), F32),
            pltpu.VMEM((depth * 8, span), F32),
        ],
        compiler_params=pltpu.CompilerParams(vmem_limit_bytes=(lay.total + 3 * slots + 14) * slab_bytes + 12 * 2**20),
    )(*operands, *[jnp.asarray(c) for c in consts])

    shared = lax.all_to_all(info, ("height", "plane"), 0, 0, tiled=True)

    cell = sources % cells
    column = sources // cells
    wide_elem = column % plane
    deep_elem = column // plane
    owner = (deep_elem // elems) * plane + wide_elem
    place = (deep_elem % elems) * cells + cell
    return pl.pallas_call(
        combine_kernel,
        out_shape=(
            jax.ShapeDtypeStruct(cotangent.shape, F32),
            jax.ShapeDtypeStruct(cotangent.shape, F32),
            jax.ShapeDtypeStruct(sources.shape, F32),
        ),
        in_specs=[vmem] * 4,
        out_specs=(vmem, vmem, vmem),
        compiler_params=pltpu.CompilerParams(vmem_limit_bytes=8 * 2**20),
    )(shared, fields, owner, place)


def solution(mesh):
    counts = (mesh.shape["height"], mesh.shape["plane"])
    field = P("height", "plane", None)
    return jax.shard_map(
        functools.partial(per_device, counts),
        mesh=mesh,
        in_specs=(field, field, field, P()),
        out_specs=(field, field, P()),
        check_vma=False,
    )
```

```python
import functools

import jax
import jax.numpy as jnp
import ml_dtypes
import numpy as np
from jax import lax
from jax.experimental import pallas as pl
from jax.experimental.pallas import tpu as pltpu
from jax.sharding import PartitionSpec as P

INV_STEP = 20.0
SHIFTS = (0.5, 1.5)
GROUP = 4
REACH = 4
PAIRS = ((0, 0), (0, 1), (0, 2), (1, 1), (1, 2), (2, 2))
BANDS = ((0, 0), (0, 1), (1, 1), (1, 2), (2, 2))
TINY = 1e-30
HIGHEST = lax.Precision.HIGHEST
F32 = jnp.float32
BF16 = jnp.bfloat16


def gll_tables():
    points = np.array([-1.0, -0.8717401485096066, -0.5917001814331423, -0.2092992179024789, 0.2092992179024789, 0.5917001814331423, 0.8717401485096066, 1.0])
    weights = np.array([1.0 / 28.0, 0.2107042271435061, 0.3411226924835044, 0.4124587946587038, 0.4124587946587038, 0.3411226924835044, 0.2107042271435061, 1.0 / 28.0])
    product = np.array([np.prod([points[col] - points[others] for others in range(8) if others != col]) for col in range(8)])
    derivative = np.zeros((8, 8))
    for row in range(8):
        for col in range(8):
            if row != col:
                derivative[row, col] = product[row] / (product[col] * (points[row] - points[col]))
        derivative[row, row] = -np.sum(derivative[row])
    return derivative, weights, np.sum(derivative**2 * weights[:, None], axis=0)


def pieces(matrix):
    out, rest = [], matrix
    for _ in range(3):
        piece = rest.astype(ml_dtypes.bfloat16)
        out.append(piece)
        rest = rest - piece.astype(np.float64)
    return out


def tables(span):
    derivative, weights, stiff = gll_tables()
    line = (derivative.T * weights) @ derivative / weights[:, None]
    eye = np.eye(8)
    face = pieces(np.kron(line, eye) + np.kron(eye, line))
    face_mat = np.concatenate([np.concatenate([piece, piece], axis=1) for piece in face], axis=0)
    ends_mat = np.concatenate([np.concatenate([p[0::8], p[7::8]], axis=0) for p in np.split(face_mat, 3)], axis=0)
    row = pieces(np.kron(np.eye(span // 8), line.T))
    row_a = np.concatenate([np.concatenate([row[0], row[1]], 1)] * 2, axis=0)
    none = np.zeros_like(row[2])
    row_b = np.concatenate([np.concatenate([row[2], none], 1), np.concatenate([none, row[2]], 1)], axis=0)
    tile = np.tile(weights, span // 8)
    ratio = stiff / weights
    omega = weights[:, None, None] * weights[None, :, None] * tile[None, None, :]
    quot = ratio[:, None, None] + ratio[None, :, None] + np.tile(ratio, span // 8)[None, None, :]
    return face_mat, ends_mat, row_a, row_b, omega.astype(np.float32), quot.astype(np.float32)


def coef_rows(elems):
    return -(-(2 * elems) // 8) * 8


def seams(span):
    lane = lax.broadcasted_iota(jnp.int32, (8, span), 1)
    return (lane % 8 == 0) & (lane > 0), (lane % 8 == 7) & (lane < span - 1)


def tall(mask, like):
    return jnp.concatenate([mask] * (like.shape[0] // 8), axis=0) if like.shape[0] > 8 else mask


def join_span(values):
    span = values.shape[1]
    opens, closes = seams(span)
    up, down = pltpu.roll(values, 1, 1), pltpu.roll(values, span - 1, 1)
    return values + jnp.where(tall(opens, values), up, jnp.where(tall(closes, values), down, 0.0))


def join_depth(values):
    planes = []
    layers = values.shape[0] // 64
    for elem in range(layers):
        top = elem * 64
        first, last = values[top : top + 8], values[top + 56 : top + 64]
        if elem > 0:
            first = first + values[top - 8 : top]
        if elem < layers - 1:
            last = last + values[top + 64 : top + 72]
        planes += [first, values[top + 8 : top + 56], last]
    return jnp.concatenate(planes, axis=0)


def pack_kernel(shape, cot_ref, lines_ref, out_ref):
    depth, elems, parts = shape
    span = lines_ref.shape[1]
    spread = (lax.broadcasted_iota(jnp.int32, (parts, span), 1) // 8 == lax.broadcasted_iota(jnp.int32, (parts, span), 0)).astype(F32)
    coef = lines_ref[:, :parts]
    pair = [coef[2 * e : 2 * e + 1] * (1.0 / INV_STEP) for e in range(elems)] + [coef[2 * e + 1 : 2 * e + 2] for e in range(elems)]
    coef = jnp.concatenate([*pair, coef[2 * elems :]], axis=0)
    coef = jnp.dot(coef, spread, precision=HIGHEST, preferred_element_type=F32)
    heavy = jnp.concatenate([jnp.broadcast_to(coef[elems + e : elems + e + 1], (64, span)) for e in range(elems)], axis=0)
    value = join_depth(join_span(heavy * cot_ref[...].reshape(depth * 8, span)))
    out_ref[: depth * 8, :] = value
    out_ref[depth * 8 :, :] = coef


def edge_kernel(depth, msg_ref, out_ref):
    rows = msg_ref.shape[0] // 2
    low, high = (msg_ref[pl.ds(rows + node, depth, stride=8), :] for node in (0, 7))
    out_ref[:depth] = jnp.where(lax.rem(lax.axis_index("plane"), 2) == 0, high, low)
    out_ref[depth:] = msg_ref[rows + depth * 8 :, :]


def widen_kernel(depth, edge_ref, out_ref):
    span = edge_ref.shape[1]
    out_ref[: depth * 8] = jnp.concatenate([jnp.broadcast_to(edge_ref[z : z + 1, :], (8, span)) for z in range(depth)], axis=0)
    out_ref[depth * 8 :] = edge_ref[depth:, :]


class Layout:
    def __init__(self, tall):
        wide = 2 * REACH + 1
        self.wide = wide
        self.at_once = 1 if tall else 3
        self.sums = 0
        self.minv = max(wide, 5 * self.at_once)
        self.ratio = self.minv + wide
        self.basis = self.ratio + 5
        self.second = self.basis + 3 * wide
        self.total = self.second + wide * self.at_once


def basis_kernel(counts, *refs):
    height, plane = counts
    n_in = 5 * height
    msgs = refs[:n_in]
    face_ref, ends_ref, row_a_ref, row_b_ref, omega_ref, quot_ref = refs[n_in : n_in + 6]
    fields_ref, info_ref = refs[n_in + 6 : n_in + 8]
    pool, raw, coef, weigh = refs[n_in + 8 :]
    rows, span = pool.shape[1:]
    depth = rows // 8
    own_depth = depth // height
    own_rows = own_depth * 8
    elems = depth // 8
    own_elems = elems // height
    height_pos = lax.axis_index("height")
    plane_pos = lax.axis_index("plane")
    member = lax.rem(plane_pos, GROUP)
    even = lax.rem(plane_pos // GROUP, 2) == 0
    slab_rows = own_rows + coef_rows(own_elems)
    whole = elems > 4
    lay = Layout(whole)
    wide = lay.wide

    sub = lax.broadcasted_iota(jnp.int32, (8, span), 0)
    opens, closes = seams(span)

    def stage(msg, piece, slot, block):
        top = piece * slab_rows
        raw[slot, pl.ds(pl.multiple_of(block * own_rows, own_rows), own_rows)] = msg[top : top + own_rows, :]
        for kind in range(2):
            for elem in range(own_elems):
                at = top + own_rows + kind * own_elems + elem
                coef[slot, kind, block * own_elems + elem] = jnp.broadcast_to(msg[at : at + 1, :], (8, span))

    before, here, after = 1, 1 + GROUP, 1 + 2 * GROUP
    early = member < GROUP // 2
    lone = jnp.where(
        early,
        jnp.where(member == 0, 0, after + jnp.bitwise_xor(member, 3)),
        jnp.where(member == GROUP - 1, 3 * GROUP + 1, before + jnp.bitwise_xor(member, 3)),
    )
    def slots(base, flips):
        return [base + jnp.bitwise_xor(member, flip) for flip in flips]

    roles = (
        slots(here, (0, 1)),
        slots(here, (2, 3)),
        slots(jnp.where(even, after, before), (0, 1)),
        slots(jnp.where(even, before, after), (0, 1)),
        [*slots(jnp.where(early, before, after), (2, 3)), lone],
    )
    for turn in range(height):
        block = lax.rem(height_pos - turn + height, height)
        for msg, places in zip(msgs[turn * len(roles) :], roles):
            for piece, slot in enumerate(places):
                stage(msg, piece, slot, block)

    def face_at(slot, width_node):
        return slot, pl.ds(width_node, depth, stride=8)

    def join_width(store, slot):
        low, high = face_at(slot, 7), face_at(slot + 1, 0)
        both = store[low] + store[high]
        store[low] = both
        store[high] = both

    def loop(start, stop, body, step=1):
        if whole:
            lax.fori_loop(start, stop, lambda at, carry: (body([at]), carry)[1], 0)
        else:
            for at in range(start, stop, step):
                body(list(range(at, min(at + step, stop))))

    def each(body):
        return lambda slabs: [body(at) for at in slabs]

    def split(values):
        one = values.astype(BF16)
        return one, (values - one.astype(F32)).astype(BF16)

    def along_span(halves):
        wides = [jnp.dot(jnp.concatenate(h, axis=1), row_a_ref[...], preferred_element_type=F32) for h in halves]
        if len(halves) == 2:
            extra = jnp.dot(jnp.concatenate([halves[0][0], halves[1][0]], axis=1), row_b_ref[...], preferred_element_type=F32)
            extras = [extra[:, :span], extra[:, span:]]
        else:
            extras = [jnp.dot(halves[0][0], row_b_ref[:span, :span], preferred_element_type=F32)]
        return [(w[:, :span] + w[:, span:]) + x for w, x in zip(wides, extras)]

    def along_face(matrix, halves, elem):
        top = elem * 64
        stacks = [jnp.concatenate([piece[top : top + 64] for piece in h], axis=0) for h in halves]
        made = jnp.dot(matrix, stacks[0] if len(stacks) == 1 else jnp.concatenate(stacks, axis=1), preferred_element_type=F32)
        count = made.shape[0] // 3
        return made[:count] + (made[count : 2 * count] + made[2 * count :])

    def scaled(slot, kind, elem, scale):
        value = coef[slot, kind, elem]
        return value if scale == 1.0 else value * scale

    def operator(fields, slots, scale=1.0, start=0):
        halves = [split(v) for v in fields]
        lines = along_span(halves)
        out = [[] for _ in fields]
        for elem in range(fields[0].shape[0] // 64):
            top = elem * 64
            face = along_face(face_ref[...], halves, elem)
            for i, v in enumerate(fields):
                cap = tall(scaled(slots[i], 1, start + elem, scale), face)
                kap = tall(scaled(slots[i], 0, start + elem, scale), face)
                lin = lines[i][top : top + 64] + face[:, i * span : (i + 1) * span]
                out[i].append(cap * v[top : top + 64] + kap * lin)
        return [jnp.concatenate(o, axis=0) for o in out]

    def ends(sources, targets, at, scale):
        halves = [split(pool[s]) for s in sources]
        edges = [pool[s, pl.ds(node, depth, stride=8)] for s, node in zip(sources, (7, 0))]
        lines = along_span([split(jnp.concatenate(edges, axis=0))])[0]
        both = [along_face(ends_ref[...], halves, elem) for elem in range(elems)]
        for i in range(2):
            joined = []
            for elem in range(elems):
                lin = lines[i * depth + elem * 8 : i * depth + elem * 8 + 8] + both[elem][8 * (1 - i) : 8 * (2 - i), i * span : (i + 1) * span]
                slot = member + at[i]
                joined.append(join_span(scaled(slot, 1, elem, scale) * edges[i][elem * 8 : elem * 8 + 8] + scaled(slot, 0, elem, scale) * lin))
            final = []
            for elem in range(elems):
                value = joined[elem]
                if elem > 0:
                    value = value + jnp.where(sub == 0, pltpu.roll(joined[elem - 1], 1, 0), 0.0)
                if elem < elems - 1:
                    value = value + jnp.where(sub == 7, pltpu.roll(joined[elem + 1], 7, 0), 0.0)
                final.append(value)
            pool[face_at(targets[i], (7, 0)[i])] = jnp.concatenate(final, axis=0)

    def step(chains, low, high, shift):
        def apply(work):
            made = operator([pool[here + at] for here, _, at in work], [member + at for _, _, at in work], 1.0 / shift)
            for (_, sums, at), value in zip(work, made):
                pool[sums + at] = join_depth(join_span(value))

        if whole:
            for here, sums, after in chains:
                loop(low + 1, high, each(lambda at: apply([(here, sums, at)])))
        else:
            work = [(here, sums, at) for here, sums, _ in chains for at in range(low + 1, high)]
            for first in range(0, len(work), 2):
                apply(work[first : first + 2])
        for here, sums, _ in chains:
            ends((here + low, here + high), (sums + low, sums + high), (low, high), 1.0 / shift)
        for here, sums, after in chains:
            loop(low, high, each(lambda at: join_width(pool, sums + at)))

            def advance(at):
                pool[after + at] = pool[lay.minv + at - 1] * pool[sums + at] - pool[here + at]

            loop(low + 1, high, each(advance))

    def constant(kind, at):
        layers = [[join_span(coef[member + at + side, kind, elem]) for elem in range(elems)] for side in (-1, 0, 1)]
        wide_sum = lambda low, mid, high: mid + jnp.where(sub == 0, low, jnp.where(sub == 7, high, 0.0))
        inside = [wide_sum(*(layers[side][elem] for side in range(3))) for elem in range(elems)]
        planes = []
        for elem in range(elems):
            first = inside[elem] if elem == 0 else inside[elem] + inside[elem - 1]
            last = inside[elem] if elem == elems - 1 else inside[elem] + inside[elem + 1]
            planes += [first] + [inside[elem]] * 6 + [last]
        return jnp.concatenate(planes, axis=0)

    def inverse_slab(at):
        quot = jnp.concatenate([quot_ref[...].reshape(64, span)] * elems, axis=0)
        mass = constant(1, at)
        inverse = 1.0 / jnp.maximum(mass + quot * constant(0, at), TINY)
        pool[lay.minv + at - 1] = inverse
        return inverse, mass

    def first_slab(at):
        inverse, _ = inverse_slab(at)
        pool[lay.basis + at - 1] = inverse * raw[member + at]

    def inner_slab(at):
        inverse, mass = inverse_slab(at)
        pool[lay.basis + at - 1] = inverse * raw[member + at]
        pool[lay.ratio + at - 3] = inverse * mass

    def join_blocks(slot):
        for block in range(1, height):
            low, high = pl.ds(block * own_rows - 8, 8), pl.ds(block * own_rows, 8)
            both = raw[slot, low] + raw[slot, high]
            raw[slot, low] = both
            raw[slot, high] = both

    loop(0, wide + 2, each(lambda at: join_blocks(member + at)))
    loop(0, wide + 1, each(lambda at: join_width(raw, member + at)))
    loop(1, 3, each(first_slab))
    loop(3, wide - 1, each(inner_slab))
    loop(wide - 1, wide + 1, each(first_slab))

    mid = REACH + 1

    def own(slot):
        value = pool[slot, :own_rows]
        for block in range(1, height):
            value = jnp.where(height_pos == block, pool[slot, block * own_rows : (block + 1) * own_rows], value)
        return value

    shape = (own_depth, 8, span)
    zpos = lax.broadcasted_iota(jnp.int32, shape, 0) + height_pos * own_depth
    xpos = lax.broadcasted_iota(jnp.int32, shape, 1) + plane_pos * 8

    def copies(pos, extent):
        return jnp.where(((pos % 8 == 7) & (pos < extent - 1)) | ((pos % 8 == 0) & (pos > 0)), 0.5, 1.0)

    share = copies(zpos, depth) * copies(xpos, plane * 8) * jnp.where(opens | closes, 0.5, 1.0)
    omega = jnp.concatenate([omega_ref[...].reshape(64, span)] * own_elems, axis=0)
    weigh[...] = share.reshape(own_rows, span) * omega / own(lay.minv + REACH)

    for level in range(2):
        step([(lay.basis + level * wide - 1, lay.sums - 1, lay.basis + (level + 1) * wide - 1)], 1 + level, wide - level, SHIFTS[level])
    for vec in range(3):
        fields_ref[vec] = own(lay.basis + vec * wide + REACH)

    def second(vecs):
        homes = [lay.second + wide * i for i in range(lay.at_once)]
        sums = [lay.sums + 5 * i - 3 for i in range(lay.at_once)]
        for vec, home in zip(vecs, homes):

            def begin(at):
                pool[home + at - 3] = pool[lay.ratio + at - 3] * pool[lay.basis + vec * wide + at - 1]

            loop(3, 8, each(begin))
        step([(h - 3, t, h + 1) for h, t in zip(homes, sums)], 3, 7, SHIFTS[0])
        step([(h + 1, t, h + 3) for h, t in zip(homes, sums)], 4, 6, SHIFTS[1])
        for vec, home in zip(vecs, homes):
            for level, slot in enumerate((2, 6, 8)):
                fields_ref[3 + 3 * level + vec] = own(home + slot)

    if lay.at_once == 3:
        second([0, 1, 2])
    else:
        loop(0, 3, each(lambda vec: second([vec])))

    slot = member + mid
    start = height_pos * own_elems

    def total(values):
        return jnp.sum(values.reshape(shape), axis=0)

    parts = []
    left = [weigh[...] * fields_ref[i] for i in range(3)]
    parts += [total(left[i] * fields_ref[j]) for i, j in BANDS]
    lasts = (2, 9, 10, 11)
    energy = []
    for k in (0, 2):
        energy += operator([fields_ref[i] for i in lasts[k : k + 2]], [slot] * 2, 1.0, start)
    energy = [omega * e for e in energy]
    parts.append(total(fields_ref[2] * energy[0]))
    for k, l in BANDS:
        left = [weigh[...] * fields_ref[3 + 3 * k + i] for i in range(3)]
        parts += [total(left[i] * fields_ref[3 + 3 * l + j]) for i, j in PAIRS]
    parts += [total(fields_ref[9 + i] * energy[1 + j]) for i, j in PAIRS]
    lines = [jnp.sum(part, axis=0, keepdims=True) for part in parts]
    lines.append(jnp.zeros((span - len(lines), span), F32))
    sums = lax.dot_general(jnp.ones((8, span), F32), jnp.concatenate(lines, axis=0), (((1,), (1,)), ((), ())), precision=HIGHEST, preferred_element_type=F32)

    heavy = jnp.concatenate([jnp.concatenate([coef[slot, 1, start + elem]] * 8, axis=0) for elem in range(own_elems)], axis=0) * (omega * 0.125)
    rows_of = []
    for index in range(12):
        mass = heavy * fields_ref[index]
        for elem in range(own_elems):
            rows_of.append(jnp.sum(mass[elem * 64 : elem * 64 + 64], axis=0, keepdims=True))
    stack = jnp.concatenate(rows_of, axis=0)
    cells = span // 8
    per_row = span // cells
    spread = (lax.broadcasted_iota(jnp.int32, (span, span), 0) // 8 == lax.broadcasted_iota(jnp.int32, (span, span), 1) % cells).astype(F32)
    stack = jnp.dot(stack, spread, precision=HIGHEST, preferred_element_type=F32)
    place = lax.broadcasted_iota(jnp.int32, stack.shape, 0) % per_row == lax.broadcasted_iota(jnp.int32, stack.shape, 1) // cells
    stack = jnp.where(place, stack, 0.0).reshape(stack.shape[0] // per_row, per_row, span)
    info = jnp.concatenate([jnp.sum(stack, axis=1), sums[:1]], axis=0)
    info_ref[...] = jnp.broadcast_to(info[None], info_ref.shape)


def galerkin(gram, energy):
    n00, n01, n11, n12, n22 = gram
    first, later = SHIFTS
    n02 = (first / later) * (n11 + n01) - n01
    h00, h01, h02 = first * (n01 + n00), first * (n11 + n01), first * (n12 + n02)
    h11, h12 = later * (n12 + n11), later * (n22 + n12)
    low10, low20 = h01 / h00, h02 / h00
    piv1 = h11 - low10 * h01
    off12 = h12 - low10 * h02
    low21 = off12 / piv1
    piv2 = energy - low20 * h02 - low21 * off12
    y0 = n00
    y1 = n01 - low10 * y0
    y2 = n02 - low20 * y0 - low21 * y1
    c2 = y2 / piv2
    c1 = y1 / piv1 - low21 * c2
    c0 = y0 / h00 - low10 * c1 - low20 * c2
    return c0, c1, c2


def combine_kernel(info_ref, fields_ref, owner_ref, place_ref, second_ref, first_ref, grad_ref):
    devices, lines, span = info_ref.shape
    ones = jnp.ones((devices, span), F32)
    contract = (((0,), (0,)), ((), ()))
    wide = lax.dot_general(info_ref[:, lines - 1, :], ones, contract, precision=HIGHEST, preferred_element_type=F32)
    take = [wide[i : i + 1, :] for i in range(6 + 30 + 6)]
    coef = galerkin(take[:5], take[5])
    double = [(2.0 if i != j else 1.0) * coef[i] * coef[j] for i, j in PAIRS]
    gram = [sum(f * t for f, t in zip(double, take[at : at + 6])) for at in range(6, 36, 6)]
    at = 36
    energy = sum(f * t for f, t in zip(double, take[at : at + 6]))
    outer = galerkin(gram, energy)
    factors = list(coef) + [d * c for d in outer for c in coef]

    second = factors[0] * fields_ref[0] + factors[1] * fields_ref[1] + factors[2] * fields_ref[2]
    second_ref[...] = second.reshape(second_ref.shape)
    first = factors[3] * fields_ref[3]
    for i in range(4, 12):
        first = first + factors[i] * fields_ref[i]
    first_ref[...] = first.reshape(first_ref.shape)

    per_line = 12 // (lines - 1)
    cells = span // per_line
    row = lax.broadcasted_iota(jnp.int32, (span, span), 0)
    for step in range(2):
        holder = (owner_ref[step : step + 1, :] == lax.broadcasted_iota(jnp.int32, (devices, span), 0)).astype(F32)
        here = place_ref[step : step + 1, :] == row % cells
        result = jnp.zeros((1, span), F32)
        for line in range(lines - 1):
            fields = [f for f in range(line * per_line, (line + 1) * per_line) if (f >= 3) == (step == 0)]
            if not fields:
                continue
            picked = lax.dot_general(info_ref[:, line, :], holder, contract, precision=HIGHEST, preferred_element_type=F32)
            picked = jnp.where(here, picked, 0.0)
            for f in fields:
                lo = (f - line * per_line) * cells
                result = result + factors[f] * jnp.sum(picked[lo : lo + cells], axis=0, keepdims=True)
        grad_ref[step : step + 1, :] = result


def per_device(counts, cotangent, conductivity, capacity, sources):
    height, plane = counts
    depth, _, span = cotangent.shape
    elems = depth // 8
    cells = span // 8
    groups = plane // GROUP
    devices = height * plane
    vmem = pl.BlockSpec(memory_space=pltpu.VMEM)

    rows = depth * 8 + coef_rows(elems)
    lines = jnp.concatenate([conductivity, capacity], axis=1).reshape(elems * 2, cells)
    lines = jnp.pad(lines, ((0, rows - depth * 8 - 2 * elems), (0, span - cells)))
    message = pl.pallas_call(
        functools.partial(pack_kernel, (depth, elems, cells)),
        out_shape=jax.ShapeDtypeStruct((rows, span), F32),
        in_specs=[vmem] * 2,
        out_specs=vmem,
        compiler_params=pltpu.CompilerParams(vmem_limit_bytes=4 * 2**20),
    )(cotangent, lines)

    def move(value, pairs):
        return lax.ppermute(value, "plane", pairs) if pairs else jnp.zeros_like(value)

    def both_ways(pairs):
        return [*pairs, *((b, a) for a, b in pairs)]

    def shift(gap, moving):
        return [(g * GROUP + m, (g + gap) * GROUP + m) for g in range(groups) for m in moving if 0 <= g + gap < groups]

    half = jnp.concatenate([message, move(message, [(p, p ^ 1) for p in range(plane)])], axis=0)
    every = range(GROUP)
    pair = move(half, both_ways([(a, b) for a, b in shift(1, every) if (a // GROUP) % 2 == 0]))
    cross = move(half, both_ways([(a, b) for a, b in shift(1, every) if (a // GROUP) % 2 == 1]))
    other = move(half, [(p, p ^ 2) for p in range(plane)])
    side = move(other, shift(1, (0, 1)) + shift(-1, (2, 3)))
    edge = pl.pallas_call(
        functools.partial(edge_kernel, depth),
        out_shape=jax.ShapeDtypeStruct((rows - depth * 7, span), F32),
        in_specs=[vmem],
        out_specs=vmem,
        compiler_params=pltpu.CompilerParams(vmem_limit_bytes=4 * 2**20),
    )(other)
    edge = move(edge, shift(2, (0,)) + shift(-1, (1,)) + shift(1, (2,)) + shift(-2, (3,)))
    lone = pl.pallas_call(
        functools.partial(widen_kernel, depth),
        out_shape=jax.ShapeDtypeStruct((rows, span), F32),
        in_specs=[vmem],
        out_specs=vmem,
        cost_estimate=pl.CostEstimate(flops=100000000, bytes_accessed=3000000, transcendentals=0),
        compiler_params=pltpu.CompilerParams(vmem_limit_bytes=4 * 2**20),
    )(edge)
    sent = (half, other, pair, cross, jnp.concatenate([side, lone], axis=0))
    operands = list(sent)
    for turn in range(1, height):
        operands += [lax.ppermute(arr, "height", [(h, (h + turn) % height) for h in range(height)]) for arr in sent]

    lay = Layout(elems * height > 4)
    consts = tables(span)
    slots = 3 * GROUP + 2
    slab_bytes = 4 * depth * 8 * height * span
    fields, info = pl.pallas_call(
        functools.partial(basis_kernel, counts),
        out_shape=(jax.ShapeDtypeStruct((12, depth * 8, span), F32), jax.ShapeDtypeStruct((devices, 12 * elems * cells // span + 1, span), F32)),
        in_specs=[vmem] * (len(operands) + len(consts)),
        out_specs=(vmem, vmem),
        scratch_shapes=[
            pltpu.VMEM((lay.total, depth * 8 * height, span), F32),
            pltpu.VMEM((slots, depth * 8 * height, span), F32),
            pltpu.VMEM((slots, 2, elems * height, 8, span), F32),
            pltpu.VMEM((depth * 8, span), F32),
        ],
        compiler_params=pltpu.CompilerParams(vmem_limit_bytes=(lay.total + 3 * slots + 14) * slab_bytes + 12 * 2**20),
    )(*operands, *[jnp.asarray(c) for c in consts])

    shared = lax.all_to_all(info, ("height", "plane"), 0, 0, tiled=True)

    cell = sources % cells
    column = sources // cells
    wide_elem = column % plane
    deep_elem = column // plane
    owner = (deep_elem // elems) * plane + wide_elem
    place = (deep_elem % elems) * cells + cell
    return pl.pallas_call(
        combine_kernel,
        out_shape=(
            jax.ShapeDtypeStruct(cotangent.shape, F32),
            jax.ShapeDtypeStruct(cotangent.shape, F32),
            jax.ShapeDtypeStruct(sources.shape, F32),
        ),
        in_specs=[vmem] * 4,
        out_specs=(vmem, vmem, vmem),
        compiler_params=pltpu.CompilerParams(vmem_limit_bytes=8 * 2**20),
    )(shared, fields, owner, place)


def solution(mesh):
    counts = (mesh.shape["height"], mesh.shape["plane"])
    field = P("height", "plane", None)
    return jax.shard_map(
        functools.partial(per_device, counts),
        mesh=mesh,
        in_specs=(field, field, field, P()),
        out_specs=(field, field, P()),
        check_vma=False,
    )
```
